32 devices in a mesh: dp: 8 (over z, y), grp: 4 (over x, core).
Axes of the slice: x: 2, y: 2, z: 4, core: 2. Of those that a mesh axis runs over, the one named last changes fastest.
Arguments:
- states: bfloat16 [4096, 2048], P(('dp', 'grp')), may hold values from -60 to 60
- projection: bfloat16 [2048, 768], replicated, may hold values from -0.125 to 0.125
- owner_group: int32 [4096, 1], P(('dp', 'grp')), may hold values from 0 to 7; in each aligned block of 128 rows (0 to 127, 128 to 255, ...) at most 32 rows name the same one
- cluster_sub: int32 [4096], P(('dp', 'grp')), may hold values from 0 to 3
- priority: int32 [4096], P(('dp', 'grp')), may hold values from 0 to 4095, each once
Outputs:
- dup_score: float32 [4096], P(('dp', 'grp'))
The draws below stay inside these ranges and needn't reach their ends.
Inputs may be any that keep to these rules, and one draw needn't show every extreme that they name: `owner_group`: in each aligned block of 128 rows (the rows of one device) no owner is named by more than 32 rows; in some block some owner is named by exactly 32 rows.
All inputs are finite; a program needn't handle non-finite values.
Results may differ from the reference program's by a relative error of at most 0.0012.
Values may be sent and summed in bfloat16 or wider, within the bound.
No kernel may reach another device: no remote copies, remote signals or barrier semaphores. Data moves between devices by JAX's collectives and lax.ppermute only.
A program may use at most 64 MiB of HBM per device.

```python
import math
import jax
import jax.numpy as jnp
import numpy as np
from jax import lax

DIN = 2048
DE = 768
ROW_DEV = 128
SUBS = 4
SLOT = 32
ROWS = 4096
N_DP = 8


def draw_states(key, part):
    key_noise = jax.random.fold_in(key, 11)
    key_scale = jax.random.fold_in(key, 12)
    row_scale = 10.0 ** jax.random.uniform(key_scale, (ROWS, 1), jnp.float32)
    noise_draw = jax.random.normal(key_noise, (ROWS, DIN), jnp.float32)
    return (row_scale * jnp.clip(noise_draw, -6.0, 6.0)).astype(jnp.bfloat16)


def place_ends(array, own_key, low, high):
    shape = array.shape
    place = [jax.random.randint(jax.random.fold_in(own_key, axis), (), 0, shape[axis]) for axis in range(len(shape))]
    array = array.at[tuple(place)].set(low)
    longest = shape.index(max(shape))
    place[longest] = (place[longest] + 1) % shape[longest]
    return array.at[tuple(place)].set(high)


def assign_block(rng, own, number, rows, count, top, most, lean):
    order = jax.random.permutation(rng, count)
    crowded, usual = portions_of(count, rows * top, most, lean, True), portions_of(count, rows * top, most, lean, False)
    places = jnp.arange(count)

    def named(lengths, offset_by):
        used = int((lengths > 0).sum())
        fixed = max(1, used // 4)
        passed = fixed + (places - fixed + offset_by * (used - fixed)) % max(1, count - fixed)
        return jnp.zeros((count,), jnp.int32).at[order[jnp.where(places < fixed, places, passed)]].set(jnp.asarray(lengths, jnp.int32))

    lengths = jnp.where(number % 4 == 0, named(crowded, number // 4), named(usual, number - number // 4 - 1))
    mixed = jax.random.permutation(jax.random.fold_in(own, 3), count)
    giver, receiver = mixed[0:count // 2 * 2:2], mixed[1:count // 2 * 2:2]
    room = jnp.minimum(lengths[giver] - 1, most - lengths[receiver]) // 2
    room = jnp.where((giver == order[0]) | (receiver == order[0]) | (lengths[receiver] == 0), 0, jnp.maximum(room, 0))
    passed = jax.random.randint(jax.random.fold_in(own, 4), (count // 2,), 0, 1 << 20) % (room + 1)
    lengths = lengths.at[giver].add(-passed).at[receiver].add(passed)
    labels = jnp.searchsorted(jnp.cumsum(lengths), jnp.arange(rows * top), side="right").astype(jnp.int32)
    table = labels.reshape(top, rows).T
    table = table[jax.random.permutation(jax.random.fold_in(own, 1), rows)]
    offset_by = jax.random.randint(jax.random.fold_in(own, 2), (rows, 1), 0, top)
    return jnp.take_along_axis(table, (jnp.arange(top)[None, :] + offset_by) % top, axis=1)


def portions_of(amount, total, bound, slope, full):
    loads = [(1 << 20) // math.isqrt(rank ** slope) + 1 for rank in range(1, amount + 1)]
    largest = bound if full else min(bound, max(-(-total // amount), total * loads[0] // sum(loads)))
    least = 1 if total - largest >= amount - 1 else 0
    counts, surplus = [largest] + [least] * (amount - 1), total - largest - least * (amount - 1)
    while surplus > 0:
        free = [i for i in range(1, amount) if counts[i] < largest] or [i for i in range(1, amount) if counts[i] < bound]
        mass, budget = sum([loads[i] for i in free]), surplus
        for i in free:
            addition = min(bound - counts[i], max(1, budget * loads[i] // mass), surplus)
            counts[i] = counts[i] + addition
            surplus = surplus - addition
    return np.array(counts)


def gaussian(rng, shape, width, reach, held_as=jnp.bfloat16):
    return jnp.clip(width * jax.random.normal(rng, shape, jnp.float32), -reach, reach).astype(held_as)


def setup_inputs(seed: int = 0) -> dict:
    seeds = jax.random.split(jax.random.key(seed), 6)
    states = draw_states(jax.random.fold_in(seeds[5], 71), 0)
    projection = gaussian(seeds[1], (DIN, DE), DIN ** -0.5, 0.125)
    owner_group_keys = jax.random.split(jax.random.fold_in(seeds[2], 1), ROWS // ROW_DEV)
    owner_group_turns = jax.random.permutation(jax.random.fold_in(seeds[2], 3), ROWS // ROW_DEV)
    owner_group = jax.vmap(lambda own, number: assign_block(jax.random.fold_in(seeds[2], 2), own, number, ROW_DEV, N_DP, 1, SLOT, 1))(owner_group_keys, owner_group_turns).reshape((ROWS, 1))
    cluster_sub = place_ends(jax.random.randint(seeds[3], (ROWS,), 0, SUBS), jax.random.fold_in(seeds[3], 1), 0, SUBS - 1).astype(jnp.int32)
    priority = jax.random.permutation(seeds[4], ROWS).astype(jnp.int32)
    return dict(states=states, projection=projection, owner_group=owner_group, cluster_sub=cluster_sub, priority=priority)


block_rows = 256

def reference(states, projection, owner_group, cluster_sub, priority):
    projected = jnp.dot(states, projection, preferred_element_type=jnp.float32)
    square_sum = lax.optimization_barrier(jnp.sum(projected * projected, axis=1, keepdims=True))
    inverse_norm = lax.rsqrt(square_sum + 1e-06)
    embedding = (projected * inverse_norm).astype(jnp.bfloat16)
    cluster = (owner_group[:, 0] * SUBS + cluster_sub).astype(jnp.int32)
    sort_key = cluster * ROWS + priority
    sort_order = jnp.argsort(sort_key).astype(jnp.int32)
    sorted_emb = embedding[sort_order]
    sorted_cluster = cluster[sort_order]
    cluster_first = jnp.searchsorted(sorted_cluster, sorted_cluster, side='left').astype(jnp.int32)
    position = jnp.arange(ROWS, dtype=jnp.int32)

    def one_block(block_index):
        first_row = (block_index * block_rows).astype(jnp.int32)
        query_emb = lax.dynamic_slice_in_dim(sorted_emb, first_row, block_rows, 0)
        query_cl = lax.dynamic_slice_in_dim(sorted_cluster, first_row, block_rows, 0)
        query_pos = lax.dynamic_slice_in_dim(position, first_row, block_rows, 0)
        low_block = (lax.dynamic_index_in_dim(cluster_first, first_row, 0, keepdims=False) // block_rows).astype(jnp.int32)

        def key_step(key_block, running):
            key_start = (key_block * block_rows).astype(jnp.int32)
            key_emb = lax.dynamic_slice_in_dim(sorted_emb, key_start, block_rows, 0)
            key_cl = lax.dynamic_slice_in_dim(sorted_cluster, key_start, block_rows, 0)
            key_pos = lax.dynamic_slice_in_dim(position, key_start, block_rows, 0)
            cosine = jnp.dot(query_emb, key_emb.T, preferred_element_type=jnp.float32)
            earlier = (key_cl[None, :] == query_cl[:, None]) & (key_pos[None, :] < query_pos[:, None])
            return jnp.maximum(running, lax.optimization_barrier(jnp.max(jnp.where(earlier, cosine, -1.0), axis=1)))
        start_value = jnp.full((block_rows,), -1.0, jnp.float32)
        return lax.fori_loop(low_block, (block_index + 1).astype(jnp.int32), key_step, start_value)
    scores = lax.map(one_block, jnp.arange(ROWS // block_rows, dtype=jnp.int32)).reshape(ROWS)
    return jnp.zeros((ROWS,), scores.dtype).at[sort_order].set(scores)
```

```python
import math

import jax
import jax.numpy as jnp
from jax import lax
from jax.experimental import pallas as pl
from jax.experimental.pallas import tpu as pltpu
from jax.sharding import PartitionSpec as P

AXES = ("dp", "grp")
NOTE_ROWS = 8
RADIX = 256
VMEM = pl.BlockSpec(memory_space=pltpu.VMEM)


def embed_kernel(states_ref, proj_ref, owner_ref, sub_ref, prio_ref, block_ref, total):
    step = pl.program_id(0)
    rows, width = total.shape
    part = jnp.dot(states_ref[...], proj_ref[...], preferred_element_type=jnp.float32)

    @pl.when(step == 0)
    def _():
        total[...] = part

    @pl.when(step > 0)
    def _():
        total[...] += part

    @pl.when(step == pl.num_programs(0) - 1)
    def _():
        projected = total[...]
        square_sum = jnp.sum(projected * projected, axis=1, keepdims=True)
        embedding = projected * lax.rsqrt(square_sum + 1e-06)
        prio = prio_ref[...]
        high = lax.shift_right_logical(prio, 8)
        fields = (owner_ref[...], sub_ref[...], high, prio - high * RADIX)
        notes = [jnp.broadcast_to(f.astype(jnp.float32), (NOTE_ROWS, rows)) for f in fields]
        notes.append(jnp.zeros((NOTE_ROWS, width - len(fields) * rows), jnp.float32))
        block = jnp.concatenate([embedding, jnp.concatenate(notes, axis=1)], axis=0)
        block_ref[...] = block.astype(jnp.bfloat16)


def embed(states, projection, owner, sub, prio):
    rows, depth = states.shape
    width = projection.shape[1]
    steps = 4
    line = pl.BlockSpec((1, rows), lambda k: (0, 0))
    return pl.pallas_call(
        embed_kernel,
        grid=(steps,),
        in_specs=[
            pl.BlockSpec((rows, depth // steps), lambda k: (0, k)),
            pl.BlockSpec((depth // steps, width), lambda k: (k, 0)),
            line,
            line,
            line,
        ],
        out_specs=pl.BlockSpec((rows + NOTE_ROWS, width), lambda k: (0, 0)),
        out_shape=jax.ShapeDtypeStruct((rows + NOTE_ROWS, width), jnp.bfloat16),
        scratch_shapes=[pltpu.VMEM((rows, width), jnp.float32)],
        compiler_params=pltpu.CompilerParams(vmem_limit_bytes=32 << 20),
        name="embed",
    )(states, projection, owner, sub, prio)


def read_notes(tail, rows):
    owner, sub, high, low = (tail[:, i * rows:(i + 1) * rows] for i in range(4))
    return owner * 4.0 + sub, high * float(RADIX) + low


def score_kernel(num_query, num_key, *refs):
    query_refs, key_refs = refs[:num_query], refs[num_query:num_query + num_key]
    out_refs = refs[num_query + num_key:2 * num_query + num_key]
    query_emb = refs[-1]
    rows = query_emb.shape[0] // num_query
    query_cluster, query_prio = [], []
    for i, ref in enumerate(query_refs):
        block = ref[...]
        query_emb[i * rows:(i + 1) * rows, :] = block[:rows]
        cluster, prio = read_notes(block[rows:].astype(jnp.float32), rows)
        query_cluster.append(cluster[:1])
        query_prio.append(prio[:1])
    query_cluster = jnp.concatenate(query_cluster, axis=1)
    query_prio = jnp.concatenate(query_prio, axis=1)
    best = jnp.full((1, num_query * rows), -1.0, jnp.float32)
    for ref in key_refs:
        block = ref[...]
        cluster, prio = read_notes(block[rows:].astype(jnp.float32), rows)
        key_cluster, key_prio = cluster.T[:, :1], prio.T[:, :1]
        cosine = lax.dot_general(
            block[:rows], query_emb[...], (((1,), (1,)), ((), ())),
            preferred_element_type=jnp.float32,
        )
        earlier = (key_cluster == query_cluster) & (key_prio < query_prio)
        found = jnp.max(jnp.where(earlier, cosine, -1.0), axis=0, keepdims=True)
        best = jnp.maximum(best, found)
    for i, ref in enumerate(out_refs):
        ref[...] = best[:, i * rows:(i + 1) * rows]


def score(queries, keys, rows):
    width = queries[0].shape[1]
    return pl.pallas_call(
        lambda *refs: score_kernel(len(queries), len(keys), *refs),
        in_specs=[VMEM] * (len(queries) + len(keys)),
        out_specs=[VMEM] * len(queries),
        out_shape=[jax.ShapeDtypeStruct((1, rows), jnp.float32)] * len(queries),
        scratch_shapes=[pltpu.VMEM((len(queries) * rows, width), jnp.bfloat16)],
        compiler_params=pltpu.CompilerParams(vmem_limit_bytes=48 << 20),
        name="score",
    )(*queries, *keys)


def on_device(states, projection, owner_group, cluster_sub, priority):
    num_dp, num_grp = lax.axis_size("dp"), lax.axis_size("grp")
    devices = num_dp * num_grp
    rows = states.shape[0]
    line = min(num_dp, 1 << (int(math.log2(devices)) // 2))
    plane = devices // line

    def line_shift(array, step):
        pairs = [(i, (i // plane + step) % line * plane + i % plane) for i in range(devices)]
        return lax.ppermute(array, AXES, pairs)

    def plane_swap(array, step):
        pairs = [(i, i // plane * plane + (i % plane ^ step)) for i in range(devices)]
        return lax.ppermute(array, AXES, pairs)

    block = embed(
        states,
        projection,
        owner_group.reshape(1, rows),
        cluster_sub.reshape(1, rows),
        priority.reshape(1, rows),
    )
    keys = [block] + [plane_swap(block, step) for step in range(1, plane)]
    queries = [block] + [line_shift(block, step) for step in range(1, line)]
    best = score(queries, keys, rows)
    total = best[0]
    for step in range(1, line):
        total = jnp.maximum(total, line_shift(best[step], -step))
    return total.reshape(rows)


def solution(mesh):
    in_specs = (
        P(("dp", "grp"), None),
        P(),
        P(("dp", "grp"), None),
        P(("dp", "grp")),
        P(("dp", "grp")),
    )
    out_specs = P(("dp", "grp"))
    return jax.shard_map(
        on_device, mesh=mesh, in_specs=in_specs, out_specs=out_specs, check_vma=False
    )
```

```python
import math

import jax
import jax.numpy as jnp
from jax import lax
from jax.experimental import pallas as pl
from jax.experimental.pallas import tpu as pltpu
from jax.sharding import Mesh, PartitionSpec as P

AXES = ("line", "mid", "grp")
PLANE = ("mid", "grp")
NOTE_ROWS = 8
RADIX = 256
CHUNKS = 4
VMEM = pl.BlockSpec(memory_space=pltpu.VMEM)
HBM = pl.BlockSpec(memory_space=pltpu.HBM)


def embed_kernel(
    states_hbm, proj_hbm, owner_hbm, sub_hbm, prio_hbm, block_ref,
    states, proj, owner, sub, prio, big_sem, small_sem,
):
    rows, depth = states.shape
    width = proj.shape[1]
    span = depth // CHUNKS
    copies = []
    for i in range(CHUNKS):
        part = pl.ds(i * span, span)
        pair = (
            pltpu.make_async_copy(states_hbm.at[:, part], states.at[:, part], big_sem.at[0, i]),
            pltpu.make_async_copy(proj_hbm.at[part], proj.at[part], big_sem.at[1, i]),
        )
        copies.append(pair)
        for copy in pair:
            copy.start()
    small = [
        pltpu.make_async_copy(src, dst, small_sem.at[i])
        for i, (src, dst) in enumerate(((owner_hbm, owner), (sub_hbm, sub), (prio_hbm, prio)))
    ]
    for copy in small:
        copy.start()
    projected = None
    for i, pair in enumerate(copies):
        for copy in pair:
            copy.wait()
        part = slice(i * span, (i + 1) * span)
        term = jnp.dot(states[:, part], proj[part, :], preferred_element_type=jnp.float32)
        projected = term if projected is None else projected + term
    square_sum = jnp.sum(projected * projected, axis=1, keepdims=True)
    embedding = projected * lax.rsqrt(square_sum + 1e-06)
    for copy in small:
        copy.wait()
    rank = prio[...]
    high = lax.shift_right_logical(rank, 8)
    fields = (owner[...] + 1, sub[...], high, rank - high * RADIX)
    notes = [jnp.broadcast_to(f.astype(jnp.float32), (NOTE_ROWS, rows)) for f in fields]
    notes.append(jnp.zeros((NOTE_ROWS, width - len(fields) * rows), jnp.float32))
    block = jnp.concatenate([embedding, jnp.concatenate(notes, axis=1)], axis=0)
    block_ref[...] = block.astype(jnp.bfloat16)


def embed(states, projection, owner, sub, prio):
    rows, depth = states.shape
    width = projection.shape[1]
    return pl.pallas_call(
        embed_kernel,
        in_specs=[HBM] * 5,
        out_specs=VMEM,
        out_shape=jax.ShapeDtypeStruct((rows + NOTE_ROWS, width), jnp.bfloat16),
        scratch_shapes=[
            pltpu.VMEM((rows, depth), jnp.bfloat16),
            pltpu.VMEM((depth, width), jnp.bfloat16),
            pltpu.VMEM((1, rows), jnp.int32),
            pltpu.VMEM((1, rows), jnp.int32),
            pltpu.VMEM((1, rows), jnp.int32),
            pltpu.SemaphoreType.DMA((2, CHUNKS)),
            pltpu.SemaphoreType.DMA((3,)),
        ],
        compiler_params=pltpu.CompilerParams(vmem_limit_bytes=60 << 20),
        name="embed",
    )(states, projection, owner, sub, prio)


def read_notes(tail, rows):
    owner, sub, high, low = (tail[:, i * rows:(i + 1) * rows] for i in range(4))
    return (owner - 1.0) * 4.0 + sub, high * float(RADIX) + low


def score_kernel(steps, num_in, *refs):
    plane_refs, in_refs = refs[:len(steps)], refs[len(steps):len(steps) + num_in]
    own_out, plane_out = refs[len(steps) + num_in:len(steps) + num_in + 2]
    in_outs = refs[len(steps) + num_in + 2:-1]
    lane_emb = refs[-1]
    rows = lane_emb.shape[0] // (1 + num_in)
    place = lax.axis_index("mid") * lax.axis_size("grp") + lax.axis_index("grp")
    lane_cluster, lane_prio = [], []
    for i, ref in enumerate((plane_refs[0],) + tuple(in_refs)):
        block = ref[...]
        lane_emb[i * rows:(i + 1) * rows, :] = block[:rows]
        cluster, prio = read_notes(block[rows:].astype(jnp.float32), rows)
        lane_cluster.append(cluster[:1])
        lane_prio.append(prio[:1])
    lane_cluster = jnp.concatenate(lane_cluster, axis=1)
    lane_prio = jnp.concatenate(lane_prio, axis=1)
    best = jnp.full((1, (1 + num_in) * rows), -1.0, jnp.float32)
    for step, ref in zip(steps, plane_refs):
        block = ref[...]
        cluster, prio = read_notes(block[rows:].astype(jnp.float32), rows)
        row_cluster, row_prio = cluster.T[:, :1], prio.T[:, :1]
        cosine = lax.dot_general(
            block[:rows], lane_emb[...], (((1,), (1,)), ((), ())),
            preferred_element_type=jnp.float32,
        )
        same = row_cluster == lane_cluster
        found = jnp.where(same & (row_prio < lane_prio), cosine, -1.0)
        best = jnp.maximum(best, jnp.max(found, axis=0, keepdims=True))
        back = jnp.where(same & (lane_prio < row_prio), cosine, -1.0)
        folded = back[:, rows:2 * rows]
        for i in range(1, num_in):
            folded = jnp.maximum(folded, back[:, (i + 1) * rows:(i + 2) * rows])
        line = jnp.max(folded.T, axis=0, keepdims=True)
        plane_out[pl.ds(place ^ step, 1), :] = line
    own_out[...] = best[:, :rows]
    for i, ref in enumerate(in_outs):
        ref[...] = best[:, (i + 1) * rows:(i + 2) * rows]


def score(steps, plane_blocks, in_blocks, rows):
    width = plane_blocks[0].shape[1]
    plane, num_in = len(plane_blocks), len(in_blocks)
    line = jax.ShapeDtypeStruct((1, rows), jnp.float32)
    return pl.pallas_call(
        lambda *refs: score_kernel(steps, num_in, *refs),
        in_specs=[VMEM] * (plane + num_in),
        out_specs=[VMEM] * (2 + num_in),
        out_shape=[line, jax.ShapeDtypeStruct((plane, rows), jnp.float32)] + [line] * num_in,
        scratch_shapes=[pltpu.VMEM(((1 + num_in) * rows, width), jnp.bfloat16)],
        compiler_params=pltpu.CompilerParams(vmem_limit_bytes=48 << 20),
        name="score",
    )(*plane_blocks, *in_blocks)


def tournament(line):
    moves = [[(i, (i + s) % line) for i in range(line)] for s in range(1, (line + 1) // 2)]
    if line % 2 == 0:
        half = line // 2
        moves.append([(i, i + half) if i % 2 else (i + half, i) for i in range(half)])
    return moves


def on_device(states, projection, owner_group, cluster_sub, priority):
    line, grp = lax.axis_size("line"), lax.axis_size("grp")
    plane = lax.axis_size("mid") * grp
    rows = states.shape[0]

    def move(array, pairs):
        whole = [(a * plane + p, b * plane + p) for a, b in pairs for p in range(plane)]
        return lax.ppermute(array, AXES, whole)

    def swap(array, step):
        pairs = [(i, i // plane * plane + (i % plane ^ step)) for i in range(line * plane)]
        return lax.ppermute(array, AXES, pairs)

    block = embed(
        states,
        projection,
        owner_group.reshape(1, rows),
        cluster_sub.reshape(1, rows),
        priority.reshape(1, rows),
    )
    moves = tournament(line)
    in_blocks = [move(block, pairs) for pairs in moves]
    steps, plane_blocks = [], []
    for step in range(0, plane, 2):
        here = block if step == 0 else swap(block, step)
        steps += [step, step + 1]
        plane_blocks += [here, swap(here, 1)]
    own, plane_best, *in_best = score(steps, plane_blocks, in_blocks, rows)
    back = lax.all_to_all(plane_best, PLANE, split_axis=0, concat_axis=0, tiled=True)
    total = jnp.maximum(own, jnp.max(back, axis=0, keepdims=True))
    where = lax.axis_index("line")
    for pairs, best in zip(moves, in_best):
        home = move(best, [(b, a) for a, b in pairs])
        if len(pairs) < line:
            sent = jnp.zeros((), jnp.bool_)
            for a, _ in pairs:
                sent = sent | (where == a)
            home = jnp.where(sent, home, -1.0)
        total = jnp.maximum(total, home)
    return total.reshape(rows)


def solution(mesh):
    num_dp, num_grp = mesh.shape["dp"], mesh.shape["grp"]
    line = min(num_dp, 1 << (int(math.log2(num_dp * num_grp)) // 2))
    split = Mesh(mesh.devices.reshape(line, num_dp // line, num_grp), AXES)
    in_specs = (P(AXES, None), P(), P(AXES, None), P(AXES), P(AXES))
    return jax.shard_map(
        on_device, mesh=split, in_specs=in_specs, out_specs=P(AXES), check_vma=False
    )
```

```python
import math

import jax
import jax.numpy as jnp
from jax import lax
from jax.experimental import pallas as pl
from jax.experimental.pallas import tpu as pltpu
from jax.sharding import Mesh, PartitionSpec as P

AXES = ("line", "mid", "grp")
PLANE = ("mid", "grp")
NOTE_ROWS = 8
RADIX = 256
CHUNKS = 4
VMEM = pl.BlockSpec(memory_space=pltpu.VMEM)
HBM = pl.BlockSpec(memory_space=pltpu.HBM)


def embed_kernel(
    states_hbm, proj_hbm, owner_hbm, sub_hbm, prio_hbm, block_ref,
    states, proj, owner, sub, prio, big_sem, small_sem,
):
    rows, depth = states.shape
    width = proj.shape[1]
    span = depth // CHUNKS
    copies = []
    for i in range(CHUNKS):
        part = pl.ds(i * span, span)
        pair = (
            pltpu.make_async_copy(states_hbm.at[:, part], states.at[:, part], big_sem.at[0, i]),
            pltpu.make_async_copy(proj_hbm.at[part], proj.at[part], big_sem.at[1, i]),
        )
        copies.append(pair)
        for copy in pair:
            copy.start()
    small = [
        pltpu.make_async_copy(src, dst, small_sem.at[i])
        for i, (src, dst) in enumerate(((owner_hbm, owner), (sub_hbm, sub), (prio_hbm, prio)))
    ]
    for copy in small:
        copy.start()
    projected = None
    for i, pair in enumerate(copies):
        for copy in pair:
            copy.wait()
        part = slice(i * span, (i + 1) * span)
        term = jnp.dot(states[:, part], proj[part, :], preferred_element_type=jnp.float32)
        projected = term if projected is None else projected + term
    square_sum = jnp.sum(projected * projected, axis=1, keepdims=True)
    embedding = projected * lax.rsqrt(square_sum + 1e-06)
    for copy in small:
        copy.wait()
    rank = prio[...]
    high = lax.shift_right_logical(rank, 8)
    fields = (owner[...] + 1, sub[...], high, rank - high * RADIX)
    notes = [jnp.broadcast_to(f.astype(jnp.float32), (NOTE_ROWS, rows)) for f in fields]
    notes.append(jnp.zeros((NOTE_ROWS, width - len(fields) * rows), jnp.float32))
    block = jnp.concatenate([embedding, jnp.concatenate(notes, axis=1)], axis=0)
    block_ref[...] = block.astype(jnp.bfloat16)


def embed(states, projection, owner, sub, prio):
    rows, depth = states.shape
    width = projection.shape[1]
    return pl.pallas_call(
        embed_kernel,
        in_specs=[HBM] * 5,
        out_specs=VMEM,
        out_shape=jax.ShapeDtypeStruct((rows + NOTE_ROWS, width), jnp.bfloat16),
        scratch_shapes=[
            pltpu.VMEM((rows, depth), jnp.bfloat16),
            pltpu.VMEM((depth, width), jnp.bfloat16),
            pltpu.VMEM((1, rows), jnp.int32),
            pltpu.VMEM((1, rows), jnp.int32),
            pltpu.VMEM((1, rows), jnp.int32),
            pltpu.SemaphoreType.DMA((2, CHUNKS)),
            pltpu.SemaphoreType.DMA((3,)),
        ],
        compiler_params=pltpu.CompilerParams(vmem_limit_bytes=60 << 20),
        name="embed",
    )(states, projection, owner, sub, prio)


def read_notes(tail, rows):
    owner, sub, high, low = (tail[:, i * rows:(i + 1) * rows] for i in range(4))
    return (owner - 1.0) * 4.0 + sub, high * float(RADIX) + low


def score_kernel(steps, num_lane, num_before, *refs):
    plane = len(steps)
    plane_refs, lane_refs = refs[:plane], refs[plane:plane + num_lane]
    before = refs[plane + num_lane:plane + num_lane + num_before]
    plane_out, lane_outs, lane_emb = refs[-2 - num_lane], refs[-1 - num_lane:-1], refs[-1]
    rows = lane_emb.shape[0] // num_lane
    place = lax.axis_index("mid") * lax.axis_size("grp") + lax.axis_index("grp")
    lane_cluster, lane_prio = [], []
    for i, ref in enumerate(lane_refs):
        block = ref[...]
        lane_emb[i * rows:(i + 1) * rows, :] = block[:rows]
        cluster, prio = read_notes(block[rows:].astype(jnp.float32), rows)
        lane_cluster.append(cluster[:1])
        lane_prio.append(prio[:1])
    lane_cluster = jnp.concatenate(lane_cluster, axis=1)
    lane_prio = jnp.concatenate(lane_prio, axis=1)
    best = jnp.full((1, num_lane * rows), -1.0, jnp.float32)
    if before:
        plane_out[...] = before[0][...]
        best = jnp.concatenate([ref[...] for ref in before[1:]], axis=1)
    else:
        plane_out[...] = jnp.full(plane_out.shape, -1.0, jnp.float32)
    for step, ref in zip(steps, plane_refs):
        block = ref[...]
        cluster, prio = read_notes(block[rows:].astype(jnp.float32), rows)
        row_cluster, row_prio = cluster.T[:, :1], prio.T[:, :1]
        cosine = lax.dot_general(
            block[:rows], lane_emb[...], (((1,), (1,)), ((), ())),
            preferred_element_type=jnp.float32,
        )
        same = row_cluster == lane_cluster
        found = jnp.where(same & (row_prio < lane_prio), cosine, -1.0)
        best = jnp.maximum(best, jnp.max(found, axis=0, keepdims=True))
        back = jnp.where(same & (lane_prio < row_prio), cosine, -1.0)
        folded = back[:, rows:2 * rows]
        for i in range(2, num_lane):
            folded = jnp.maximum(folded, back[:, i * rows:(i + 1) * rows])
        plane_out[pl.ds(place ^ step, 1), :] = jnp.max(folded.T, axis=0, keepdims=True)
    for i, ref in enumerate(lane_outs):
        ref[...] = best[:, i * rows:(i + 1) * rows]


def score(name, plane, steps, plane_blocks, lane_blocks, before, rows):
    width = plane_blocks[0].shape[1]
    part, num_lane = len(plane_blocks), len(lane_blocks)
    line = jax.ShapeDtypeStruct((1, rows), jnp.float32)
    macs = part * num_lane * rows * rows * width
    return pl.pallas_call(
        lambda *refs: score_kernel(steps, num_lane, len(before), *refs),
        in_specs=[VMEM] * (part + num_lane + len(before)),
        out_specs=[VMEM] * (1 + num_lane),
        out_shape=[jax.ShapeDtypeStruct((plane, rows), jnp.float32)] + [line] * num_lane,
        scratch_shapes=[pltpu.VMEM((num_lane * rows, width), jnp.bfloat16)],
        compiler_params=pltpu.CompilerParams(vmem_limit_bytes=48 << 20),
        cost_estimate=pl.CostEstimate(
            flops=2 * macs, bytes_accessed=2 * (part + num_lane) * rows * width, transcendentals=0
        ),
        name=name,
    )(*plane_blocks, *lane_blocks, *before)


def tournament(line):
    moves = [[(i, (i + s) % line) for i in range(line)] for s in range(1, (line + 1) // 2)]
    if line % 2 == 0:
        half = line // 2
        moves.append([(i, i + half) if i % 2 else (i + half, i) for i in range(half)])
    return moves


def on_device(states, projection, owner_group, cluster_sub, priority):
    line, grp = lax.axis_size("line"), lax.axis_size("grp")
    plane = lax.axis_size("mid") * grp
    rows = states.shape[0]

    def move(array, pairs):
        whole = [(a * plane + p, b * plane + p) for a, b in pairs for p in range(plane)]
        return lax.ppermute(array, AXES, whole)

    def swap(array, step):
        pairs = [(i, i // plane * plane + (i % plane ^ step)) for i in range(line * plane)]
        return lax.ppermute(array, AXES, pairs)

    block = embed(
        states,
        projection,
        owner_group.reshape(1, rows),
        cluster_sub.reshape(1, rows),
        priority.reshape(1, rows),
    )
    moves = tournament(line)
    in_blocks = [move(block, pairs) for pairs in moves]
    far = [swap(block, step) for step in range(2, plane, 2)]
    near = lax.optimization_barrier((block, far[0]))[0]
    steps, plane_blocks = [], []
    for step, here in zip(range(0, plane, 2), [block] + far):
        steps += [step, step + 1]
        plane_blocks += [here, swap(here if step else near, 1)]
    lanes = [block] + in_blocks
    best = score("score_most", plane, steps[:-2], plane_blocks[:-2], lanes, [], rows)
    best = score("score_rest", plane, steps[-2:], plane_blocks[-2:], lanes, best, rows)
    plane_best, own, *in_best = best
    back = lax.all_to_all(plane_best, PLANE, split_axis=0, concat_axis=0, tiled=True)
    total = jnp.maximum(own, jnp.max(back, axis=0, keepdims=True))
    where = lax.axis_index("line")
    for pairs, best in zip(moves, in_best):
        home = move(best, [(b, a) for a, b in pairs])
        if len(pairs) < line:
            sent = jnp.zeros((), jnp.bool_)
            for a, _ in pairs:
                sent = sent | (where == a)
            home = jnp.where(sent, home, -1.0)
        total = jnp.maximum(total, home)
    return total.reshape(rows)


def solution(mesh):
    num_dp, num_grp = mesh.shape["dp"], mesh.shape["grp"]
    line = min(num_dp, 1 << (int(math.log2(num_dp * num_grp)) // 2))
    split = Mesh(mesh.devices.reshape(line, num_dp // line, num_grp), AXES)
    in_specs = (P(AXES, None), P(), P(AXES, None), P(AXES), P(AXES))
    return jax.shard_map(
        on_device, mesh=split, in_specs=in_specs, out_specs=P(AXES), check_vma=False
    )
```

```python
import math

import jax
import jax.numpy as jnp
from jax import lax
from jax.experimental import pallas as pl
from jax.experimental.pallas import tpu as pltpu
from jax.sharding import Mesh, PartitionSpec as P

AXES = ("line", "mid", "grp")
PLANE = ("mid", "grp")
NOTE_ROWS = 8
RADIX = 256
CHUNKS = 4
VMEM = pl.BlockSpec(memory_space=pltpu.VMEM)
HBM = pl.BlockSpec(memory_space=pltpu.HBM)


def embed_kernel(
    states_hbm, proj_hbm, owner_hbm, sub_hbm, prio_hbm, block_ref,
    states, proj, owner, sub, prio, big_sem, small_sem,
):
    rows, depth = states.shape
    width = proj.shape[1]
    span = depth // CHUNKS
    copies = []
    for i in range(CHUNKS):
        part = pl.ds(i * span, span)
        pair = (
            pltpu.make_async_copy(states_hbm.at[:, part], states.at[:, part], big_sem.at[0, i]),
            pltpu.make_async_copy(proj_hbm.at[part], proj.at[part], big_sem.at[1, i]),
        )
        copies.append(pair)
        for copy in pair:
            copy.start()
    small = [
        pltpu.make_async_copy(src, dst, small_sem.at[i])
        for i, (src, dst) in enumerate(((owner_hbm, owner), (sub_hbm, sub), (prio_hbm, prio)))
    ]
    for copy in small:
        copy.start()
    projected = None
    for i, pair in enumerate(copies):
        for copy in pair:
            copy.wait()
        part = slice(i * span, (i + 1) * span)
        term = jnp.dot(states[:, part], proj[part, :], preferred_element_type=jnp.float32)
        projected = term if projected is None else projected + term
    square_sum = jnp.sum(projected * projected, axis=1, keepdims=True)
    embedding = projected * lax.rsqrt(square_sum + 1e-06)
    for copy in small:
        copy.wait()
    rank = prio[...]
    high = lax.shift_right_logical(rank, 8)
    fields = (owner[...] + 1, sub[...], high, rank - high * RADIX)
    notes = [jnp.broadcast_to(f.astype(jnp.float32), (NOTE_ROWS, rows)) for f in fields]
    notes.append(jnp.zeros((NOTE_ROWS, width - len(fields) * rows), jnp.float32))
    block = jnp.concatenate([embedding, jnp.concatenate(notes, axis=1)], axis=0)
    block_ref[...] = block.astype(jnp.bfloat16)


def embed(states, projection, owner, sub, prio):
    rows, depth = states.shape
    width = projection.shape[1]
    return pl.pallas_call(
        embed_kernel,
        in_specs=[HBM] * 5,
        out_specs=VMEM,
        out_shape=jax.ShapeDtypeStruct((rows + NOTE_ROWS, width), jnp.bfloat16),
        scratch_shapes=[
            pltpu.VMEM((rows, depth), jnp.bfloat16),
            pltpu.VMEM((depth, width), jnp.bfloat16),
            pltpu.VMEM((1, rows), jnp.int32),
            pltpu.VMEM((1, rows), jnp.int32),
            pltpu.VMEM((1, rows), jnp.int32),
            pltpu.SemaphoreType.DMA((2, CHUNKS)),
            pltpu.SemaphoreType.DMA((3,)),
        ],
        compiler_params=pltpu.CompilerParams(vmem_limit_bytes=60 << 20),
        name="embed",
    )(states, projection, owner, sub, prio)


def read_notes(ref, rows):
    tail = ref[rows:, :].astype(jnp.float32)
    owner, sub, high, low = (tail[:1, i * rows:(i + 1) * rows] for i in range(4))
    return (owner - 1.0) * 4.0 + sub, high * float(RADIX) + low


def score_kernel(steps, num_lane, products, num_before, hold, *refs):
    part = len(steps)
    row_refs, lane_refs = refs[:part], refs[part:part + num_lane]
    before = refs[part + num_lane:part + num_lane + num_before]
    outs = refs[part + num_lane + num_before:]
    plane_out, lane_outs = outs[0], outs[1:1 + num_lane]
    plane, rows = plane_out.shape
    place = lax.axis_index("mid") * lax.axis_size("grp") + lax.axis_index("grp")
    row_notes = [read_notes(ref, rows) for ref in row_refs]
    lane_notes = [read_notes(ref, rows) for ref in lane_refs]
    fill = jnp.zeros((-2 * part % 8, rows), jnp.float32)
    lines = [line for pair in row_notes for line in pair]
    columns = jnp.concatenate(lines + ([fill] if fill.size else []), axis=0).T
    if hold:
        outs[-1][...] = row_refs[0][...]
    back = jnp.full((rows, rows), -1.0, jnp.float32)
    lane_ids = lax.broadcasted_iota(jnp.int32, (rows, rows), 1)
    best = [None] * num_lane
    for row_set, lane_set in products:
        cosine = lax.dot_general(
            jnp.concatenate([row_refs[i][:rows, :] for i in row_set], axis=0),
            jnp.concatenate([lane_refs[j][:rows, :] for j in lane_set], axis=0),
            (((1,), (1,)), ((), ())),
            preferred_element_type=jnp.float32,
        )
        for m, i in enumerate(row_set):
            row_cluster, row_prio = columns[:, 2 * i:2 * i + 1], columns[:, 2 * i + 1:2 * i + 2]
            folded = None
            for n, j in enumerate(lane_set):
                lane_cluster, lane_prio = lane_notes[j]
                here = cosine[m * rows:(m + 1) * rows, n * rows:(n + 1) * rows]
                same = jnp.where(row_cluster == lane_cluster, here, -1.0)
                earlier = row_prio < lane_prio
                found = jnp.where(earlier, same, -1.0)
                best[j] = found if best[j] is None else jnp.maximum(best[j], found)
                if j > 0:
                    other = jnp.where(earlier, -1.0, same)
                    folded = other if folded is None else jnp.maximum(folded, other)
            if folded is not None:
                line = jnp.max(folded, axis=1, keepdims=True)
                back = jnp.maximum(back, jnp.where(lane_ids == (place ^ steps[i]), line, -1.0))
    plane_best = back.T[:plane]
    if before:
        plane_best = jnp.maximum(plane_best, before[0][...])
    plane_out[...] = plane_best
    for j, ref in enumerate(lane_outs):
        line = jnp.max(best[j], axis=0, keepdims=True)
        if j + 1 < num_before:
            line = jnp.maximum(line, before[1 + j][...])
        ref[...] = line


def score(name, steps, row_blocks, lane_blocks, products, before, plane, rows, hold=False):
    width = row_blocks[0].shape[1]
    part, num_lane = len(row_blocks), len(lane_blocks)
    line = jax.ShapeDtypeStruct((1, rows), jnp.float32)
    macs = sum(len(r) * len(c) for r, c in products) * rows * rows * width
    return pl.pallas_call(
        lambda *refs: score_kernel(steps, num_lane, products, len(before), hold, *refs),
        in_specs=[VMEM] * (part + num_lane + len(before)),
        out_specs=[VMEM] * (1 + num_lane + hold),
        out_shape=[jax.ShapeDtypeStruct((plane, rows), jnp.float32)]
        + [line] * num_lane
        + [jax.ShapeDtypeStruct(row_blocks[0].shape, row_blocks[0].dtype)] * hold,
        compiler_params=pltpu.CompilerParams(vmem_limit_bytes=48 << 20),
        cost_estimate=pl.CostEstimate(
            flops=2 * macs, bytes_accessed=2 * (part + num_lane) * rows * width, transcendentals=0
        ),
        name=name,
    )(*row_blocks, *lane_blocks, *before)


def tournament(line):
    moves = [[(i, (i + s) % line) for i in range(line)] for s in range(1, (line + 1) // 2)]
    if line % 2 == 0:
        half = line // 2
        moves.append([(i, i + half) if i % 2 else (i + half, i) for i in range(half)])
    return moves


def on_device(states, projection, owner_group, cluster_sub, priority):
    line, grp = lax.axis_size("line"), lax.axis_size("grp")
    plane = lax.axis_size("mid") * grp
    rows = states.shape[0]

    def move(array, pairs):
        whole = [(a * plane + p, b * plane + p) for a, b in pairs for p in range(plane)]
        return lax.ppermute(array, AXES, whole)

    def swap(array, step):
        pairs = [(i, i // plane * plane + (i % plane ^ step)) for i in range(line * plane)]
        return lax.ppermute(array, AXES, pairs)

    block = embed(
        states,
        projection,
        owner_group.reshape(1, rows),
        cluster_sub.reshape(1, rows),
        priority.reshape(1, rows),
    )
    moves = tournament(line)
    in_blocks = [move(block, pairs) for pairs in moves]
    lanes = [block] + in_blocks
    every = tuple(range(len(lanes)))
    early = [((0,), every[:-1])]
    *best, held = score("score_own", (0,), [block], lanes[:-1], early, [], plane, rows, True)
    steps, plane_blocks = [], []
    for step in range(0, plane, 2):
        here = swap(block, step) if step else held
        steps += [step, step + 1]
        plane_blocks += [here, swap(here, 1)]
    lanes = [held] + in_blocks
    most, rest = (steps[:-2], plane_blocks[:-2]), (steps[-2:], plane_blocks[-2:])
    split = [(tuple(range(1, plane - 2)), every), ((0,), every[-1:])]
    best = score("score_most", *most, lanes, split, best, plane, rows)
    best = score("score_rest", *rest, lanes, [((0, 1), every)], best, plane, rows)
    plane_best, own, *in_best = best
    back = lax.all_to_all(plane_best, PLANE, split_axis=0, concat_axis=0, tiled=True)
    total = jnp.maximum(own, jnp.max(back, axis=0, keepdims=True))
    where = lax.axis_index("line")
    for pairs, best in zip(moves, in_best):
        home = move(best, [(b, a) for a, b in pairs])
        if len(pairs) < line:
            sent = jnp.zeros((), jnp.bool_)
            for a, _ in pairs:
                sent = sent | (where == a)
            home = jnp.where(sent, home, -1.0)
        total = jnp.maximum(total, home)
    return total.reshape(rows)


def solution(mesh):
    num_dp, num_grp = mesh.shape["dp"], mesh.shape["grp"]
    line = min(num_dp, 1 << (int(math.log2(num_dp * num_grp)) // 2))
    split = Mesh(mesh.devices.reshape(line, num_dp // line, num_grp), AXES)
    in_specs = (P(AXES, None), P(), P(AXES, None), P(AXES), P(AXES))
    return jax.shard_map(
        on_device, mesh=split, in_specs=in_specs, out_specs=P(AXES), check_vma=False
    )
```

```python
import math

import jax
import jax.numpy as jnp
from jax import lax
from jax.experimental import pallas as pl
from jax.experimental.pallas import tpu as pltpu
from jax.sharding import Mesh, PartitionSpec as P

AXES = ("line", "mid", "grp")
NOTE_ROWS = 8
RADIX = 256
CHUNKS = 4
VMEM = pl.BlockSpec(memory_space=pltpu.VMEM)
HBM = pl.BlockSpec(memory_space=pltpu.HBM)


def embed_kernel(
    states_hbm, proj_hbm, owner_hbm, sub_hbm, prio_hbm, block_ref,
    states, proj, owner, sub, prio, big_sem, small_sem,
):
    rows, depth = states.shape
    width = proj.shape[1]
    span = depth // CHUNKS
    copies = []
    for i in range(CHUNKS):
        part = pl.ds(i * span, span)
        pair = (
            pltpu.make_async_copy(states_hbm.at[:, part], states.at[:, part], big_sem.at[0, i]),
            pltpu.make_async_copy(proj_hbm.at[part], proj.at[part], big_sem.at[1, i]),
        )
        copies.append(pair)
        for copy in pair:
            copy.start()
    small = [
        pltpu.make_async_copy(src, dst, small_sem.at[i])
        for i, (src, dst) in enumerate(((owner_hbm, owner), (sub_hbm, sub), (prio_hbm, prio)))
    ]
    for copy in small:
        copy.start()
    projected = None
    for i, pair in enumerate(copies):
        for copy in pair:
            copy.wait()
        part = slice(i * span, (i + 1) * span)
        term = jnp.dot(states[:, part], proj[part, :], preferred_element_type=jnp.float32)
        projected = term if projected is None else projected + term
    square_sum = jnp.sum(projected * projected, axis=1, keepdims=True)
    embedding = projected * lax.rsqrt(square_sum + 1e-06)
    for copy in small:
        copy.wait()
    rank = prio[...]
    high = lax.shift_right_logical(rank, 8)
    fields = (owner[...] + 1, sub[...], high, rank - high * RADIX)
    notes = [jnp.broadcast_to(f.astype(jnp.float32), (NOTE_ROWS, rows)) for f in fields]
    notes.append(jnp.zeros((NOTE_ROWS, width - len(fields) * rows), jnp.float32))
    block = jnp.concatenate([embedding, jnp.concatenate(notes, axis=1)], axis=0)
    block_ref[...] = block.astype(jnp.bfloat16)


def embed(states, projection, owner, sub, prio):
    rows, depth = states.shape
    width = projection.shape[1]
    return pl.pallas_call(
        embed_kernel,
        in_specs=[HBM] * 5,
        out_specs=VMEM,
        out_shape=jax.ShapeDtypeStruct((rows + NOTE_ROWS, width), jnp.bfloat16),
        scratch_shapes=[
            pltpu.VMEM((rows, depth), jnp.bfloat16),
            pltpu.VMEM((depth, width), jnp.bfloat16),
            pltpu.VMEM((1, rows), jnp.int32),
            pltpu.VMEM((1, rows), jnp.int32),
            pltpu.VMEM((1, rows), jnp.int32),
            pltpu.SemaphoreType.DMA((2, CHUNKS)),
            pltpu.SemaphoreType.DMA((3,)),
        ],
        compiler_params=pltpu.CompilerParams(vmem_limit_bytes=60 << 20),
        name="embed",
    )(states, projection, owner, sub, prio)


def read_notes(ref, rows):
    tail = ref[rows:, :].astype(jnp.float32)
    owner, sub, high, low = (tail[:1, i * rows:(i + 1) * rows] for i in range(4))
    return (owner - 1.0) * 4.0 + sub, high * float(RADIX) + low


def score_kernel(row_count, lane_count, has_lines, has_backs, hold, *refs):
    refs = list(refs)
    row_refs = [refs.pop(0) for _ in range(row_count)]
    lane_refs = [refs.pop(0) for _ in range(lane_count)]
    seen_lines = refs.pop(0) if has_lines else None
    seen_backs = [refs.pop(0) for _ in range(row_count)] if has_backs else None
    lines_out, *back_outs = refs[:1 + row_count]
    rows = lines_out.shape[1]
    if hold:
        refs[-1][...] = row_refs[0][...]
    row_notes = [read_notes(ref, rows) for ref in row_refs]
    lane_notes = [read_notes(ref, rows) for ref in lane_refs]
    fill = jnp.zeros((-2 * row_count % 8, rows), jnp.float32)
    lines = [line for pair in row_notes for line in pair]
    columns = jnp.concatenate(lines + ([fill] if fill.size else []), axis=0).T
    cosine = lax.dot_general(
        jnp.concatenate([ref[:rows, :] for ref in row_refs], axis=0),
        jnp.concatenate([ref[:rows, :] for ref in lane_refs], axis=0),
        (((1,), (1,)), ((), ())),
        preferred_element_type=jnp.float32,
    )
    best = [jnp.full((rows, rows), -1.0, jnp.float32)] * lane_count
    table = jnp.full((rows, rows), -1.0, jnp.float32)
    lane_ids = lax.broadcasted_iota(jnp.int32, (rows, rows), 1)
    for i in range(row_count):
        row_cluster, row_prio = columns[:, 2 * i:2 * i + 1], columns[:, 2 * i + 1:2 * i + 2]
        back = jnp.full((rows, rows), -1.0, jnp.float32)
        for j, (lane_cluster, lane_prio) in enumerate(lane_notes):
            here = cosine[i * rows:(i + 1) * rows, j * rows:(j + 1) * rows]
            same = jnp.where(row_cluster == lane_cluster, here, -1.0)
            earlier = row_prio < lane_prio
            best[j] = jnp.maximum(best[j], jnp.where(earlier, same, -1.0))
            if j > 0:
                back = jnp.maximum(back, jnp.where(earlier, -1.0, same))
        table = jnp.where(lane_ids == i, jnp.max(back, axis=1, keepdims=True), table)
    table = table.T
    for i, ref in enumerate(back_outs):
        line = table[i:i + 1]
        ref[...] = jnp.maximum(line, seen_backs[i][...]) if has_backs else line
    lines = jnp.concatenate([jnp.max(b, axis=0, keepdims=True) for b in best], axis=0)
    lines_out[...] = jnp.maximum(lines, seen_lines[...]) if has_lines else lines


def score(name, row_blocks, lane_blocks, lines=(), backs=(), hold=False):
    high, width = row_blocks[0].shape
    rows = high - NOTE_ROWS
    inputs = [*row_blocks, *lane_blocks, *lines, *backs]
    shapes = [(len(lane_blocks), rows)] + [(1, rows)] * len(row_blocks)
    outs = [jax.ShapeDtypeStruct(shape, jnp.float32) for shape in shapes]
    if hold:
        outs.append(jax.ShapeDtypeStruct((high, width), row_blocks[0].dtype))
    counts = len(row_blocks), len(lane_blocks)
    flags = len(lines) > 0, len(backs) > 0, hold
    return pl.pallas_call(
        lambda *refs: score_kernel(*counts, *flags, *refs),
        in_specs=[VMEM] * len(inputs),
        out_specs=[VMEM] * len(outs),
        out_shape=outs,
        compiler_params=pltpu.CompilerParams(vmem_limit_bytes=48 << 20),
        cost_estimate=pl.CostEstimate(
            flops=2 * math.prod(counts) * rows * rows * width,
            bytes_accessed=2 * sum(counts) * rows * width,
            transcendentals=0,
        ),
        name=name,
    )(*inputs)


def tournament(line):
    moves = [[(i, (i + s) % line) for i in range(line)] for s in range(1, (line + 1) // 2)]
    if line % 2 == 0:
        half = line // 2
        pairs = [(i, i + half) if i % 2 else (i + half, i) for i in range(half)]
        sent, met = {a for a, _ in pairs}, {b for _, b in pairs}
        idle = [i for i in range(line) if i not in sent]
        free = [i for i in range(line) if i not in met]
        moves.append(pairs + list(zip(idle, free)))
    return moves


def on_device(states, projection, owner_group, cluster_sub, priority):
    line, grp = lax.axis_size("line"), lax.axis_size("grp")
    plane = lax.axis_size("mid") * grp
    rows = states.shape[0]

    def move(array, pairs):
        whole = [(a * plane + p, b * plane + p) for a, b in pairs for p in range(plane)]
        return lax.ppermute(array, AXES, whole)

    def swap(array, step):
        pairs = [(i, i // plane * plane + (i % plane ^ step)) for i in range(line * plane)]
        return lax.ppermute(array, AXES, pairs)

    block = embed(
        states,
        projection,
        owner_group.reshape(1, rows),
        cluster_sub.reshape(1, rows),
        priority.reshape(1, rows),
    )
    moves = tournament(line)
    visitors = [move(block, pairs) for pairs in moves]
    steps = range(2, plane, 2)
    plane_blocks = [swap(block, step) for step in steps]

    soon, last = plane_blocks[:-2], plane_blocks[-2:]
    lines, *backs, held = score("score_soon", [block] + soon, [block] + visitors, hold=True)
    lanes = [held] + visitors
    lines, *more = score("score_late", last, lanes, lines=[lines])
    lanes = [swap(block, 1)] + [swap(visitor, 1) for visitor in visitors]
    theirs, own_back, *backs = score(
        "score_partner", [held] + soon + last, lanes, backs=backs + more
    )
    lines = jnp.maximum(lines, swap(theirs, 1))
    total = jnp.maximum(lines[:1], own_back)
    for step, back in zip(steps, backs):
        total = jnp.maximum(total, swap(back, step))
    for i, pairs in enumerate(moves):
        total = jnp.maximum(total, move(lines[i + 1:i + 2], [(b, a) for a, b in pairs]))
    return total.reshape(rows)


def solution(mesh):
    num_dp, num_grp = mesh.shape["dp"], mesh.shape["grp"]
    line = min(num_dp, 1 << (int(math.log2(num_dp * num_grp)) // 2))
    split = Mesh(mesh.devices.reshape(line, num_dp // line, num_grp), AXES)
    in_specs = (P(AXES, None), P(), P(AXES, None), P(AXES), P(AXES))
    return jax.shard_map(
        on_device, mesh=split, in_specs=in_specs, out_specs=P(AXES), check_vma=False
    )
```

```python
import math

import jax
import jax.numpy as jnp
from jax import lax
from jax.experimental import pallas as pl
from jax.experimental.pallas import tpu as pltpu
from jax.sharding import Mesh, PartitionSpec as P

AXES = ("line", "mid", "grp")
NOTE_ROWS = 8
RADIX = 256
CHUNKS = 8
VMEM = pl.BlockSpec(memory_space=pltpu.VMEM)
HBM = pl.BlockSpec(memory_space=pltpu.HBM)


def embed_kernel(
    states_hbm, proj_hbm, owner_hbm, sub_hbm, prio_hbm, block_ref,
    states, proj, owner, sub, prio, big_sem, small_sem,
):
    rows, depth = states.shape
    width = proj.shape[1]
    span = depth // CHUNKS
    copies = []
    for i in range(CHUNKS):
        part = pl.ds(i * span, span)
        pair = (
            pltpu.make_async_copy(states_hbm.at[:, part], states.at[:, part], big_sem.at[0, i]),
            pltpu.make_async_copy(proj_hbm.at[part], proj.at[part], big_sem.at[1, i]),
        )
        copies.append(pair)
        for copy in pair:
            copy.start()
    small = [
        pltpu.make_async_copy(src, dst, small_sem.at[i])
        for i, (src, dst) in enumerate(((owner_hbm, owner), (sub_hbm, sub), (prio_hbm, prio)))
    ]
    for copy in small:
        copy.start()
    projected = None
    for i, pair in enumerate(copies):
        for copy in pair:
            copy.wait()
        part = slice(i * span, (i + 1) * span)
        term = jnp.dot(states[:, part], proj[part, :], preferred_element_type=jnp.float32)
        projected = term if projected is None else projected + term
    square_sum = jnp.sum(projected * projected, axis=1, keepdims=True)
    embedding = projected * lax.rsqrt(square_sum + 1e-06)
    for copy in small:
        copy.wait()
    rank = prio[...]
    high = lax.shift_right_logical(rank, 8)
    fields = (owner[...] + 1, sub[...], high, rank - high * RADIX)
    notes = [jnp.broadcast_to(f.astype(jnp.float32), (NOTE_ROWS, rows)) for f in fields]
    notes.append(jnp.zeros((NOTE_ROWS, width - len(fields) * rows), jnp.float32))
    block = jnp.concatenate([embedding, jnp.concatenate(notes, axis=1)], axis=0)
    block_ref[...] = block.astype(jnp.bfloat16)


def embed(states, projection, owner, sub, prio):
    rows, depth = states.shape
    width = projection.shape[1]
    return pl.pallas_call(
        embed_kernel,
        in_specs=[HBM] * 5,
        out_specs=VMEM,
        out_shape=jax.ShapeDtypeStruct((rows + NOTE_ROWS, width), jnp.bfloat16),
        scratch_shapes=[
            pltpu.VMEM((rows, depth), jnp.bfloat16),
            pltpu.VMEM((depth, width), jnp.bfloat16),
            pltpu.VMEM((1, rows), jnp.int32),
            pltpu.VMEM((1, rows), jnp.int32),
            pltpu.VMEM((1, rows), jnp.int32),
            pltpu.SemaphoreType.DMA((2, CHUNKS)),
            pltpu.SemaphoreType.DMA((3,)),
        ],
        compiler_params=pltpu.CompilerParams(vmem_limit_bytes=60 << 20),
        name="embed",
    )(states, projection, owner, sub, prio)


def read_notes(ref, rows):
    tail = ref[rows:, :].astype(jnp.float32)
    owner, sub, high, low = (tail[:1, i * rows:(i + 1) * rows] for i in range(4))
    return (owner - 1.0) * 4.0 + sub, high * float(RADIX) + low


def score_kernel(row_count, lane_count, products, back_rows, has_lines, seen_rows, hold, *refs):
    refs = list(refs)
    row_refs = [refs.pop(0) for _ in range(row_count)]
    lane_refs = [refs.pop(0) for _ in range(lane_count)]
    seen_lines = refs.pop(0) if has_lines else None
    seen_backs = {i: refs.pop(0) for i in seen_rows}
    lines_out = refs.pop(0)
    rows = lines_out.shape[1]
    if hold:
        refs[-1][...] = row_refs[0][...]
    row_notes = [read_notes(ref, rows) for ref in row_refs]
    lane_notes = [read_notes(ref, rows) for ref in lane_refs]
    fill = jnp.zeros((-2 * row_count % 8, rows), jnp.float32)
    lines = [line for pair in row_notes for line in pair]
    columns = jnp.concatenate(lines + ([fill] if fill.size else []), axis=0).T
    best, back = [None] * lane_count, [None] * row_count

    def top(old, new):
        return new if old is None else jnp.maximum(old, new)

    for row_set, lane_set in products:
        cosine = lax.dot_general(
            jnp.concatenate([row_refs[i][:rows, :] for i in row_set], axis=0),
            jnp.concatenate([lane_refs[j][:rows, :] for j in lane_set], axis=0),
            (((1,), (1,)), ((), ())),
            preferred_element_type=jnp.float32,
        )
        for m, i in enumerate(row_set):
            row_cluster, row_prio = columns[:, 2 * i:2 * i + 1], columns[:, 2 * i + 1:2 * i + 2]
            for n, j in enumerate(lane_set):
                lane_cluster, lane_prio = lane_notes[j]
                here = cosine[m * rows:(m + 1) * rows, n * rows:(n + 1) * rows]
                same = jnp.where(row_cluster == lane_cluster, here, -1.0)
                earlier = row_prio < lane_prio
                best[j] = top(best[j], jnp.where(earlier, same, -1.0))
                if j > 0:
                    back[i] = top(back[i], jnp.where(earlier, -1.0, same))
    lane_ids = lax.broadcasted_iota(jnp.int32, (rows, rows), 1)
    table = jnp.full((rows, rows), -1.0, jnp.float32)
    for i in back_rows:
        table = jnp.where(lane_ids == i, jnp.max(back[i], axis=1, keepdims=True), table)
    table = table.T
    for i in back_rows:
        line = table[i:i + 1]
        refs.pop(0)[...] = jnp.maximum(line, seen_backs[i][...]) if i in seen_backs else line
    lines = jnp.concatenate([jnp.max(b, axis=0, keepdims=True) for b in best], axis=0)
    if has_lines:
        count = seen_lines.shape[0]
        first = jnp.maximum(lines[:count], seen_lines[...])
        lines = first if count == lane_count else jnp.concatenate([first, lines[count:]], axis=0)
    lines_out[...] = lines


def score(name, row_blocks, lane_blocks, products, back_rows, lines=None, backs=None, hold=False):
    high, width = row_blocks[0].shape
    rows = high - NOTE_ROWS
    backs = backs or {}
    inputs = [*row_blocks, *lane_blocks, *([] if lines is None else [lines]), *backs.values()]
    shapes = [(len(lane_blocks), rows)] + [(1, rows)] * len(back_rows)
    outs = [jax.ShapeDtypeStruct(shape, jnp.float32) for shape in shapes]
    if hold:
        outs.append(jax.ShapeDtypeStruct((high, width), row_blocks[0].dtype))
    counts = len(row_blocks), len(lane_blocks)
    rest = products, back_rows, lines is not None, tuple(backs), hold
    macs = sum(len(r) * len(c) for r, c in products) * rows * rows * width
    return pl.pallas_call(
        lambda *refs: score_kernel(*counts, *rest, *refs),
        in_specs=[VMEM] * len(inputs),
        out_specs=[VMEM] * len(outs),
        out_shape=outs,
        compiler_params=pltpu.CompilerParams(vmem_limit_bytes=48 << 20),
        cost_estimate=pl.CostEstimate(
            flops=2 * macs, bytes_accessed=2 * sum(counts) * rows * width, transcendentals=0
        ),
        name=name,
    )(*inputs)


def tournament(line):
    moves = [[(i, (i - s) % line) for i in range(line)] for s in range(1, (line + 1) // 2)]
    if line % 2 == 0:
        half = line // 2
        pairs = [(i, i + half) if i % 2 else (i + half, i) for i in range(half)]
        sent, met = {a for a, _ in pairs}, {b for _, b in pairs}
        idle = [i for i in range(line) if i not in sent]
        free = [i for i in range(line) if i not in met]
        moves.append(pairs + list(zip(idle, free)))
    return moves


def on_device(states, projection, owner_group, cluster_sub, priority):
    line, grp = lax.axis_size("line"), lax.axis_size("grp")
    plane = lax.axis_size("mid") * grp
    rows = states.shape[0]

    def move(array, pairs):
        whole = [(a * plane + p, b * plane + p) for a, b in pairs for p in range(plane)]
        return lax.ppermute(array, AXES, whole)

    def swap(array, step):
        pairs = [(i, i // plane * plane + (i % plane ^ step)) for i in range(line * plane)]
        return lax.ppermute(array, AXES, pairs)

    block = embed(
        states,
        projection,
        owner_group.reshape(1, rows),
        cluster_sub.reshape(1, rows),
        priority.reshape(1, rows),
    )
    moves = tournament(line)
    visitors = [move(block, pairs) for pairs in moves]
    steps = range(2, plane, 2)
    plane_blocks = [swap(block, step) for step in steps]

    lanes = [block] + visitors
    every, count = tuple(range(len(lanes))), 1 + len(plane_blocks)
    most = tuple(range(count - 1))
    lines, *backs, held = score(
        "score_soon", [block] + plane_blocks[:-1], lanes[:-1], [(most, every[:-1])], most, hold=True
    )
    row_blocks = [held] + plane_blocks
    lanes[0] = lax.optimization_barrier((block, visitors[0]))[0]
    lanes[-1] = lax.optimization_barrier((lanes[-1], held))[0]
    partner = [swap(lane, 1) for lane in lanes]
    products = [(most + (count - 1,), every)]
    theirs, *backs = score(
        "score_partner", row_blocks, partner, products, most + (count - 1,), backs=dict(enumerate(backs))
    )
    lanes[0] = held
    products = [((count - 1,), every), (most, every[-1:])]
    lines, *backs = score(
        "score_late", row_blocks, lanes, products, most + (count - 1,), lines, dict(enumerate(backs))
    )
    own_back, *backs = backs
    lines = jnp.maximum(lines, swap(theirs, 1))
    total = jnp.maximum(lines[:1], own_back)
    for i, pairs in enumerate(moves):
        total = jnp.maximum(total, move(lines[i + 1:i + 2], [(b, a) for a, b in pairs]))
    for i, (step, back) in enumerate(zip(steps, backs)):
        if i == 1:
            total = lax.optimization_barrier(total)
        total = jnp.maximum(total, swap(back, step))
    return total.reshape(rows)


def solution(mesh):
    num_dp, num_grp = mesh.shape["dp"], mesh.shape["grp"]
    line = min(num_dp, 1 << (int(math.log2(num_dp * num_grp)) // 2))
    split = Mesh(mesh.devices.reshape(line, num_dp // line, num_grp), AXES)
    in_specs = (P(AXES, None), P(), P(AXES, None), P(AXES), P(AXES))
    return jax.shard_map(
        on_device, mesh=split, in_specs=in_specs, out_specs=P(AXES), check_vma=False
    )
```

```python
import math

import jax
import jax.numpy as jnp
from jax import lax
from jax.experimental import pallas as pl
from jax.experimental.pallas import tpu as pltpu
from jax.sharding import Mesh, PartitionSpec as P

AXES = ("line", "mid", "grp")
NOTE_ROWS = 8
RADIX = 256
CHUNKS = 8
VMEM = pl.BlockSpec(memory_space=pltpu.VMEM)
HBM = pl.BlockSpec(memory_space=pltpu.HBM)


def embed_kernel(
    states_hbm, proj_hbm, owner_hbm, sub_hbm, prio_hbm, block_ref,
    states, proj, owner, sub, prio, big_sem, small_sem,
):
    rows, depth = states.shape
    width = proj.shape[1]
    span = depth // CHUNKS
    copies = []
    for i in range(CHUNKS):
        part = pl.ds(i * span, span)
        pair = (
            pltpu.make_async_copy(states_hbm.at[:, part], states.at[:, part], big_sem.at[0, i]),
            pltpu.make_async_copy(proj_hbm.at[part], proj.at[part], big_sem.at[1, i]),
        )
        copies.append(pair)
        for copy in pair:
            copy.start()
    small = [
        pltpu.make_async_copy(src, dst, small_sem.at[i])
        for i, (src, dst) in enumerate(((owner_hbm, owner), (sub_hbm, sub), (prio_hbm, prio)))
    ]
    for copy in small:
        copy.start()
    projected = None
    for i, pair in enumerate(copies):
        for copy in pair:
            copy.wait()
        part = slice(i * span, (i + 1) * span)
        term = jnp.dot(states[:, part], proj[part, :], preferred_element_type=jnp.float32)
        projected = term if projected is None else projected + term
    square_sum = jnp.sum(projected * projected, axis=1, keepdims=True)
    embedding = projected * lax.rsqrt(square_sum + 1e-06)
    for copy in small:
        copy.wait()
    rank = prio[...]
    high = lax.shift_right_logical(rank, 8)
    fields = (owner[...] + 1, sub[...], high, rank - high * RADIX)
    notes = [jnp.broadcast_to(f.astype(jnp.float32), (NOTE_ROWS, rows)) for f in fields]
    notes.append(jnp.zeros((NOTE_ROWS, width - len(fields) * rows), jnp.float32))
    block = jnp.concatenate([embedding, jnp.concatenate(notes, axis=1)], axis=0)
    block_ref[...] = block.astype(jnp.bfloat16)


def embed(states, projection, owner, sub, prio):
    rows, depth = states.shape
    width = projection.shape[1]
    return pl.pallas_call(
        embed_kernel,
        in_specs=[HBM] * 5,
        out_specs=VMEM,
        out_shape=jax.ShapeDtypeStruct((rows + NOTE_ROWS, width), jnp.bfloat16),
        scratch_shapes=[
            pltpu.VMEM((rows, depth), jnp.bfloat16),
            pltpu.VMEM((depth, width), jnp.bfloat16),
            pltpu.VMEM((1, rows), jnp.int32),
            pltpu.VMEM((1, rows), jnp.int32),
            pltpu.VMEM((1, rows), jnp.int32),
            pltpu.SemaphoreType.DMA((2, CHUNKS)),
            pltpu.SemaphoreType.DMA((3,)),
        ],
        compiler_params=pltpu.CompilerParams(vmem_limit_bytes=60 << 20),
        name="embed",
    )(states, projection, owner, sub, prio)


def read_notes(ref, rows):
    tail = ref[rows:, :].astype(jnp.float32)
    owner, sub, high, low = (tail[:1, i * rows:(i + 1) * rows] for i in range(4))
    return (owner - 1.0) * 4.0 + sub, high * float(RADIX) + low


def score_kernel(row_count, lane_count, products, parts, has_lines, seen_rows, hold, *refs):
    refs = list(refs)
    row_refs = [refs.pop(0) for _ in range(row_count)]
    lane_refs = [refs.pop(0) for _ in range(lane_count)]
    seen_lines = refs.pop(0) if has_lines else None
    seen_backs = refs.pop(0) if seen_rows else None
    lines_out = refs.pop(0)
    rows = lines_out.shape[1]
    if hold:
        refs[-1][...] = row_refs[0][...]
    row_notes = [read_notes(ref, rows) for ref in row_refs]
    lane_notes = [read_notes(ref, rows) for ref in lane_refs]
    fill = jnp.zeros((-2 * row_count % 8, rows), jnp.float32)
    lines = [line for pair in row_notes for line in pair]
    columns = jnp.concatenate(lines + ([fill] if fill.size else []), axis=0).T
    best, back = [None] * lane_count, [None] * row_count

    def top(old, new):
        return new if old is None else jnp.maximum(old, new)

    for row_set, lane_set in products:
        cosine = lax.dot_general(
            jnp.concatenate([row_refs[i][:rows, :] for i in row_set], axis=0),
            jnp.concatenate([lane_refs[j][:rows, :] for j in lane_set], axis=0),
            (((1,), (1,)), ((), ())),
            preferred_element_type=jnp.float32,
        )
        for m, i in enumerate(row_set):
            row_cluster, row_prio = columns[:, 2 * i:2 * i + 1], columns[:, 2 * i + 1:2 * i + 2]
            for n, j in enumerate(lane_set):
                lane_cluster, lane_prio = lane_notes[j]
                here = cosine[m * rows:(m + 1) * rows, n * rows:(n + 1) * rows]
                same = jnp.where(row_cluster == lane_cluster, here, -1.0)
                earlier = row_prio < lane_prio
                best[j] = top(best[j], jnp.where(earlier, same, -1.0))
                if j > 0:
                    back[i] = top(back[i], jnp.where(earlier, -1.0, same))
    lane_ids = lax.broadcasted_iota(jnp.int32, (rows, rows), 1)
    table = jnp.full((rows, rows), -1.0, jnp.float32)
    for i, each in enumerate(back):
        if each is not None:
            table = jnp.where(lane_ids == i, jnp.max(each, axis=1, keepdims=True), table)
    table = table.T
    if seen_rows:
        table = jnp.maximum(table[:row_count], seen_backs[...])
    for first, stop in parts:
        refs.pop(0)[...] = table[first:stop]
    lines = jnp.concatenate([jnp.max(b, axis=0, keepdims=True) for b in best], axis=0)
    if has_lines:
        count = seen_lines.shape[0]
        first = jnp.maximum(lines[:count], seen_lines[...])
        lines = first if count == lane_count else jnp.concatenate([first, lines[count:]], axis=0)
    lines_out[...] = lines


def score(name, row_blocks, lane_blocks, products, parts, lines=None, backs=None, hold=False):
    high, width = row_blocks[0].shape
    rows = high - NOTE_ROWS
    inputs = [*row_blocks, *lane_blocks, *(seen for seen in (lines, backs) if seen is not None)]
    shapes = [(len(lane_blocks), rows)] + [(stop - first, rows) for first, stop in parts]
    outs = [jax.ShapeDtypeStruct(shape, jnp.float32) for shape in shapes]
    if hold:
        outs.append(jax.ShapeDtypeStruct((high, width), row_blocks[0].dtype))
    counts = len(row_blocks), len(lane_blocks)
    rest = products, parts, lines is not None, backs is not None, hold
    macs = sum(len(r) * len(c) for r, c in products) * rows * rows * width
    return pl.pallas_call(
        lambda *refs: score_kernel(*counts, *rest, *refs),
        in_specs=[VMEM] * len(inputs),
        out_specs=[VMEM] * len(outs),
        out_shape=outs,
        compiler_params=pltpu.CompilerParams(vmem_limit_bytes=48 << 20),
        cost_estimate=pl.CostEstimate(
            flops=2 * macs, bytes_accessed=2 * sum(counts) * rows * width, transcendentals=0
        ),
        name=name,
    )(*inputs)


def tournament(line):
    moves = [[(i, (i + s) % line) for i in range(line)] for s in range(1, (line + 1) // 2)]
    if line % 2 == 0:
        half = line // 2
        pairs = [(i, i + half) if i % 2 else (i + half, i) for i in range(half)]
        sent, met = {a for a, _ in pairs}, {b for _, b in pairs}
        idle = [i for i in range(line) if i not in sent]
        free = [i for i in range(line) if i not in met]
        moves.append(pairs + list(zip(idle, free)))
    return moves


def on_device(states, projection, owner_group, cluster_sub, priority):
    line, grp = lax.axis_size("line"), lax.axis_size("grp")
    plane = lax.axis_size("mid") * grp
    rows = states.shape[0]

    def move(array, pairs):
        whole = [(a * plane + p, b * plane + p) for a, b in pairs for p in range(plane)]
        return lax.ppermute(array, AXES, whole)

    def swap(array, step):
        pairs = [(i, i // plane * plane + (i % plane ^ step)) for i in range(line * plane)]
        return lax.ppermute(array, AXES, pairs)

    block = embed(
        states,
        projection,
        owner_group.reshape(1, rows),
        cluster_sub.reshape(1, rows),
        priority.reshape(1, rows),
    )
    moves = tournament(line)
    visitors = [move(block, pairs) for pairs in moves]
    bits = [1 << i for i in range(1, plane.bit_length() - 1)]
    row_blocks = [block]
    for bit in bits:
        row_blocks += [swap(here, bit) for here in row_blocks]

    lanes = [block] + visitors
    every, count = tuple(range(len(lanes))), len(row_blocks)
    most, last = tuple(range(count - 1)), (count - 1,)
    lines, backs, held = score(
        "score_soon", row_blocks[:-1], lanes[:-1], [(most, every[:-1])], [(0, count)], hold=True
    )
    row_blocks[0] = held
    order = lax.optimization_barrier((lanes[0], row_blocks[-2]))[0]
    partner = [swap(lane, 1) for lane in [order] + visitors]
    lanes[0] = held
    products = [(last, every), (most, every[-1:])]
    lines, backs = score(
        "score_late", row_blocks, lanes, products, [(0, count)], lines, backs
    )
    half = count // 2
    products, parts = [(most + last, every)], [(0, half), (half, count)]
    theirs, near, far = score("score_partner", row_blocks, partner, products, parts, None, backs)
    lines = jnp.maximum(lines, swap(theirs, 1))
    for bit in bits[:0:-1]:
        near = jnp.maximum(near, swap(far, bit))
        half = near.shape[0] // 2
        near, far = near[:half], near[half:]
    total = lines[:1]
    for i, pairs in reversed(list(enumerate(moves))):
        total = jnp.maximum(total, move(lines[i + 1:i + 2], [(b, a) for a, b in pairs]))
    total = lax.optimization_barrier(total)
    total = jnp.maximum(jnp.maximum(total, near), swap(far, bits[0]))
    return total.reshape(rows)


def solution(mesh):
    num_dp, num_grp = mesh.shape["dp"], mesh.shape["grp"]
    line = min(num_dp, 1 << (int(math.log2(num_dp * num_grp)) // 2))
    split = Mesh(mesh.devices.reshape(line, num_dp // line, num_grp), AXES)
    in_specs = (P(AXES, None), P(), P(AXES, None), P(AXES), P(AXES))
    return jax.shard_map(
        on_device, mesh=split, in_specs=in_specs, out_specs=P(AXES), check_vma=False
    )
```

```python
import math

import jax
import jax.numpy as jnp
from jax import lax
from jax.experimental import pallas as pl
from jax.experimental.pallas import tpu as pltpu
from jax.sharding import Mesh, PartitionSpec as P

AXES = ("line", "mid", "grp")
NOTE_ROWS = 8
RADIX = 256
CHUNKS = 8
VMEM = pl.BlockSpec(memory_space=pltpu.VMEM)
HBM = pl.BlockSpec(memory_space=pltpu.HBM)


def embed_kernel(
    states_hbm, proj_hbm, owner_hbm, sub_hbm, prio_hbm, block_ref,
    states, proj, owner, sub, prio, big_sem, small_sem,
):
    rows, depth = states.shape
    width = proj.shape[1]
    span = depth // CHUNKS
    copies = []
    for i in range(CHUNKS):
        part = pl.ds(i * span, span)
        pair = (
            pltpu.make_async_copy(states_hbm.at[:, part], states.at[:, part], big_sem.at[0, i]),
            pltpu.make_async_copy(proj_hbm.at[part], proj.at[part], big_sem.at[1, i]),
        )
        copies.append(pair)
        for copy in pair:
            copy.start()
    small = [
        pltpu.make_async_copy(src, dst, small_sem.at[i])
        for i, (src, dst) in enumerate(((owner_hbm, owner), (sub_hbm, sub), (prio_hbm, prio)))
    ]
    for copy in small:
        copy.start()
    projected = None
    for i, pair in enumerate(copies):
        for copy in pair:
            copy.wait()
        part = slice(i * span, (i + 1) * span)
        term = jnp.dot(states[:, part], proj[part, :], preferred_element_type=jnp.float32)
        projected = term if projected is None else projected + term
    square_sum = jnp.sum(projected * projected, axis=1, keepdims=True)
    embedding = projected * lax.rsqrt(square_sum + 1e-06)
    for copy in small:
        copy.wait()
    rank = prio[...]
    high = lax.shift_right_logical(rank, 8)
    fields = (owner[...] + 1, sub[...], high, rank - high * RADIX)
    notes = [jnp.broadcast_to(f.astype(jnp.float32), (NOTE_ROWS, rows)) for f in fields]
    notes.append(jnp.zeros((NOTE_ROWS, width - len(fields) * rows), jnp.float32))
    block = jnp.concatenate([embedding, jnp.concatenate(notes, axis=1)], axis=0)
    block_ref[...] = block.astype(jnp.bfloat16)


def embed(states, projection, owner, sub, prio):
    rows, depth = states.shape
    width = projection.shape[1]
    return pl.pallas_call(
        embed_kernel,
        in_specs=[HBM] * 5,
        out_specs=VMEM,
        out_shape=jax.ShapeDtypeStruct((rows + NOTE_ROWS, width), jnp.bfloat16),
        scratch_shapes=[
            pltpu.VMEM((rows, depth), jnp.bfloat16),
            pltpu.VMEM((depth, width), jnp.bfloat16),
            pltpu.VMEM((1, rows), jnp.int32),
            pltpu.VMEM((1, rows), jnp.int32),
            pltpu.VMEM((1, rows), jnp.int32),
            pltpu.SemaphoreType.DMA((2, CHUNKS)),
            pltpu.SemaphoreType.DMA((3,)),
        ],
        compiler_params=pltpu.CompilerParams(vmem_limit_bytes=60 << 20),
        name="embed",
    )(states, projection, owner, sub, prio)


def read_notes(ref, rows):
    tail = ref[rows:, :].astype(jnp.float32)
    owner, sub, high, low = (tail[:1, i * rows:(i + 1) * rows] for i in range(4))
    return (owner - 1.0) * 4.0 + sub, high * float(RADIX) + low


def score_kernel(row_count, lane_count, products, parts, has_lines, seen_rows, hold, *refs):
    refs = list(refs)
    row_refs = [refs.pop(0) for _ in range(row_count)]
    lane_refs = [refs.pop(0) for _ in range(lane_count)]
    seen_lines = refs.pop(0) if has_lines else None
    seen_backs = refs.pop(0) if seen_rows else None
    lines_out = refs.pop(0)
    rows = lines_out.shape[1]
    if hold:
        refs[-1][...] = row_refs[0][...]
    row_notes = [read_notes(ref, rows) for ref in row_refs]
    lane_notes = [read_notes(ref, rows) for ref in lane_refs]
    fill = jnp.zeros((-2 * row_count % 8, rows), jnp.float32)
    lines = [line for pair in row_notes for line in pair]
    columns = jnp.concatenate(lines + ([fill] if fill.size else []), axis=0).T
    best, back = [None] * lane_count, [None] * row_count

    def top(old, new):
        return new if old is None else jnp.maximum(old, new)

    for row_set, lane_set in products:
        cosine = lax.dot_general(
            jnp.concatenate([row_refs[i][:rows, :] for i in row_set], axis=0),
            jnp.concatenate([lane_refs[j][:rows, :] for j in lane_set], axis=0),
            (((1,), (1,)), ((), ())),
            preferred_element_type=jnp.float32,
        )
        for m, i in enumerate(row_set):
            row_cluster, row_prio = columns[:, 2 * i:2 * i + 1], columns[:, 2 * i + 1:2 * i + 2]
            for n, j in enumerate(lane_set):
                lane_cluster, lane_prio = lane_notes[j]
                here = cosine[m * rows:(m + 1) * rows, n * rows:(n + 1) * rows]
                same = jnp.where(row_cluster == lane_cluster, here, -1.0)
                earlier = row_prio < lane_prio
                best[j] = top(best[j], jnp.where(earlier, same, -1.0))
                if j > 0:
                    back[i] = top(back[i], jnp.where(earlier, -1.0, same))
    lane_ids = lax.broadcasted_iota(jnp.int32, (rows, rows), 1)
    table = jnp.full((rows, rows), -1.0, jnp.float32)
    for i, each in enumerate(back):
        if each is not None:
            table = jnp.where(lane_ids == i, jnp.max(each, axis=1, keepdims=True), table)
    table = table.T
    if seen_rows:
        table = jnp.maximum(table[:row_count], seen_backs[...])
    for first, stop in parts:
        refs.pop(0)[...] = table[first:stop]
    lines = jnp.concatenate([jnp.max(b, axis=0, keepdims=True) for b in best], axis=0)
    if has_lines:
        count = seen_lines.shape[0]
        first = jnp.maximum(lines[:count], seen_lines[...])
        lines = first if count == lane_count else jnp.concatenate([first, lines[count:]], axis=0)
    lines_out[...] = lines


def score(name, row_blocks, lane_blocks, products, parts, lines=None, backs=None, hold=False):
    high, width = row_blocks[0].shape
    rows = high - NOTE_ROWS
    inputs = [*row_blocks, *lane_blocks, *(seen for seen in (lines, backs) if seen is not None)]
    shapes = [(len(lane_blocks), rows)] + [(stop - first, rows) for first, stop in parts]
    outs = [jax.ShapeDtypeStruct(shape, jnp.float32) for shape in shapes]
    if hold:
        outs.append(jax.ShapeDtypeStruct((high, width), row_blocks[0].dtype))
    counts = len(row_blocks), len(lane_blocks)
    rest = products, parts, lines is not None, backs is not None, hold
    macs = sum(len(r) * len(c) for r, c in products) * rows * rows * width
    return pl.pallas_call(
        lambda *refs: score_kernel(*counts, *rest, *refs),
        in_specs=[VMEM] * len(inputs),
        out_specs=[VMEM] * len(outs),
        out_shape=outs,
        compiler_params=pltpu.CompilerParams(vmem_limit_bytes=48 << 20),
        cost_estimate=pl.CostEstimate(
            flops=2 * macs, bytes_accessed=2 * sum(counts) * rows * width, transcendentals=0
        ),
        name=name,
    )(*inputs)


def tournament(line):
    moves = [[(i, (i + s) % line) for i in range(line)] for s in range(1, (line + 1) // 2)]
    if line % 2 == 0:
        half = line // 2
        pairs = [(i, i + half) if i % 2 else (i + half, i) for i in range(half)]
        sent, met = {a for a, _ in pairs}, {b for _, b in pairs}
        idle = [i for i in range(line) if i not in sent]
        free = [i for i in range(line) if i not in met]
        moves.append(pairs + list(zip(idle, free)))
    return moves


def on_device(states, projection, owner_group, cluster_sub, priority):
    line, grp = lax.axis_size("line"), lax.axis_size("grp")
    plane = lax.axis_size("mid") * grp
    rows = states.shape[0]

    def move(array, pairs):
        whole = [(a * plane + p, b * plane + p) for a, b in pairs for p in range(plane)]
        return lax.ppermute(array, AXES, whole)

    def swap(array, step):
        pairs = [(i, i // plane * plane + (i % plane ^ step)) for i in range(line * plane)]
        return lax.ppermute(array, AXES, pairs)

    block = embed(
        states,
        projection,
        owner_group.reshape(1, rows),
        cluster_sub.reshape(1, rows),
        priority.reshape(1, rows),
    )
    moves = tournament(line)
    visitors = [move(block, pairs) for pairs in moves]
    bits = [1 << i for i in range(1, plane.bit_length() - 1)]
    row_blocks = [block] + [swap(block, step) for step in range(2, plane, 2)]

    lanes = [block] + visitors
    every, count = tuple(range(len(lanes))), len(row_blocks)
    most, last = tuple(range(count - 1)), (count - 1,)
    lines, backs, held = score(
        "score_soon", row_blocks[:-1], lanes[:-1], [(most, every[:-1])], [(0, count)], hold=True
    )
    row_blocks[0] = held
    partner = [lax.optimization_barrier((block, visitors[0]))[0], *visitors]
    partner[-1] = lax.optimization_barrier((partner[-1], held))[0]
    partner = [swap(lane, 1) for lane in partner]
    lanes[0] = held
    products = [(last, every), (most, every[-1:])]
    lines, backs = score(
        "score_late", row_blocks, lanes, products, [(0, count)], lines, backs
    )
    half = count // 2
    products, parts = [(most + last, every)], [(0, half), (half, count)]
    theirs, near, far = score("score_partner", row_blocks, partner, products, parts, None, backs)
    lines = jnp.maximum(lines, swap(theirs, 1))
    for bit in bits[:0:-1]:
        near = jnp.maximum(near, swap(far, bit))
        half = near.shape[0] // 2
        near, far = near[:half], near[half:]
    total = lines[:1]
    for i, pairs in reversed(list(enumerate(moves))):
        total = jnp.maximum(total, move(lines[i + 1:i + 2], [(b, a) for a, b in pairs]))
    total = lax.optimization_barrier(total)
    total = jnp.maximum(jnp.maximum(total, near), swap(far, bits[0]))
    return total.reshape(rows)


def solution(mesh):
    num_dp, num_grp = mesh.shape["dp"], mesh.shape["grp"]
    line = min(num_dp, 1 << (int(math.log2(num_dp * num_grp)) // 2))
    split = Mesh(mesh.devices.reshape(line, num_dp // line, num_grp), AXES)
    in_specs = (P(AXES, None), P(), P(AXES, None), P(AXES), P(AXES))
    return jax.shard_map(
        on_device, mesh=split, in_specs=in_specs, out_specs=P(AXES), check_vma=False
    )
```

```python
import math

import jax
import jax.numpy as jnp
from jax import lax
from jax.experimental import pallas as pl
from jax.experimental.pallas import tpu as pltpu
from jax.sharding import Mesh, PartitionSpec as P

AXES = ("line", "mid", "grp")
NOTE_ROWS = 8
RADIX = 256
CHUNKS = 8
AHEAD = 3
VMEM = pl.BlockSpec(memory_space=pltpu.VMEM)
HBM = pl.BlockSpec(memory_space=pltpu.HBM)


def embed_kernel(
    states_hbm, proj_hbm, owner_hbm, sub_hbm, prio_hbm, block_ref,
    states, proj, owner, sub, prio, big_sem, small_sem,
):
    rows, depth = states.shape
    width = proj.shape[1]
    span = depth // CHUNKS
    copies = []
    for i in range(CHUNKS):
        part = pl.ds(i * span, span)
        copies.append((
            pltpu.make_async_copy(states_hbm.at[:, part], states.at[:, part], big_sem.at[0, i]),
            pltpu.make_async_copy(proj_hbm.at[part], proj.at[part], big_sem.at[1, i]),
        ))
    small = [
        pltpu.make_async_copy(src, dst, small_sem.at[i])
        for i, (src, dst) in enumerate(((owner_hbm, owner), (sub_hbm, sub), (prio_hbm, prio)))
    ]
    for copy in [c for pair in copies[:AHEAD] for c in pair] + small:
        copy.start()
    projected = None
    for i, pair in enumerate(copies):
        for copy in pair:
            copy.wait()
        if i + AHEAD < CHUNKS:
            for copy in copies[i + AHEAD]:
                copy.start()
        part = slice(i * span, (i + 1) * span)
        term = jnp.dot(states[:, part], proj[part, :], preferred_element_type=jnp.float32)
        projected = term if projected is None else projected + term
    square_sum = jnp.sum(projected * projected, axis=1, keepdims=True)
    embedding = projected * lax.rsqrt(square_sum + 1e-06)
    for copy in small:
        copy.wait()
    rank = prio[...]
    high = lax.shift_right_logical(rank, 8)
    fields = (owner[...] + 1, sub[...], high, rank - high * RADIX)
    notes = [f.astype(jnp.float32) for f in fields]
    notes.append(jnp.zeros((NOTE_ROWS - len(fields), rows), jnp.float32))
    tiles = [embedding[:, i:i + rows] for i in range(0, width, rows)]
    block_ref[...] = jnp.concatenate(tiles + notes, axis=0).astype(jnp.bfloat16)


def embed(states, projection, owner, sub, prio):
    rows, depth = states.shape
    width = projection.shape[1]
    high = rows * (width // rows) + NOTE_ROWS
    return pl.pallas_call(
        embed_kernel,
        in_specs=[HBM] * 5,
        out_specs=VMEM,
        out_shape=jax.ShapeDtypeStruct((high, rows), jnp.bfloat16),
        scratch_shapes=[
            pltpu.VMEM((rows, depth), jnp.bfloat16),
            pltpu.VMEM((depth, width), jnp.bfloat16),
            pltpu.VMEM((1, rows), jnp.int32),
            pltpu.VMEM((1, rows), jnp.int32),
            pltpu.VMEM((1, rows), jnp.int32),
            pltpu.SemaphoreType.DMA((2, CHUNKS)),
            pltpu.SemaphoreType.DMA((3,)),
        ],
        compiler_params=pltpu.CompilerParams(vmem_limit_bytes=60 << 20),
        name="embed",
    )(states, projection, owner, sub, prio)


def read_notes(ref):
    tail = ref[ref.shape[0] - NOTE_ROWS:, :].astype(jnp.float32)
    owner, sub, high, low = (tail[i:i + 1] for i in range(4))
    return (owner - 1.0) * 4.0 + sub, high * float(RADIX) + low


def read_rows(refs):
    rows = refs[0].shape[1]
    firsts = range(0, refs[0].shape[0] - NOTE_ROWS, rows)
    return jnp.concatenate(
        [jnp.concatenate([ref[first:first + rows, :] for ref in refs], axis=0) for first in firsts],
        axis=1,
    )


def score_kernel(row_count, lane_count, products, parts, has_lines, seen_rows, hold, *refs):
    refs = list(refs)
    row_refs = [refs.pop(0) for _ in range(row_count)]
    lane_refs = [refs.pop(0) for _ in range(lane_count)]
    seen_lines = refs.pop(0) if has_lines else None
    seen_backs = refs.pop(0) if seen_rows else None
    lines_out = refs.pop(0)
    rows = lines_out.shape[1]
    if hold:
        refs[-1][...] = row_refs[0][...]
    row_notes = [read_notes(ref) for ref in row_refs]
    lane_notes = [read_notes(ref) for ref in lane_refs]
    fill = jnp.zeros((-2 * row_count % 8, rows), jnp.float32)
    lines = [line for pair in row_notes for line in pair]
    columns = jnp.concatenate(lines + ([fill] if fill.size else []), axis=0).T
    best, back = [None] * lane_count, [None] * row_count

    def top(old, new):
        return new if old is None else jnp.maximum(old, new)

    for row_set, lane_set in products:
        cosine = lax.dot_general(
            read_rows([row_refs[i] for i in row_set]),
            read_rows([lane_refs[j] for j in lane_set]),
            (((1,), (1,)), ((), ())),
            preferred_element_type=jnp.float32,
        )
        for m, i in enumerate(row_set):
            row_cluster, row_prio = columns[:, 2 * i:2 * i + 1], columns[:, 2 * i + 1:2 * i + 2]
            for n, j in enumerate(lane_set):
                lane_cluster, lane_prio = lane_notes[j]
                here = cosine[m * rows:(m + 1) * rows, n * rows:(n + 1) * rows]
                same = jnp.where(row_cluster == lane_cluster, here, -1.0)
                earlier = row_prio < lane_prio
                best[j] = top(best[j], jnp.where(earlier, same, -1.0))
                if j > 0:
                    back[i] = top(back[i], jnp.where(earlier, -1.0, same))
    lane_ids = lax.broadcasted_iota(jnp.int32, (rows, rows), 1)
    table = jnp.full((rows, rows), -1.0, jnp.float32)
    for i, each in enumerate(back):
        if each is not None:
            table = jnp.where(lane_ids == i, jnp.max(each, axis=1, keepdims=True), table)
    table = table.T
    if seen_rows:
        table = jnp.maximum(table[:row_count], seen_backs[...])
    for first, stop in parts:
        refs.pop(0)[...] = table[first:stop]
    lines = jnp.concatenate([jnp.max(b, axis=0, keepdims=True) for b in best], axis=0)
    if has_lines:
        count = seen_lines.shape[0]
        first = jnp.maximum(lines[:count], seen_lines[...])
        lines = first if count == lane_count else jnp.concatenate([first, lines[count:]], axis=0)
    lines_out[...] = lines


def score(name, row_blocks, lane_blocks, products, parts, lines=None, backs=None, hold=False):
    high, rows = row_blocks[0].shape
    width = high - NOTE_ROWS
    inputs = [*row_blocks, *lane_blocks, *(seen for seen in (lines, backs) if seen is not None)]
    shapes = [(len(lane_blocks), rows)] + [(stop - first, rows) for first, stop in parts]
    outs = [jax.ShapeDtypeStruct(shape, jnp.float32) for shape in shapes]
    if hold:
        outs.append(jax.ShapeDtypeStruct((high, rows), row_blocks[0].dtype))
    counts = len(row_blocks), len(lane_blocks)
    rest = products, parts, lines is not None, backs is not None, hold
    macs = sum(len(r) * len(c) for r, c in products) * rows * rows * width
    return pl.pallas_call(
        lambda *refs: score_kernel(*counts, *rest, *refs),
        in_specs=[VMEM] * len(inputs),
        out_specs=[VMEM] * len(outs),
        out_shape=outs,
        compiler_params=pltpu.CompilerParams(vmem_limit_bytes=48 << 20),
        cost_estimate=pl.CostEstimate(
            flops=2 * macs, bytes_accessed=2 * sum(counts) * rows * width, transcendentals=0
        ),
        name=name,
    )(*inputs)


def tournament(line):
    if line == 4:
        return [[(3, 0), (0, 2), (2, 1), (1, 3)], [(0, 1), (1, 0), (2, 3), (3, 2)]]
    moves = [[(i, (i + s) % line) for i in range(line)] for s in range(1, (line + 1) // 2)]
    if line % 2 == 0:
        half = line // 2
        pairs = [(i, i + half) if i % 2 else (i + half, i) for i in range(half)]
        sent, met = {a for a, _ in pairs}, {b for _, b in pairs}
        idle = [i for i in range(line) if i not in sent]
        free = [i for i in range(line) if i not in met]
        moves.append(pairs + list(zip(idle, free)))
    return moves


def on_device(states, projection, owner_group, cluster_sub, priority):
    line, grp = lax.axis_size("line"), lax.axis_size("grp")
    plane = lax.axis_size("mid") * grp
    rows = states.shape[0]

    def move(array, pairs):
        whole = [(a * plane + p, b * plane + p) for a, b in pairs for p in range(plane)]
        return lax.ppermute(array, AXES, whole)

    def swap(array, step):
        pairs = [(i, i // plane * plane + (i % plane ^ step)) for i in range(line * plane)]
        return lax.ppermute(array, AXES, pairs)

    block = embed(
        states,
        projection,
        owner_group.reshape(1, rows),
        cluster_sub.reshape(1, rows),
        priority.reshape(1, rows),
    )
    moves = tournament(line)
    visitors = [move(block, pairs) for pairs in moves]
    bits = [1 << i for i in range(1, plane.bit_length() - 1)]
    row_blocks = [block] + [swap(block, step) for step in range(2, plane, 2)]

    lanes = [block] + visitors
    every, count = tuple(range(len(lanes))), len(row_blocks)
    half = count // 2
    most, last = tuple(range(half)), tuple(range(half, count))
    lines, backs, held = score(
        "score_soon", row_blocks[:half], lanes[:-1], [(most, every[:-1])], [(0, count)], hold=True
    )
    row_blocks[0] = held
    partner = [lax.optimization_barrier((block, visitors[0]))[0], *visitors]
    partner[-1] = lax.optimization_barrier((partner[-1], held))[0]
    partner = [swap(lane, 1) for lane in partner]
    lanes[0] = held
    products = [(last, every), (most, every[-1:])]
    lines, backs = score(
        "score_late", row_blocks, lanes, products, [(0, count)], lines, backs
    )
    products, parts = [(most + last, every)], [(0, half), (half, count)]
    theirs, near, far = score("score_partner", row_blocks, partner, products, parts, None, backs)
    lines = jnp.maximum(lines, swap(theirs, 1))
    for bit in bits[:0:-1]:
        near = jnp.maximum(near, swap(far, bit))
        half = near.shape[0] // 2
        near, far = near[:half], near[half:]
    total = lines[:1]
    for i, pairs in reversed(list(enumerate(moves))):
        total = jnp.maximum(total, move(lines[i + 1:i + 2], [(b, a) for a, b in pairs]))
    total = lax.optimization_barrier(total)
    total = jnp.maximum(jnp.maximum(total, near), swap(far, bits[0]))
    return total.reshape(rows)


def solution(mesh):
    num_dp, num_grp = mesh.shape["dp"], mesh.shape["grp"]
    line = min(num_dp, 1 << (int(math.log2(num_dp * num_grp)) // 2))
    split = Mesh(mesh.devices.reshape(line, num_dp // line, num_grp), AXES)
    in_specs = (P(AXES, None), P(), P(AXES, None), P(AXES), P(AXES))
    return jax.shard_map(
        on_device, mesh=split, in_specs=in_specs, out_specs=P(AXES), check_vma=False
    )
```

```python
import math

import jax
import jax.numpy as jnp
from jax import lax
from jax.experimental import pallas as pl
from jax.experimental.pallas import tpu as pltpu
from jax.sharding import Mesh, PartitionSpec as P

AXES = ("line", "mid", "grp")
NOTE_ROWS = 8
RADIX = 256
CHUNKS = 8
VMEM = pl.BlockSpec(memory_space=pltpu.VMEM)
HBM = pl.BlockSpec(memory_space=pltpu.HBM)


def embed_kernel(
    states_hbm, proj_hbm, owner_hbm, sub_hbm, prio_hbm, block_ref,
    states, proj, owner, sub, prio, big_sem, small_sem,
):
    rows, depth = states.shape
    width = proj.shape[1]
    span = depth // CHUNKS
    copies = []
    for i in range(CHUNKS):
        part = pl.ds(i * span, span)
        copies.append((
            pltpu.make_async_copy(states_hbm.at[:, part], states.at[:, part], big_sem.at[0, i]),
            pltpu.make_async_copy(proj_hbm.at[part], proj.at[part], big_sem.at[1, i]),
        ))
    small = [
        pltpu.make_async_copy(src, dst, small_sem.at[i])
        for i, (src, dst) in enumerate(((owner_hbm, owner), (sub_hbm, sub), (prio_hbm, prio)))
    ]
    for copy in [c for pair in copies for c in pair] + small:
        copy.start()
    projected = None
    for i, pair in enumerate(copies):
        for copy in pair:
            copy.wait()
        part = slice(i * span, (i + 1) * span)
        term = jnp.dot(states[:, part], proj[part, :], preferred_element_type=jnp.float32)
        projected = term if projected is None else projected + term
    square_sum = jnp.sum(projected * projected, axis=1, keepdims=True)
    embedding = projected * lax.rsqrt(square_sum + 1e-06)
    for copy in small:
        copy.wait()
    rank = prio[...]
    high = lax.shift_right_logical(rank, 8)
    fields = (owner[...] + 1, sub[...], high, rank - high * RADIX)
    notes = [f.astype(jnp.float32) for f in fields]
    notes.append(jnp.zeros((NOTE_ROWS - len(fields), rows), jnp.float32))
    tiles = [embedding[:, i:i + rows] for i in range(0, width, rows)]
    block_ref[...] = jnp.concatenate(tiles + notes, axis=0).astype(jnp.bfloat16)


def embed(states, projection, owner, sub, prio):
    rows, depth = states.shape
    width = projection.shape[1]
    high = rows * (width // rows) + NOTE_ROWS
    return pl.pallas_call(
        embed_kernel,
        in_specs=[HBM] * 5,
        out_specs=VMEM,
        out_shape=jax.ShapeDtypeStruct((high, rows), jnp.bfloat16),
        scratch_shapes=[
            pltpu.VMEM((rows, depth), jnp.bfloat16),
            pltpu.VMEM((depth, width), jnp.bfloat16),
            pltpu.VMEM((1, rows), jnp.int32),
            pltpu.VMEM((1, rows), jnp.int32),
            pltpu.VMEM((1, rows), jnp.int32),
            pltpu.SemaphoreType.DMA((2, CHUNKS)),
            pltpu.SemaphoreType.DMA((3,)),
        ],
        compiler_params=pltpu.CompilerParams(vmem_limit_bytes=60 << 20),
        name="embed",
    )(states, projection, owner, sub, prio)


def read_notes(ref):
    tail = ref[ref.shape[0] - NOTE_ROWS:, :].astype(jnp.float32)
    owner, sub, high, low = (tail[i:i + 1] for i in range(4))
    return (owner - 1.0) * 4.0 + sub, high * float(RADIX) + low


def read_rows(refs):
    rows = refs[0].shape[1]
    firsts = range(0, refs[0].shape[0] - NOTE_ROWS, rows)
    return jnp.concatenate(
        [jnp.concatenate([ref[first:first + rows, :] for ref in refs], axis=0) for first in firsts],
        axis=1,
    )


def score_kernel(row_count, lane_count, products, parts, has_lines, seen_rows, hold, *refs):
    refs = list(refs)
    row_refs = [refs.pop(0) for _ in range(row_count)]
    lane_refs = [refs.pop(0) for _ in range(lane_count)]
    seen_lines = refs.pop(0) if has_lines else None
    seen_backs = refs.pop(0) if seen_rows else None
    lines_out = refs.pop(0)
    rows = lines_out.shape[1]
    if hold:
        refs[-1][...] = row_refs[0][...]
    row_notes = [read_notes(ref) for ref in row_refs]
    lane_notes = [read_notes(ref) for ref in lane_refs]
    fill = jnp.zeros((-2 * row_count % 8, rows), jnp.float32)
    lines = [line for pair in row_notes for line in pair]
    columns = jnp.concatenate(lines + ([fill] if fill.size else []), axis=0).T
    best, back = [None] * lane_count, [None] * row_count

    def top(old, new):
        return new if old is None else jnp.maximum(old, new)

    for row_set, lane_set in products:
        cosine = lax.dot_general(
            read_rows([row_refs[i] for i in row_set]),
            read_rows([lane_refs[j] for j in lane_set]),
            (((1,), (1,)), ((), ())),
            preferred_element_type=jnp.float32,
        )
        for m, i in enumerate(row_set):
            row_cluster, row_prio = columns[:, 2 * i:2 * i + 1], columns[:, 2 * i + 1:2 * i + 2]
            for n, j in enumerate(lane_set):
                lane_cluster, lane_prio = lane_notes[j]
                here = cosine[m * rows:(m + 1) * rows, n * rows:(n + 1) * rows]
                same = jnp.where(row_cluster == lane_cluster, here, -1.0)
                earlier = row_prio < lane_prio
                best[j] = top(best[j], jnp.where(earlier, same, -1.0))
                if j > 0:
                    back[i] = top(back[i], jnp.where(earlier, -1.0, same))
    lane_ids = lax.broadcasted_iota(jnp.int32, (rows, rows), 1)
    table = jnp.full((rows, rows), -1.0, jnp.float32)
    for i, each in enumerate(back):
        if each is not None:
            table = jnp.where(lane_ids == i, jnp.max(each, axis=1, keepdims=True), table)
    table = table.T
    if seen_rows:
        table = jnp.maximum(table[:row_count], seen_backs[...])
    for first, stop in parts:
        refs.pop(0)[...] = table[first:stop]
    lines = jnp.concatenate([jnp.max(b, axis=0, keepdims=True) for b in best], axis=0)
    if has_lines:
        count = seen_lines.shape[0]
        first = jnp.maximum(lines[:count], seen_lines[...])
        lines = first if count == lane_count else jnp.concatenate([first, lines[count:]], axis=0)
    lines_out[...] = lines


def score(name, row_blocks, lane_blocks, products, parts, lines=None, backs=None, hold=False):
    high, rows = row_blocks[0].shape
    width = high - NOTE_ROWS
    inputs = [*row_blocks, *lane_blocks, *(seen for seen in (lines, backs) if seen is not None)]
    shapes = [(len(lane_blocks), rows)] + [(stop - first, rows) for first, stop in parts]
    outs = [jax.ShapeDtypeStruct(shape, jnp.float32) for shape in shapes]
    if hold:
        outs.append(jax.ShapeDtypeStruct((high, rows), row_blocks[0].dtype))
    counts = len(row_blocks), len(lane_blocks)
    rest = products, parts, lines is not None, backs is not None, hold
    macs = sum(len(r) * len(c) for r, c in products) * rows * rows * width
    return pl.pallas_call(
        lambda *refs: score_kernel(*counts, *rest, *refs),
        in_specs=[VMEM] * len(inputs),
        out_specs=[VMEM] * len(outs),
        out_shape=outs,
        compiler_params=pltpu.CompilerParams(vmem_limit_bytes=48 << 20),
        cost_estimate=pl.CostEstimate(
            flops=2 * macs, bytes_accessed=2 * sum(counts) * rows * width, transcendentals=0
        ),
        name=name,
    )(*inputs)


def tournament(line):
    moves = [[(i, (i + s) % line) for i in range(line)] for s in range(1, (line + 1) // 2)]
    if line % 2 == 0:
        half = line // 2
        pairs = [(i, i + half) if i % 2 else (i + half, i) for i in range(half)]
        sent, met = {a for a, _ in pairs}, {b for _, b in pairs}
        idle = [i for i in range(line) if i not in sent]
        free = [i for i in range(line) if i not in met]
        moves.append(pairs + list(zip(idle, free)))
    return moves


def on_device(states, projection, owner_group, cluster_sub, priority):
    line, grp = lax.axis_size("line"), lax.axis_size("grp")
    plane = lax.axis_size("mid") * grp
    rows = states.shape[0]

    def move(array, pairs):
        whole = [(a * plane + p, b * plane + p) for a, b in pairs for p in range(plane)]
        return lax.ppermute(array, AXES, whole)

    def swap(array, step):
        pairs = [(i, i // plane * plane + (i % plane ^ step)) for i in range(line * plane)]
        return lax.ppermute(array, AXES, pairs)

    block = embed(
        states,
        projection,
        owner_group.reshape(1, rows),
        cluster_sub.reshape(1, rows),
        priority.reshape(1, rows),
    )
    moves = tournament(line)
    visitors = [move(block, pairs) for pairs in moves]
    bits = [1 << i for i in range(1, plane.bit_length() - 1)]
    found = {0: block}
    for bit in reversed(bits):
        found |= {step | bit: swap(here, bit) for step, here in found.items()}
    row_blocks = [found[step] for step in sorted(found)]

    lanes = [block] + visitors
    every, count = tuple(range(len(lanes))), len(row_blocks)
    half = count // 2
    soon = (0, half)
    rest = tuple(i for i in range(count) if i not in soon)
    lines, held = score(
        "score_soon", [row_blocks[i] for i in soon], lanes[:1], [((0, 1), (0,))], [], hold=True
    )
    row_blocks[0] = lanes[0] = held
    products = [(rest, every), (soon, every[1:])]
    lines, backs = score("score_late", row_blocks, lanes, products, [(0, count)], lines)
    ready = lax.optimization_barrier((lanes[-1], row_blocks[1], held, *visitors[:-1]))[0]
    partner = [swap(lane, 1) for lane in lanes[:-1] + [ready]]
    products, parts = [(tuple(range(count)), every)], [(0, half), (half, count)]
    theirs, near, far = score("score_partner", row_blocks, partner, products, parts, None, backs)
    lines = jnp.maximum(lines, swap(theirs, 1))
    for bit in bits[:0:-1]:
        near = jnp.maximum(near, swap(far, bit))
        half = near.shape[0] // 2
        near, far = near[:half], near[half:]
    total = lines[:1]
    for i, pairs in reversed(list(enumerate(moves))):
        total = jnp.maximum(total, move(lines[i + 1:i + 2], [(b, a) for a, b in pairs]))
    total = lax.optimization_barrier(total)
    total = jnp.maximum(jnp.maximum(total, near), swap(far, bits[0]))
    return total.reshape(rows)


def solution(mesh):
    num_dp, num_grp = mesh.shape["dp"], mesh.shape["grp"]
    line = min(num_dp, 1 << (int(math.log2(num_dp * num_grp)) // 2))
    split = Mesh(mesh.devices.reshape(line, num_dp // line, num_grp), AXES)
    in_specs = (P(AXES, None), P(), P(AXES, None), P(AXES), P(AXES))
    return jax.shard_map(
        on_device, mesh=split, in_specs=in_specs, out_specs=P(AXES), check_vma=False
    )
```

```python
import math

import jax
import jax.numpy as jnp
from jax import lax
from jax.experimental import pallas as pl
from jax.experimental.pallas import tpu as pltpu
from jax.sharding import Mesh, PartitionSpec as P

AXES = ("line", "mid", "grp")
NOTE_ROWS = 8
RADIX = 256
CHUNKS = 8
VMEM = pl.BlockSpec(memory_space=pltpu.VMEM)
HBM = pl.BlockSpec(memory_space=pltpu.HBM)


def embed_kernel(
    states_hbm, proj_hbm, owner_hbm, sub_hbm, prio_hbm, block_ref,
    states, proj, owner, sub, prio, big_sem, small_sem,
):
    rows, depth = states.shape
    width = proj.shape[1]
    span = depth // CHUNKS
    copies = []
    for i in range(CHUNKS):
        part = pl.ds(i * span, span)
        copies.append((
            pltpu.make_async_copy(states_hbm.at[:, part], states.at[:, part], big_sem.at[0, i]),
            pltpu.make_async_copy(proj_hbm.at[part], proj.at[part], big_sem.at[1, i]),
        ))
    small = [
        pltpu.make_async_copy(src, dst, small_sem.at[i])
        for i, (src, dst) in enumerate(((owner_hbm, owner), (sub_hbm, sub), (prio_hbm, prio)))
    ]
    for copy in [c for pair in copies for c in pair] + small:
        copy.start()
    projected = None
    for i, pair in enumerate(copies):
        for copy in pair:
            copy.wait()
        part = slice(i * span, (i + 1) * span)
        term = jnp.dot(states[:, part], proj[part, :], preferred_element_type=jnp.float32)
        projected = term if projected is None else projected + term
    square_sum = jnp.sum(projected * projected, axis=1, keepdims=True)
    embedding = projected * lax.rsqrt(square_sum + 1e-06)
    for copy in small:
        copy.wait()
    rank = prio[...]
    high = lax.shift_right_logical(rank, 8)
    fields = (owner[...] + 1, sub[...], high, rank - high * RADIX)
    notes = [f.astype(jnp.float32) for f in fields]
    notes.append(jnp.zeros((NOTE_ROWS - len(fields), rows), jnp.float32))
    tiles = [embedding[:, i:i + rows] for i in range(0, width, rows)]
    block_ref[...] = jnp.concatenate(tiles + notes, axis=0).astype(jnp.bfloat16)


def embed(states, projection, owner, sub, prio):
    rows, depth = states.shape
    width = projection.shape[1]
    high = rows * (width // rows) + NOTE_ROWS
    return pl.pallas_call(
        embed_kernel,
        in_specs=[HBM] * 5,
        out_specs=VMEM,
        out_shape=jax.ShapeDtypeStruct((high, rows), jnp.bfloat16),
        scratch_shapes=[
            pltpu.VMEM((rows, depth), jnp.bfloat16),
            pltpu.VMEM((depth, width), jnp.bfloat16),
            pltpu.VMEM((1, rows), jnp.int32),
            pltpu.VMEM((1, rows), jnp.int32),
            pltpu.VMEM((1, rows), jnp.int32),
            pltpu.SemaphoreType.DMA((2, CHUNKS)),
            pltpu.SemaphoreType.DMA((3,)),
        ],
        compiler_params=pltpu.CompilerParams(vmem_limit_bytes=60 << 20),
        name="embed",
    )(states, projection, owner, sub, prio)


def read_notes(block):
    ref = block[-1]
    tail = ref[ref.shape[0] - NOTE_ROWS:, :].astype(jnp.float32)
    owner, sub, high, low = (tail[i:i + 1] for i in range(4))
    return (owner - 1.0) * 4.0 + sub, high * float(RADIX) + low


def read_rows(blocks):
    rows = blocks[0][0].shape[1]
    tiles = [
        [ref[i * rows:(i + 1) * rows, :] for ref in block for i in range(ref.shape[0] // rows)]
        for block in blocks
    ]
    return jnp.concatenate([jnp.concatenate(column, axis=0) for column in zip(*tiles)], axis=1)


def score_kernel(row_sizes, lane_sizes, home, products, parts, has_lines, prefix, has_backs, hold, *refs):
    refs = list(refs)
    row_refs = [[refs.pop(0) for _ in range(size)] for size in row_sizes]
    lane_refs = [[refs.pop(0) for _ in range(size)] for size in lane_sizes]
    row_count, lane_count = len(row_refs), len(lane_refs)
    seen_lines = refs.pop(0) if has_lines else None
    seen_backs = refs.pop(0) if has_backs else None
    line_parts, back_parts = parts
    rows = refs[0].shape[1]
    if hold:
        refs[-1][...] = row_refs[0][0][...]
    row_notes = [read_notes(ref) for ref in row_refs]
    lane_notes = [read_notes(ref) for ref in lane_refs]
    fill = jnp.zeros((-2 * row_count % 8, rows), jnp.float32)
    lines = [line for pair in row_notes for line in pair]
    columns = jnp.concatenate(lines + ([fill] if fill.size else []), axis=0).T
    best, back = [None] * lane_count, [None] * row_count

    def top(old, new):
        return new if old is None else jnp.maximum(old, new)

    for row_set, lane_set in products:
        cosine = lax.dot_general(
            read_rows([row_refs[i] for i in row_set]),
            read_rows([lane_refs[j] for j in lane_set]),
            (((1,), (1,)), ((), ())),
            preferred_element_type=jnp.float32,
        )
        for m, i in enumerate(row_set):
            row_cluster, row_prio = columns[:, 2 * i:2 * i + 1], columns[:, 2 * i + 1:2 * i + 2]
            for n, j in enumerate(lane_set):
                lane_cluster, lane_prio = lane_notes[j]
                here = cosine[m * rows:(m + 1) * rows, n * rows:(n + 1) * rows]
                same = jnp.where(row_cluster == lane_cluster, here, -1.0)
                earlier = row_prio < lane_prio
                best[j] = top(best[j], jnp.where(earlier, same, -1.0))
                if j not in home:
                    back[i] = top(back[i], jnp.where(earlier, -1.0, same))
    lane_ids = lax.broadcasted_iota(jnp.int32, (rows, rows), 1)
    table = jnp.full((rows, rows), -1.0, jnp.float32)
    for i, each in enumerate(back):
        if each is not None:
            table = jnp.where(lane_ids == i, jnp.max(each, axis=1, keepdims=True), table)
    table = table.T
    lines = [jnp.max(each, axis=0, keepdims=True) for each in best]
    if prefix:
        lines = [seen_lines[...]] + lines
    elif has_lines:
        for j in range(seen_lines.shape[0]):
            lines[j] = jnp.maximum(lines[j], seen_lines[j:j + 1, :])
    for first, stop in line_parts:
        refs.pop(0)[...] = jnp.concatenate(lines[first:stop], axis=0)
    if has_backs:
        table = jnp.maximum(table[:row_count], seen_backs[...])
    for first, stop in back_parts:
        refs.pop(0)[...] = table[first:stop]


def score(
    name, row_blocks, lane_blocks, home, products, line_parts, back_parts,
    lines=None, prefix=False, backs=None, hold=False,
):
    high, rows = row_blocks[0][0].shape
    width = high - NOTE_ROWS
    inputs = [part for block in (*row_blocks, *lane_blocks) for part in block]
    inputs += [seen for seen in (lines, backs) if seen is not None]
    ahead = lines.shape[0] if prefix else 0
    heights = [stop - first + ahead for first, stop in line_parts]
    heights += [stop - first for first, stop in back_parts]
    outs = [jax.ShapeDtypeStruct((height, rows), jnp.float32) for height in heights]
    if hold:
        outs.append(jax.ShapeDtypeStruct((high, rows), row_blocks[0][0].dtype))
    sizes = tuple(map(len, row_blocks)), tuple(map(len, lane_blocks))
    if prefix:
        line_parts = [(0, 1 + len(lane_blocks))]
    flags = lines is not None, prefix, backs is not None, hold
    macs = sum(len(r) * len(c) for r, c in products) * rows * rows * width
    return pl.pallas_call(
        lambda *refs: score_kernel(*sizes, home, products, (line_parts, back_parts), *flags, *refs),
        in_specs=[VMEM] * len(inputs),
        out_specs=[VMEM] * len(outs),
        out_shape=outs,
        compiler_params=pltpu.CompilerParams(vmem_limit_bytes=48 << 20),
        cost_estimate=pl.CostEstimate(
            flops=2 * macs,
            bytes_accessed=2 * (len(row_blocks) + len(lane_blocks)) * rows * width,
            transcendentals=0,
        ),
        name=name,
    )(*inputs)


def tournament(line):
    moves = [[(i, (i + s) % line) for i in range(line)] for s in range(1, (line + 1) // 2)]
    if line % 2 == 0:
        half = line // 2
        pairs = [(i, i + half) if i % 2 else (i + half, i) for i in range(half)]
        sent, met = {a for a, _ in pairs}, {b for _, b in pairs}
        idle = [i for i in range(line) if i not in sent]
        free = [i for i in range(line) if i not in met]
        moves.append(pairs + list(zip(idle, free)))
    return moves


def on_device(states, projection, owner_group, cluster_sub, priority):
    line, grp = lax.axis_size("line"), lax.axis_size("grp")
    plane = lax.axis_size("mid") * grp
    rows = states.shape[0]

    def move(array, pairs):
        whole = [(a * plane + p, b * plane + p) for a, b in pairs for p in range(plane)]
        return lax.ppermute(array, AXES, whole)

    def swap(array, step):
        pairs = [(i, i // plane * plane + (i % plane ^ step)) for i in range(line * plane)]
        return lax.ppermute(array, AXES, pairs)

    block = embed(
        states,
        projection,
        owner_group.reshape(1, rows),
        cluster_sub.reshape(1, rows),
        priority.reshape(1, rows),
    )
    moves = tournament(line)
    visitors = [move(block, pairs) for pairs in moves]
    bits = [1 << i for i in range(1, plane.bit_length() - 1)]
    cut = block.shape[0] // (2 * rows) * rows

    def halves(parts):
        whole = lax.optimization_barrier((parts[0], visitors[0]))[0]
        return parts if len(parts) > 1 else (whole[:cut], whole[cut:])

    found = {0: (block,)}
    for bit in bits:
        found[bit] = (swap(block, bit),)
    for step in range(0, plane, 2):
        if step not in found:
            low, high = step & -step, 1 << (step.bit_length() - 1)
            upper, lower = halves(found[step ^ high])[0], halves(found[step ^ low])[1]
            found[step] = swap(upper, high), swap(lower, low)
    row_blocks = [found[step] for step in sorted(found)]

    count, mine = len(row_blocks), 1 + len(visitors)
    half, every = count // 2, tuple(range(count))
    soon, known = tuple(range(half + 1)), tuple(range(mine - 1))
    rest = every[half + 1:]
    lines, backs, held = score(
        "score_early", [row_blocks[i] for i in soon], [(lane,) for lane in [block] + visitors[:-1]],
        (0,), [(soon, known)], [(0, mine - 1)], [(0, count)], hold=True,
    )
    row_blocks[0] = (held,)
    own = lax.optimization_barrier((block, visitors[0]))[0]
    partner = [swap(lane, 1) for lane in [own] + visitors[:-1]]
    ready = lax.optimization_barrier((visitors[-1], held, *partner, *row_blocks[-1]))[0]
    lanes = [(lane,) for lane in [held] + visitors + partner]
    numbers = tuple(range(len(lanes)))
    lines, theirs, backs = score(
        "score_most", row_blocks, lanes, (0, mine), [(rest, numbers), (soon, numbers[mine - 1:])],
        [(0, mine), (mine, len(lanes))], [(0, count)], lines, False, backs,
    )
    theirs, near, far = score(
        "score_last", row_blocks, [(swap(ready, 1),)], (), [(every, (0,))],
        [(0, 1)], [(0, half), (half, count)], theirs, True, backs,
    )
    lines = jnp.maximum(lines, swap(theirs, 1))
    for bit in bits[:0:-1]:
        near = jnp.maximum(near, swap(far, bit))
        half = near.shape[0] // 2
        near, far = near[:half], near[half:]
    total = lines[:1]
    for i, pairs in reversed(list(enumerate(moves))):
        total = jnp.maximum(total, move(lines[i + 1:i + 2], [(b, a) for a, b in pairs]))
    total = lax.optimization_barrier(total)
    total = jnp.maximum(jnp.maximum(total, near), swap(far, bits[0]))
    return total.reshape(rows)


def solution(mesh):
    num_dp, num_grp = mesh.shape["dp"], mesh.shape["grp"]
    line = min(num_dp, 1 << (int(math.log2(num_dp * num_grp)) // 2))
    split = Mesh(mesh.devices.reshape(line, num_dp // line, num_grp), AXES)
    in_specs = (P(AXES, None), P(), P(AXES, None), P(AXES), P(AXES))
    return jax.shard_map(
        on_device, mesh=split, in_specs=in_specs, out_specs=P(AXES), check_vma=False
    )
```

```python
import math

import jax
import jax.numpy as jnp
from jax import lax
from jax.experimental import pallas as pl
from jax.experimental.pallas import tpu as pltpu
from jax.sharding import Mesh, PartitionSpec as P

AXES = ("line", "mid", "grp")
NOTE_ROWS = 8
RADIX = 256
CHUNKS = 8
VMEM = pl.BlockSpec(memory_space=pltpu.VMEM)
HBM = pl.BlockSpec(memory_space=pltpu.HBM)


def embed_kernel(
    states_hbm, proj_hbm, owner_hbm, sub_hbm, prio_hbm, block_ref,
    states, proj, owner, sub, prio, big_sem, small_sem,
):
    rows, depth = states.shape
    width = proj.shape[1]
    span = depth // CHUNKS
    copies = []
    for i in range(CHUNKS):
        part = pl.ds(i * span, span)
        copies.append((
            pltpu.make_async_copy(states_hbm.at[:, part], states.at[:, part], big_sem.at[0, i]),
            pltpu.make_async_copy(proj_hbm.at[part], proj.at[part], big_sem.at[1, i]),
        ))
    small = [
        pltpu.make_async_copy(src, dst, small_sem.at[i])
        for i, (src, dst) in enumerate(((owner_hbm, owner), (sub_hbm, sub), (prio_hbm, prio)))
    ]
    for copy in [c for pair in copies for c in pair] + small:
        copy.start()
    projected = None
    for i, pair in enumerate(copies):
        for copy in pair:
            copy.wait()
        part = slice(i * span, (i + 1) * span)
        term = jnp.dot(states[:, part], proj[part, :], preferred_element_type=jnp.float32)
        projected = term if projected is None else projected + term
    square_sum = jnp.sum(projected * projected, axis=1, keepdims=True)
    embedding = projected * lax.rsqrt(square_sum + 1e-06)
    for copy in small:
        copy.wait()
    rank = prio[...]
    high = lax.shift_right_logical(rank, 8)
    fields = (owner[...] + 1, sub[...], high, rank - high * RADIX)
    notes = [f.astype(jnp.float32) for f in fields]
    notes.append(jnp.zeros((NOTE_ROWS - len(fields), rows), jnp.float32))
    tiles = [embedding[:, i:i + rows] for i in range(0, width, rows)]
    block_ref[...] = jnp.concatenate(tiles + notes, axis=0).astype(jnp.bfloat16)


def embed(states, projection, owner, sub, prio):
    rows, depth = states.shape
    width = projection.shape[1]
    high = rows * (width // rows) + NOTE_ROWS
    return pl.pallas_call(
        embed_kernel,
        in_specs=[HBM] * 5,
        out_specs=VMEM,
        out_shape=jax.ShapeDtypeStruct((high, rows), jnp.bfloat16),
        scratch_shapes=[
            pltpu.VMEM((rows, depth), jnp.bfloat16),
            pltpu.VMEM((depth, width), jnp.bfloat16),
            pltpu.VMEM((1, rows), jnp.int32),
            pltpu.VMEM((1, rows), jnp.int32),
            pltpu.VMEM((1, rows), jnp.int32),
            pltpu.SemaphoreType.DMA((2, CHUNKS)),
            pltpu.SemaphoreType.DMA((3,)),
        ],
        compiler_params=pltpu.CompilerParams(vmem_limit_bytes=60 << 20),
        name="embed",
    )(states, projection, owner, sub, prio)


def read_notes(block):
    ref = block[-1]
    tail = ref[ref.shape[0] - NOTE_ROWS:, :].astype(jnp.float32)
    owner, sub, high, low = (tail[i:i + 1] for i in range(4))
    return (owner - 1.0) * 4.0 + sub, high * float(RADIX) + low


def read_rows(blocks):
    rows = blocks[0][0].shape[1]
    tiles = [
        [ref[i * rows:(i + 1) * rows, :] for ref in block for i in range(ref.shape[0] // rows)]
        for block in blocks
    ]
    return jnp.concatenate([jnp.concatenate(column, axis=0) for column in zip(*tiles)], axis=1)


def score_kernel(row_sizes, lane_sizes, home, products, parts, has_lines, prefix, has_backs, hold, *refs):
    refs = list(refs)
    row_refs = [[refs.pop(0) for _ in range(size)] for size in row_sizes]
    lane_refs = [[refs.pop(0) for _ in range(size)] for size in lane_sizes]
    row_count, lane_count = len(row_refs), len(lane_refs)
    seen_lines = refs.pop(0) if has_lines else None
    seen_backs = refs.pop(0) if has_backs else None
    line_parts, back_parts = parts
    rows = refs[0].shape[1]
    if hold:
        refs[-1][...] = row_refs[0][0][...]
    row_notes = [read_notes(ref) for ref in row_refs]
    lane_notes = [read_notes(ref) for ref in lane_refs]
    fill = jnp.zeros((-2 * row_count % 8, rows), jnp.float32)
    lines = [line for pair in row_notes for line in pair]
    columns = jnp.concatenate(lines + ([fill] if fill.size else []), axis=0).T
    best, back = [None] * lane_count, [None] * row_count

    def top(old, new):
        return new if old is None else jnp.maximum(old, new)

    for row_set, lane_set in products:
        cosine = lax.dot_general(
            read_rows([row_refs[i] for i in row_set]),
            read_rows([lane_refs[j] for j in lane_set]),
            (((1,), (1,)), ((), ())),
            preferred_element_type=jnp.float32,
        )
        for m, i in enumerate(row_set):
            row_cluster, row_prio = columns[:, 2 * i:2 * i + 1], columns[:, 2 * i + 1:2 * i + 2]
            for n, j in enumerate(lane_set):
                lane_cluster, lane_prio = lane_notes[j]
                here = cosine[m * rows:(m + 1) * rows, n * rows:(n + 1) * rows]
                same = jnp.where(row_cluster == lane_cluster, here, -1.0)
                earlier = row_prio < lane_prio
                best[j] = top(best[j], jnp.where(earlier, same, -1.0))
                if j not in home:
                    back[i] = top(back[i], jnp.where(earlier, -1.0, same))
    lane_ids = lax.broadcasted_iota(jnp.int32, (rows, rows), 1)
    table = jnp.full((rows, rows), -1.0, jnp.float32)
    for i, each in enumerate(back):
        if each is not None:
            table = jnp.where(lane_ids == i, jnp.max(each, axis=1, keepdims=True), table)
    table = table.T
    lines = [jnp.max(each, axis=0, keepdims=True) for each in best]
    if prefix:
        lines = [seen_lines[...]] + lines
    elif has_lines:
        for j in range(seen_lines.shape[0]):
            lines[j] = jnp.maximum(lines[j], seen_lines[j:j + 1, :])
    for first, stop in line_parts:
        refs.pop(0)[...] = jnp.concatenate(lines[first:stop], axis=0)
    if has_backs:
        table = jnp.maximum(table[:row_count], seen_backs[...])
    for first, stop in back_parts:
        refs.pop(0)[...] = table[first:stop]


def score(
    name, row_blocks, lane_blocks, home, products, line_parts, back_parts,
    lines=None, prefix=False, backs=None, hold=False,
):
    high, rows = row_blocks[0][0].shape
    width = high - NOTE_ROWS
    inputs = [part for block in (*row_blocks, *lane_blocks) for part in block]
    inputs += [seen for seen in (lines, backs) if seen is not None]
    ahead = lines.shape[0] if prefix else 0
    heights = [stop - first + ahead for first, stop in line_parts]
    heights += [stop - first for first, stop in back_parts]
    outs = [jax.ShapeDtypeStruct((height, rows), jnp.float32) for height in heights]
    if hold:
        outs.append(jax.ShapeDtypeStruct((high, rows), row_blocks[0][0].dtype))
    sizes = tuple(map(len, row_blocks)), tuple(map(len, lane_blocks))
    if prefix:
        line_parts = [(0, 1 + len(lane_blocks))]
    flags = lines is not None, prefix, backs is not None, hold
    macs = sum(len(r) * len(c) for r, c in products) * rows * rows * width
    return pl.pallas_call(
        lambda *refs: score_kernel(*sizes, home, products, (line_parts, back_parts), *flags, *refs),
        in_specs=[VMEM] * len(inputs),
        out_specs=[VMEM] * len(outs),
        out_shape=outs,
        compiler_params=pltpu.CompilerParams(vmem_limit_bytes=48 << 20),
        cost_estimate=pl.CostEstimate(
            flops=2 * macs,
            bytes_accessed=2 * (len(row_blocks) + len(lane_blocks)) * rows * width,
            transcendentals=0,
        ),
        name=name,
    )(*inputs)


def tournament(line):
    moves = [[(i, (i + s) % line) for i in range(line)] for s in range(1, (line + 1) // 2)]
    if line % 2 == 0:
        half = line // 2
        pairs = [(i, i + half) if i % 2 else (i + half, i) for i in range(half)]
        sent, met = {a for a, _ in pairs}, {b for _, b in pairs}
        idle = [i for i in range(line) if i not in sent]
        free = [i for i in range(line) if i not in met]
        moves.append(pairs + list(zip(idle, free)))
    return moves


def on_device(states, projection, owner_group, cluster_sub, priority):
    line, grp = lax.axis_size("line"), lax.axis_size("grp")
    plane = lax.axis_size("mid") * grp
    rows = states.shape[0]

    def move(array, pairs):
        whole = [(a * plane + p, b * plane + p) for a, b in pairs for p in range(plane)]
        return lax.ppermute(array, AXES, whole)

    def swap(array, step):
        pairs = [(i, i // plane * plane + (i % plane ^ step)) for i in range(line * plane)]
        return lax.ppermute(array, AXES, pairs)

    block = embed(
        states,
        projection,
        owner_group.reshape(1, rows),
        cluster_sub.reshape(1, rows),
        priority.reshape(1, rows),
    )
    moves = tournament(line)
    visitors = [move(block, pairs) for pairs in moves]
    bits = [1 << i for i in range(1, plane.bit_length() - 1)]
    found = {0: (block,)}
    for bit in reversed(bits):
        found |= {step | bit: (swap(*here, bit),) for step, here in found.items()}
    row_blocks = [found[step] for step in sorted(found)]

    count, mine = len(row_blocks), 1 + len(visitors)
    half, every = count // 2, tuple(range(count))
    soon = tuple(range(half + 1))
    rest = every[half + 1:]
    lines, held = score(
        "score_own", [row_blocks[i] for i in soon], [(block,)], (0,), [(soon, (0,))],
        [(0, 1)], [], hold=True,
    )
    row_blocks[0] = (held,)
    own = lax.optimization_barrier((block, *row_blocks[1]))[0]
    ready = lax.optimization_barrier((visitors[-1], held))[0]
    partner = [swap(lane, 1) for lane in [own] + visitors[:-1] + [ready]]
    lanes = [(lane,) for lane in [held] + visitors + partner[:-1]]
    numbers = tuple(range(len(lanes)))
    lines, theirs, backs = score(
        "score_most", row_blocks, lanes, (0, mine), [(rest, numbers), (soon, numbers[1:])],
        [(0, mine), (mine, len(lanes))], [(0, count)], lines,
    )
    theirs, near, far = score(
        "score_last", row_blocks, [(partner[-1],)], (), [(every, (0,))],
        [(0, 1)], [(0, half), (half, count)], theirs, True, backs,
    )
    lines = jnp.maximum(lines, swap(theirs, 1))
    for bit in bits[:0:-1]:
        near = jnp.maximum(near, swap(far, bit))
        half = near.shape[0] // 2
        near, far = near[:half], near[half:]
    total = lines[:1]
    for i, pairs in reversed(list(enumerate(moves))):
        total = jnp.maximum(total, move(lines[i + 1:i + 2], [(b, a) for a, b in pairs]))
    total = lax.optimization_barrier(total)
    total = jnp.maximum(jnp.maximum(total, near), swap(far, bits[0]))
    return total.reshape(rows)


def solution(mesh):
    num_dp, num_grp = mesh.shape["dp"], mesh.shape["grp"]
    line = min(num_dp, 1 << (int(math.log2(num_dp * num_grp)) // 2))
    split = Mesh(mesh.devices.reshape(line, num_dp // line, num_grp), AXES)
    in_specs = (P(AXES, None), P(), P(AXES, None), P(AXES), P(AXES))
    return jax.shard_map(
        on_device, mesh=split, in_specs=in_specs, out_specs=P(AXES), check_vma=False
    )
```

```python
import math

import jax
import jax.numpy as jnp
from jax import lax
from jax.experimental import pallas as pl
from jax.experimental.pallas import tpu as pltpu
from jax.sharding import Mesh, PartitionSpec as P

AXES = ("line", "mid", "grp")
NOTE_ROWS = 8
RADIX = 256
CHUNKS = 8
VMEM = pl.BlockSpec(memory_space=pltpu.VMEM)
HBM = pl.BlockSpec(memory_space=pltpu.HBM)


def embed_kernel(
    states_hbm, proj_hbm, owner_hbm, sub_hbm, prio_hbm, block_ref,
    states, proj, owner, sub, prio, big_sem, small_sem,
):
    rows, depth = states.shape
    width = proj.shape[1]
    span = depth // CHUNKS
    copies = []
    for i in range(CHUNKS):
        part = pl.ds(i * span, span)
        copies.append((
            pltpu.make_async_copy(states_hbm.at[:, part], states.at[:, part], big_sem.at[0, i]),
            pltpu.make_async_copy(proj_hbm.at[part], proj.at[part], big_sem.at[1, i]),
        ))
    small = [
        pltpu.make_async_copy(src, dst, small_sem.at[i])
        for i, (src, dst) in enumerate(((owner_hbm, owner), (sub_hbm, sub), (prio_hbm, prio)))
    ]
    for copy in [c for pair in copies for c in pair] + small:
        copy.start()
    projected = None
    for i, pair in enumerate(copies):
        for copy in pair:
            copy.wait()
        part = slice(i * span, (i + 1) * span)
        term = jnp.dot(states[:, part], proj[part, :], preferred_element_type=jnp.float32)
        projected = term if projected is None else projected + term
    square_sum = jnp.sum(projected * projected, axis=1, keepdims=True)
    embedding = projected * lax.rsqrt(square_sum + 1e-06)
    for copy in small:
        copy.wait()
    rank = prio[...]
    high = lax.shift_right_logical(rank, 8)
    fields = (owner[...] + 1, sub[...], high, rank - high * RADIX)
    notes = [f.astype(jnp.float32) for f in fields]
    notes.append(jnp.zeros((NOTE_ROWS - len(fields), rows), jnp.float32))
    tiles = [embedding[:, i:i + rows] for i in range(0, width, rows)]
    block_ref[...] = jnp.concatenate(tiles + notes, axis=0).astype(jnp.bfloat16)


def embed(states, projection, owner, sub, prio):
    rows, depth = states.shape
    width = projection.shape[1]
    high = rows * (width // rows) + NOTE_ROWS
    return pl.pallas_call(
        embed_kernel,
        in_specs=[HBM] * 5,
        out_specs=VMEM,
        out_shape=jax.ShapeDtypeStruct((high, rows), jnp.bfloat16),
        scratch_shapes=[
            pltpu.VMEM((rows, depth), jnp.bfloat16),
            pltpu.VMEM((depth, width), jnp.bfloat16),
            pltpu.VMEM((1, rows), jnp.int32),
            pltpu.VMEM((1, rows), jnp.int32),
            pltpu.VMEM((1, rows), jnp.int32),
            pltpu.SemaphoreType.DMA((2, CHUNKS)),
            pltpu.SemaphoreType.DMA((3,)),
        ],
        compiler_params=pltpu.CompilerParams(vmem_limit_bytes=60 << 20),
        name="embed",
    )(states, projection, owner, sub, prio)


def read_notes(block):
    ref = block[-1]
    tail = ref[ref.shape[0] - NOTE_ROWS:, :].astype(jnp.float32)
    owner, sub, high, low = (tail[i:i + 1] for i in range(4))
    return (owner - 1.0) * 4.0 + sub, high * float(RADIX) + low


def read_rows(blocks):
    rows = blocks[0][0].shape[1]
    tiles = [
        [ref[i * rows:(i + 1) * rows, :] for ref in block for i in range(ref.shape[0] // rows)]
        for block in blocks
    ]
    return jnp.concatenate([jnp.concatenate(column, axis=0) for column in zip(*tiles)], axis=1)


def score_kernel(row_sizes, lane_sizes, home, products, parts, has_lines, prefix, has_backs, hold, *refs):
    refs = list(refs)
    row_refs = [[refs.pop(0) for _ in range(size)] for size in row_sizes]
    lane_refs = [[refs.pop(0) for _ in range(size)] for size in lane_sizes]
    row_count, lane_count = len(row_refs), len(lane_refs)
    seen_lines = refs.pop(0) if has_lines else None
    seen_backs = refs.pop(0) if has_backs else None
    line_parts, back_parts = parts
    rows = refs[0].shape[1]
    if hold:
        refs[-1][...] = row_refs[0][0][...]
    row_notes = [read_notes(ref) for ref in row_refs]
    lane_notes = [read_notes(ref) for ref in lane_refs]
    fill = jnp.zeros((-2 * row_count % 8, rows), jnp.float32)
    lines = [line for pair in row_notes for line in pair]
    columns = jnp.concatenate(lines + ([fill] if fill.size else []), axis=0).T
    best, back = [None] * lane_count, [None] * row_count

    def top(old, new):
        return new if old is None else jnp.maximum(old, new)

    for row_set, lane_set in products:
        cosine = lax.dot_general(
            read_rows([row_refs[i] for i in row_set]),
            read_rows([lane_refs[j] for j in lane_set]),
            (((1,), (1,)), ((), ())),
            preferred_element_type=jnp.float32,
        )
        for m, i in enumerate(row_set):
            row_cluster, row_prio = columns[:, 2 * i:2 * i + 1], columns[:, 2 * i + 1:2 * i + 2]
            for n, j in enumerate(lane_set):
                lane_cluster, lane_prio = lane_notes[j]
                here = cosine[m * rows:(m + 1) * rows, n * rows:(n + 1) * rows]
                same = jnp.where(row_cluster == lane_cluster, here, -1.0)
                earlier = row_prio < lane_prio
                best[j] = top(best[j], jnp.where(earlier, same, -1.0))
                if j not in home:
                    back[i] = top(back[i], jnp.where(earlier, -1.0, same))
    lane_ids = lax.broadcasted_iota(jnp.int32, (rows, rows), 1)
    table = jnp.full((rows, rows), -1.0, jnp.float32)
    for i, each in enumerate(back):
        if each is not None:
            table = jnp.where(lane_ids == i, jnp.max(each, axis=1, keepdims=True), table)
    table = table.T
    lines = [jnp.max(each, axis=0, keepdims=True) for each in best]
    if prefix:
        lines = [seen_lines[...]] + lines
    elif has_lines:
        for j in range(seen_lines.shape[0]):
            lines[j] = jnp.maximum(lines[j], seen_lines[j:j + 1, :])
    for first, stop in line_parts:
        refs.pop(0)[...] = jnp.concatenate(lines[first:stop], axis=0)
    if has_backs:
        table = jnp.maximum(table[:row_count], seen_backs[...])
    for first, stop in back_parts:
        refs.pop(0)[...] = table[first:stop]


def score(
    name, row_blocks, lane_blocks, home, products, line_parts, back_parts,
    lines=None, prefix=False, backs=None, hold=False,
):
    high, rows = row_blocks[0][0].shape
    width = high - NOTE_ROWS
    inputs = [part for block in (*row_blocks, *lane_blocks) for part in block]
    inputs += [seen for seen in (lines, backs) if seen is not None]
    ahead = lines.shape[0] if prefix else 0
    heights = [stop - first + ahead for first, stop in line_parts]
    heights += [stop - first for first, stop in back_parts]
    outs = [jax.ShapeDtypeStruct((height, rows), jnp.float32) for height in heights]
    if hold:
        outs.append(jax.ShapeDtypeStruct((high, rows), row_blocks[0][0].dtype))
    sizes = tuple(map(len, row_blocks)), tuple(map(len, lane_blocks))
    if prefix:
        line_parts = [(0, 1 + len(lane_blocks))]
    flags = lines is not None, prefix, backs is not None, hold
    macs = sum(len(r) * len(c) for r, c in products) * rows * rows * width
    return pl.pallas_call(
        lambda *refs: score_kernel(*sizes, home, products, (line_parts, back_parts), *flags, *refs),
        in_specs=[VMEM] * len(inputs),
        out_specs=[VMEM] * len(outs),
        out_shape=outs,
        compiler_params=pltpu.CompilerParams(vmem_limit_bytes=48 << 20),
        cost_estimate=pl.CostEstimate(
            flops=2 * macs,
            bytes_accessed=2 * (len(row_blocks) + len(lane_blocks)) * rows * width,
            transcendentals=0,
        ),
        name=name,
    )(*inputs)


def tournament(line):
    moves = [[(i, (i - s) % line) for i in range(line)] for s in range(1, (line + 1) // 2)]
    if line % 2 == 0:
        half = line // 2
        pairs = [(i, i + half) if i % 2 else (i + half, i) for i in range(half)]
        sent, met = {a for a, _ in pairs}, {b for _, b in pairs}
        idle = [i for i in range(line) if i not in sent]
        free = [i for i in range(line) if i not in met]
        moves.insert(0, pairs + list(zip(idle, free)))
    return moves


def on_device(states, projection, owner_group, cluster_sub, priority):
    line, grp = lax.axis_size("line"), lax.axis_size("grp")
    plane = lax.axis_size("mid") * grp
    rows = states.shape[0]

    def move(array, pairs):
        whole = [(a * plane + p, b * plane + p) for a, b in pairs for p in range(plane)]
        return lax.ppermute(array, AXES, whole)

    def swap(array, step):
        pairs = [(i, i // plane * plane + (i % plane ^ step)) for i in range(line * plane)]
        return lax.ppermute(array, AXES, pairs)

    block = embed(
        states,
        projection,
        owner_group.reshape(1, rows),
        cluster_sub.reshape(1, rows),
        priority.reshape(1, rows),
    )
    moves = tournament(line)
    visitors = [move(block, pairs) for pairs in moves]
    bits = [1 << i for i in range(1, plane.bit_length() - 1)]
    cut = block.shape[0] // (2 * rows) * rows

    def halves(parts):
        whole = lax.optimization_barrier((parts[0], visitors[0]))[0]
        return parts if len(parts) > 1 else (whole[:cut], whole[cut:])

    found = {0: (block,)}
    for bit in bits:
        found[bit] = (swap(block, bit),)
    for step in range(0, plane, 2):
        if step not in found:
            low, high = step & -step, 1 << (step.bit_length() - 1)
            upper, lower = halves(found[step ^ high])[0], halves(found[step ^ low])[1]
            found[step] = swap(upper, high), swap(lower, low)
    row_blocks = [found[step] for step in sorted(found)]

    count, mine = len(row_blocks), 1 + len(visitors)
    half, every = count // 2, tuple(range(count))
    soon, known = tuple(range(half + 1)), tuple(range(mine - 1))
    rest = every[half + 1:]
    lines, backs, held = score(
        "score_early", [row_blocks[i] for i in soon], [(lane,) for lane in [block] + visitors[:-1]],
        (0,), [(soon, known)], [(0, mine - 1)], [(0, count)], hold=True,
    )
    row_blocks[0] = (held,)
    own = lax.optimization_barrier((block, visitors[0]))[0]
    partner = [swap(lane, 1) for lane in [own] + visitors[:-1]]
    ready = lax.optimization_barrier((visitors[-1], held, *partner, *row_blocks[-1]))[0]
    lanes = [(lane,) for lane in [held] + visitors + partner]
    numbers = tuple(range(len(lanes)))
    lines, theirs, backs = score(
        "score_most", row_blocks, lanes, (0, mine), [(rest, numbers), (soon, numbers[mine - 1:])],
        [(0, mine), (mine, len(lanes))], [(0, count)], lines, False, backs,
    )
    theirs, near, far = score(
        "score_last", row_blocks, [(swap(ready, 1),)], (), [(every, (0,))],
        [(0, 1)], [(0, half), (half, count)], theirs, True, backs,
    )
    lines = jnp.maximum(lines, swap(theirs, 1))
    for bit in bits[:0:-1]:
        near = jnp.maximum(near, swap(far, bit))
        half = near.shape[0] // 2
        near, far = near[:half], near[half:]
    total = lines[:1]
    for i, pairs in reversed(list(enumerate(moves))):
        total = jnp.maximum(total, move(lines[i + 1:i + 2], [(b, a) for a, b in pairs]))
    total = lax.optimization_barrier(total)
    total = jnp.maximum(jnp.maximum(total, near), swap(far, bits[0]))
    return total.reshape(rows)


def solution(mesh):
    num_dp, num_grp = mesh.shape["dp"], mesh.shape["grp"]
    line = min(num_dp, 1 << (int(math.log2(num_dp * num_grp)) // 2))
    split = Mesh(mesh.devices.reshape(line, num_dp // line, num_grp), AXES)
    in_specs = (P(AXES, None), P(), P(AXES, None), P(AXES), P(AXES))
    return jax.shard_map(
        on_device, mesh=split, in_specs=in_specs, out_specs=P(AXES), check_vma=False
    )
```

```python
import math

import jax
import jax.numpy as jnp
from jax import lax
from jax.experimental import pallas as pl
from jax.experimental.pallas import tpu as pltpu
from jax.sharding import Mesh, PartitionSpec as P

AXES = ("line", "mid", "grp")
NOTE_ROWS = 8
RADIX = 256
CHUNKS = 8
VMEM = pl.BlockSpec(memory_space=pltpu.VMEM)
HBM = pl.BlockSpec(memory_space=pltpu.HBM)


def embed_kernel(
    states_hbm, proj_hbm, owner_hbm, sub_hbm, prio_hbm, block_ref,
    states, proj, owner, sub, prio, big_sem, small_sem,
):
    rows, depth = states.shape
    width = proj.shape[1]
    span = depth // CHUNKS
    copies = []
    for i in range(CHUNKS):
        part = pl.ds(i * span, span)
        copies.append((
            pltpu.make_async_copy(states_hbm.at[:, part], states.at[:, part], big_sem.at[0, i]),
            pltpu.make_async_copy(proj_hbm.at[part], proj.at[part], big_sem.at[1, i]),
        ))
    small = [
        pltpu.make_async_copy(src, dst, small_sem.at[i])
        for i, (src, dst) in enumerate(((owner_hbm, owner), (sub_hbm, sub), (prio_hbm, prio)))
    ]
    for copy in [c for pair in copies for c in pair] + small:
        copy.start()
    projected = None
    for i, pair in enumerate(copies):
        for copy in pair:
            copy.wait()
        part = slice(i * span, (i + 1) * span)
        term = jnp.dot(states[:, part], proj[part, :], preferred_element_type=jnp.float32)
        projected = term if projected is None else projected + term
    square_sum = jnp.sum(projected * projected, axis=1, keepdims=True)
    embedding = projected * lax.rsqrt(square_sum + 1e-06)
    for copy in small:
        copy.wait()
    rank = prio[...]
    high = lax.shift_right_logical(rank, 8)
    fields = (owner[...] + 1, sub[...], high, rank - high * RADIX)
    notes = [f.astype(jnp.float32) for f in fields]
    notes.append(jnp.zeros((NOTE_ROWS - len(fields), rows), jnp.float32))
    tiles = [embedding[:, i:i + rows] for i in range(0, width, rows)]
    block_ref[...] = jnp.concatenate(tiles + notes, axis=0).astype(jnp.bfloat16)


def embed(states, projection, owner, sub, prio):
    rows, depth = states.shape
    width = projection.shape[1]
    high = rows * (width // rows) + NOTE_ROWS
    return pl.pallas_call(
        embed_kernel,
        in_specs=[HBM] * 5,
        out_specs=VMEM,
        out_shape=jax.ShapeDtypeStruct((high, rows), jnp.bfloat16),
        scratch_shapes=[
            pltpu.VMEM((rows, depth), jnp.bfloat16),
            pltpu.VMEM((depth, width), jnp.bfloat16),
            pltpu.VMEM((1, rows), jnp.int32),
            pltpu.VMEM((1, rows), jnp.int32),
            pltpu.VMEM((1, rows), jnp.int32),
            pltpu.SemaphoreType.DMA((2, CHUNKS)),
            pltpu.SemaphoreType.DMA((3,)),
        ],
        compiler_params=pltpu.CompilerParams(vmem_limit_bytes=60 << 20),
        name="embed",
    )(states, projection, owner, sub, prio)


def read_notes(ref):
    tail = ref[ref.shape[0] - NOTE_ROWS:, :].astype(jnp.float32)
    owner, sub, high, low = (tail[i:i + 1] for i in range(4))
    return (owner - 1.0) * 4.0 + sub, high * float(RADIX) + low


def read_rows(refs):
    rows = refs[0].shape[1]
    firsts = range(0, refs[0].shape[0] - NOTE_ROWS, rows)
    return jnp.concatenate(
        [jnp.concatenate([ref[first:first + rows, :] for ref in refs], axis=0) for first in firsts],
        axis=1,
    )


def score_kernel(row_count, lane_count, products, parts, has_lines, seen_rows, hold, *refs):
    refs = list(refs)
    row_refs = [refs.pop(0) for _ in range(row_count)]
    lane_refs = [refs.pop(0) for _ in range(lane_count)]
    seen_lines = refs.pop(0) if has_lines else None
    seen_backs = refs.pop(0) if seen_rows else None
    lines_out = refs.pop(0)
    rows = lines_out.shape[1]
    if hold:
        refs[-1][...] = row_refs[0][...]
    row_notes = [read_notes(ref) for ref in row_refs]
    lane_notes = [read_notes(ref) for ref in lane_refs]
    fill = jnp.zeros((-2 * row_count % 8, rows), jnp.float32)
    lines = [line for pair in row_notes for line in pair]
    columns = jnp.concatenate(lines + ([fill] if fill.size else []), axis=0).T
    best, back = [None] * lane_count, [None] * row_count

    def top(old, new):
        return new if old is None else jnp.maximum(old, new)

    for row_set, lane_set in products:
        cosine = lax.dot_general(
            read_rows([row_refs[i] for i in row_set]),
            read_rows([lane_refs[j] for j in lane_set]),
            (((1,), (1,)), ((), ())),
            preferred_element_type=jnp.float32,
        )
        for m, i in enumerate(row_set):
            row_cluster, row_prio = columns[:, 2 * i:2 * i + 1], columns[:, 2 * i + 1:2 * i + 2]
            for n, j in enumerate(lane_set):
                lane_cluster, lane_prio = lane_notes[j]
                here = cosine[m * rows:(m + 1) * rows, n * rows:(n + 1) * rows]
                same = jnp.where(row_cluster == lane_cluster, here, -1.0)
                earlier = row_prio < lane_prio
                best[j] = top(best[j], jnp.where(earlier, same, -1.0))
                if j > 0:
                    back[i] = top(back[i], jnp.where(earlier, -1.0, same))
    lane_ids = lax.broadcasted_iota(jnp.int32, (rows, rows), 1)
    table = jnp.full((rows, rows), -1.0, jnp.float32)
    for i, each in enumerate(back):
        if each is not None:
            table = jnp.where(lane_ids == i, jnp.max(each, axis=1, keepdims=True), table)
    table = table.T
    if seen_rows:
        table = jnp.maximum(table[:row_count], seen_backs[...])
    for first, stop in parts:
        refs.pop(0)[...] = table[first:stop]
    lines = jnp.concatenate([jnp.max(b, axis=0, keepdims=True) for b in best], axis=0)
    if has_lines:
        count = seen_lines.shape[0]
        first = jnp.maximum(lines[:count], seen_lines[...])
        lines = first if count == lane_count else jnp.concatenate([first, lines[count:]], axis=0)
    lines_out[...] = lines


def score(name, row_blocks, lane_blocks, products, parts, lines=None, backs=None, hold=False):
    high, rows = row_blocks[0].shape
    width = high - NOTE_ROWS
    inputs = [*row_blocks, *lane_blocks, *(seen for seen in (lines, backs) if seen is not None)]
    shapes = [(len(lane_blocks), rows)] + [(stop - first, rows) for first, stop in parts]
    outs = [jax.ShapeDtypeStruct(shape, jnp.float32) for shape in shapes]
    if hold:
        outs.append(jax.ShapeDtypeStruct((high, rows), row_blocks[0].dtype))
    counts = len(row_blocks), len(lane_blocks)
    rest = products, parts, lines is not None, backs is not None, hold
    macs = sum(len(r) * len(c) for r, c in products) * rows * rows * width
    return pl.pallas_call(
        lambda *refs: score_kernel(*counts, *rest, *refs),
        in_specs=[VMEM] * len(inputs),
        out_specs=[VMEM] * len(outs),
        out_shape=outs,
        compiler_params=pltpu.CompilerParams(vmem_limit_bytes=48 << 20),
        cost_estimate=pl.CostEstimate(
            flops=2 * macs, bytes_accessed=2 * sum(counts) * rows * width, transcendentals=0
        ),
        name=name,
    )(*inputs)


def tournament(line):
    moves = [[(i, (i + s) % line) for i in range(line)] for s in range(1, (line + 1) // 2)]
    if line % 2 == 0:
        half = line // 2
        pairs = [(i, i + half) if i % 2 else (i + half, i) for i in range(half)]
        sent, met = {a for a, _ in pairs}, {b for _, b in pairs}
        idle = [i for i in range(line) if i not in sent]
        free = [i for i in range(line) if i not in met]
        moves.append(pairs + list(zip(idle, free)))
    return moves


def on_device(states, projection, owner_group, cluster_sub, priority):
    line, grp = lax.axis_size("line"), lax.axis_size("grp")
    plane = lax.axis_size("mid") * grp
    rows = states.shape[0]

    def move(array, pairs):
        whole = [(a * plane + p, b * plane + p) for a, b in pairs for p in range(plane)]
        return lax.ppermute(array, AXES, whole)

    def swap(array, step):
        pairs = [(i, i // plane * plane + (i % plane ^ step)) for i in range(line * plane)]
        return lax.ppermute(array, AXES, pairs)

    block = embed(
        states,
        projection,
        owner_group.reshape(1, rows),
        cluster_sub.reshape(1, rows),
        priority.reshape(1, rows),
    )
    moves = tournament(line)
    visitors = [move(block, pairs) for pairs in moves]
    bits = [1 << i for i in range(1, plane.bit_length() - 1)]
    found = {0: block}
    for bit in reversed(bits):
        found |= {step | bit: swap(here, bit) for step, here in found.items()}
    row_blocks = [found[step] for step in sorted(found)]

    lanes = [block] + visitors
    every, count = tuple(range(len(lanes))), len(row_blocks)
    half = count // 2
    soon = (0, half)
    rest = tuple(i for i in range(count) if i not in soon)
    lines, held = score(
        "score_soon", [row_blocks[i] for i in soon], lanes[:1], [((0, 1), (0,))], [], hold=True
    )
    row_blocks[0] = lanes[0] = held
    products = [(rest, every), (soon, every[1:])]
    lines, backs = score("score_late", row_blocks, lanes, products, [(0, count)], lines)
    partner = [lax.optimization_barrier((held, visitors[0]))[0]]
    partner += [lax.optimization_barrier((visitor, row_blocks[1]))[0] for visitor in visitors]
    partner = [swap(lane, 1) for lane in partner]
    products, parts = [(tuple(range(count)), every)], [(0, half), (half, count)]
    theirs, near, far = score("score_partner", row_blocks, partner, products, parts, None, backs)
    lines = jnp.maximum(lines, swap(theirs, 1))
    for bit in bits[:0:-1]:
        near = jnp.maximum(near, swap(far, bit))
        half = near.shape[0] // 2
        near, far = near[:half], near[half:]
    total = lines[:1]
    for i, pairs in reversed(list(enumerate(moves))):
        total = jnp.maximum(total, move(lines[i + 1:i + 2], [(b, a) for a, b in pairs]))
    total = lax.optimization_barrier(total)
    total = jnp.maximum(jnp.maximum(total, near), swap(far, bits[0]))
    return total.reshape(rows)


def solution(mesh):
    num_dp, num_grp = mesh.shape["dp"], mesh.shape["grp"]
    line = min(num_dp, 1 << (int(math.log2(num_dp * num_grp)) // 2))
    split = Mesh(mesh.devices.reshape(line, num_dp // line, num_grp), AXES)
    in_specs = (P(AXES, None), P(), P(AXES, None), P(AXES), P(AXES))
    return jax.shard_map(
        on_device, mesh=split, in_specs=in_specs, out_specs=P(AXES), check_vma=False
    )
```

```python
import math

import jax
import jax.numpy as jnp
from jax import lax
from jax.experimental import pallas as pl
from jax.experimental.pallas import tpu as pltpu
from jax.sharding import Mesh, PartitionSpec as P

AXES = ("line", "mid", "grp")
NOTE_ROWS = 8
RADIX = 256
CHUNKS = 8
VMEM = pl.BlockSpec(memory_space=pltpu.VMEM)
HBM = pl.BlockSpec(memory_space=pltpu.HBM)


def embed_kernel(
    states_hbm, proj_hbm, owner_hbm, sub_hbm, prio_hbm, block_ref,
    states, proj, owner, sub, prio, big_sem, small_sem,
):
    rows, depth = states.shape
    width = proj.shape[1]
    span = depth // CHUNKS
    copies = []
    for i in range(CHUNKS):
        part = pl.ds(i * span, span)
        copies.append((
            pltpu.make_async_copy(states_hbm.at[:, part], states.at[:, part], big_sem.at[0, i]),
            pltpu.make_async_copy(proj_hbm.at[part], proj.at[part], big_sem.at[1, i]),
        ))
    small = [
        pltpu.make_async_copy(src, dst, small_sem.at[i])
        for i, (src, dst) in enumerate(((owner_hbm, owner), (sub_hbm, sub), (prio_hbm, prio)))
    ]
    for copy in [c for pair in copies for c in pair] + small:
        copy.start()
    projected = None
    for i, pair in enumerate(copies):
        for copy in pair:
            copy.wait()
        part = slice(i * span, (i + 1) * span)
        term = jnp.dot(states[:, part], proj[part, :], preferred_element_type=jnp.float32)
        projected = term if projected is None else projected + term
    square_sum = jnp.sum(projected * projected, axis=1, keepdims=True)
    embedding = projected * lax.rsqrt(square_sum + 1e-06)
    for copy in small:
        copy.wait()
    rank = prio[...]
    high = lax.shift_right_logical(rank, 8)
    fields = (owner[...] + 1, sub[...], high, rank - high * RADIX)
    notes = [f.astype(jnp.float32) for f in fields]
    notes.append(jnp.zeros((NOTE_ROWS - len(fields), rows), jnp.float32))
    tiles = [embedding[:, i:i + rows] for i in range(0, width, rows)]
    block_ref[...] = jnp.concatenate(tiles + notes, axis=0).astype(jnp.bfloat16)


def embed(states, projection, owner, sub, prio):
    rows, depth = states.shape
    width = projection.shape[1]
    high = rows * (width // rows) + NOTE_ROWS
    return pl.pallas_call(
        embed_kernel,
        in_specs=[HBM] * 5,
        out_specs=VMEM,
        out_shape=jax.ShapeDtypeStruct((high, rows), jnp.bfloat16),
        scratch_shapes=[
            pltpu.VMEM((rows, depth), jnp.bfloat16),
            pltpu.VMEM((depth, width), jnp.bfloat16),
            pltpu.VMEM((1, rows), jnp.int32),
            pltpu.VMEM((1, rows), jnp.int32),
            pltpu.VMEM((1, rows), jnp.int32),
            pltpu.SemaphoreType.DMA((2, CHUNKS)),
            pltpu.SemaphoreType.DMA((3,)),
        ],
        compiler_params=pltpu.CompilerParams(vmem_limit_bytes=40 << 20),
        name="embed",
    )(*(pltpu.with_memory_space_constraint(x, pltpu.HBM) for x in (states, projection, owner, sub, prio)))


def read_notes(ref):
    tail = ref[ref.shape[0] - NOTE_ROWS:, :].astype(jnp.float32)
    owner, sub, high, low = (tail[i:i + 1] for i in range(4))
    return (owner - 1.0) * 4.0 + sub, high * float(RADIX) + low


def read_rows(refs):
    rows = refs[0].shape[1]
    firsts = range(0, refs[0].shape[0] - NOTE_ROWS, rows)
    return jnp.concatenate(
        [jnp.concatenate([ref[first:first + rows, :] for ref in refs], axis=0) for first in firsts],
        axis=1,
    )


def score_kernel(row_count, lane_count, products, parts, has_lines, seen_rows, hold, *refs):
    refs = list(refs)
    row_refs = [refs.pop(0) for _ in range(row_count)]
    lane_refs = [refs.pop(0) for _ in range(lane_count)]
    seen_lines = refs.pop(0) if has_lines else None
    seen_backs = refs.pop(0) if seen_rows else None
    lines_out = refs.pop(0)
    rows = lines_out.shape[1]
    if hold:
        refs[-1][...] = row_refs[0][...]
    row_notes = [read_notes(ref) for ref in row_refs]
    lane_notes = [read_notes(ref) for ref in lane_refs]
    fill = jnp.zeros((-2 * row_count % 8, rows), jnp.float32)
    lines = [line for pair in row_notes for line in pair]
    columns = jnp.concatenate(lines + ([fill] if fill.size else []), axis=0).T
    best, back = [None] * lane_count, [None] * row_count

    def top(old, new):
        return new if old is None else jnp.maximum(old, new)

    for row_set, lane_set in products:
        cosine = lax.dot_general(
            read_rows([row_refs[i] for i in row_set]),
            read_rows([lane_refs[j] for j in lane_set]),
            (((1,), (1,)), ((), ())),
            preferred_element_type=jnp.float32,
        )
        for m, i in enumerate(row_set):
            row_cluster, row_prio = columns[:, 2 * i:2 * i + 1], columns[:, 2 * i + 1:2 * i + 2]
            for n, j in enumerate(lane_set):
                lane_cluster, lane_prio = lane_notes[j]
                here = cosine[m * rows:(m + 1) * rows, n * rows:(n + 1) * rows]
                same = jnp.where(row_cluster == lane_cluster, here, -1.0)
                earlier = row_prio < lane_prio
                best[j] = top(best[j], jnp.where(earlier, same, -1.0))
                if j > 0:
                    back[i] = top(back[i], jnp.where(earlier, -1.0, same))
    lane_ids = lax.broadcasted_iota(jnp.int32, (rows, rows), 1)
    table = jnp.full((rows, rows), -1.0, jnp.float32)
    for i, each in enumerate(back):
        if each is not None:
            table = jnp.where(lane_ids == i, jnp.max(each, axis=1, keepdims=True), table)
    table = table.T
    if seen_rows:
        table = jnp.maximum(table[:row_count], seen_backs[...])
    for first, stop in parts:
        refs.pop(0)[...] = table[first:stop]
    lines = jnp.concatenate([jnp.max(b, axis=0, keepdims=True) for b in best], axis=0)
    if has_lines:
        count = seen_lines.shape[0]
        first = jnp.maximum(lines[:count], seen_lines[...])
        lines = first if count == lane_count else jnp.concatenate([first, lines[count:]], axis=0)
    lines_out[...] = lines


def score(name, row_blocks, lane_blocks, products, parts, lines=None, backs=None, hold=False):
    high, rows = row_blocks[0].shape
    width = high - NOTE_ROWS
    inputs = [*row_blocks, *lane_blocks, *(seen for seen in (lines, backs) if seen is not None)]
    shapes = [(len(lane_blocks), rows)] + [(stop - first, rows) for first, stop in parts]
    outs = [jax.ShapeDtypeStruct(shape, jnp.float32) for shape in shapes]
    if hold:
        outs.append(jax.ShapeDtypeStruct((high, rows), row_blocks[0].dtype))
    counts = len(row_blocks), len(lane_blocks)
    rest = products, parts, lines is not None, backs is not None, hold
    macs = sum(len(r) * len(c) for r, c in products) * rows * rows * width
    return pl.pallas_call(
        lambda *refs: score_kernel(*counts, *rest, *refs),
        in_specs=[VMEM] * len(inputs),
        out_specs=[VMEM] * len(outs),
        out_shape=outs,
        compiler_params=pltpu.CompilerParams(vmem_limit_bytes=48 << 20),
        cost_estimate=pl.CostEstimate(
            flops=2 * macs, bytes_accessed=2 * sum(counts) * rows * width, transcendentals=0
        ),
        name=name,
    )(*inputs)


def tournament(line):
    moves = [[(i, (i + s) % line) for i in range(line)] for s in range(1, (line + 1) // 2)]
    if line % 2 == 0:
        half = line // 2
        pairs = [(i, i + half) if i % 2 else (i + half, i) for i in range(half)]
        sent, met = {a for a, _ in pairs}, {b for _, b in pairs}
        idle = [i for i in range(line) if i not in sent]
        free = [i for i in range(line) if i not in met]
        moves.append(pairs + list(zip(idle, free)))
    return moves


def on_device(states, projection, owner_group, cluster_sub, priority):
    line, grp = lax.axis_size("line"), lax.axis_size("grp")
    plane = lax.axis_size("mid") * grp
    rows = states.shape[0]

    def move(array, pairs):
        whole = [(a * plane + p, b * plane + p) for a, b in pairs for p in range(plane)]
        return lax.ppermute(array, AXES, whole)

    def swap(array, step):
        pairs = [(i, i // plane * plane + (i % plane ^ step)) for i in range(line * plane)]
        return lax.ppermute(array, AXES, pairs)

    block = embed(
        states,
        projection,
        owner_group.reshape(1, rows),
        cluster_sub.reshape(1, rows),
        priority.reshape(1, rows),
    )
    moves = tournament(line)
    visitors = [move(block, pairs) for pairs in moves]
    bits = [1 << i for i in range(1, plane.bit_length() - 1)]
    found = {0: block}
    for bit in reversed(bits):
        found |= {step | bit: swap(here, bit) for step, here in found.items()}
    row_blocks = [found[step] for step in sorted(found)]

    lanes = [block] + visitors
    every, count = tuple(range(len(lanes))), len(row_blocks)
    half = count // 2
    soon = (0, half)
    rest = tuple(i for i in range(count) if i not in soon)
    lines, held = score(
        "score_soon", [row_blocks[i] for i in soon], lanes[:1], [((0, 1), (0,))], [], hold=True
    )
    row_blocks[0] = lanes[0] = held
    products = [(rest, every), (soon, every[1:])]
    lines, backs = score("score_late", row_blocks, lanes, products, [(0, count)], lines)
    partner = [lax.optimization_barrier((held, visitors[0]))[0]]
    partner += [lax.optimization_barrier((visitor, row_blocks[1]))[0] for visitor in visitors]
    partner = [swap(lane, 1) for lane in partner]
    products, parts = [(tuple(range(count)), every)], [(0, half), (half, count)]
    theirs, near, far = score("score_partner", row_blocks, partner, products, parts, None, backs)
    lines = jnp.maximum(lines, swap(theirs, 1))
    for bit in bits[:0:-1]:
        near = jnp.maximum(near, swap(far, bit))
        half = near.shape[0] // 2
        near, far = near[:half], near[half:]
    total = lines[:1]
    for i, pairs in reversed(list(enumerate(moves))):
        total = jnp.maximum(total, move(lines[i + 1:i + 2], [(b, a) for a, b in pairs]))
    total = lax.optimization_barrier(total)
    total = jnp.maximum(jnp.maximum(total, near), swap(far, bits[0]))
    return total.reshape(rows)


def solution(mesh):
    num_dp, num_grp = mesh.shape["dp"], mesh.shape["grp"]
    line = min(num_dp, 1 << (int(math.log2(num_dp * num_grp)) // 2))
    split = Mesh(mesh.devices.reshape(line, num_dp // line, num_grp), AXES)
    in_specs = (P(AXES, None), P(), P(AXES, None), P(AXES), P(AXES))
    return jax.shard_map(
        on_device, mesh=split, in_specs=in_specs, out_specs=P(AXES), check_vma=False
    )
```

```python
import math

import jax
import jax.numpy as jnp
from jax import lax
from jax.experimental import pallas as pl
from jax.experimental.pallas import tpu as pltpu
from jax.sharding import Mesh, PartitionSpec as P

AXES = ("line", "mid", "grp")
NOTE_ROWS = 8
RADIX = 256
CHUNKS = 8
VMEM = pl.BlockSpec(memory_space=pltpu.VMEM)
HBM = pl.BlockSpec(memory_space=pltpu.HBM)


def embed_kernel(
    states_hbm, proj_hbm, owner_hbm, sub_hbm, prio_hbm, block_ref,
    states, proj, owner, sub, prio, big_sem, small_sem,
):
    rows, depth = states.shape
    width = proj.shape[1]
    span = depth // CHUNKS
    copies = []
    for i in range(CHUNKS):
        part = pl.ds(i * span, span)
        copies.append((
            pltpu.make_async_copy(states_hbm.at[:, part], states.at[:, part], big_sem.at[0, i]),
            pltpu.make_async_copy(proj_hbm.at[part], proj.at[part], big_sem.at[1, i]),
        ))
    small = [
        pltpu.make_async_copy(src, dst, small_sem.at[i])
        for i, (src, dst) in enumerate(((owner_hbm, owner), (sub_hbm, sub), (prio_hbm, prio)))
    ]
    for copy in [c for pair in copies for c in pair] + small:
        copy.start()
    projected = None
    for i, pair in enumerate(copies):
        for copy in pair:
            copy.wait()
        part = slice(i * span, (i + 1) * span)
        term = jnp.dot(states[:, part], proj[part, :], preferred_element_type=jnp.float32)
        projected = term if projected is None else projected + term
    square_sum = jnp.sum(projected * projected, axis=1, keepdims=True)
    embedding = projected * lax.rsqrt(square_sum + 1e-06)
    for copy in small:
        copy.wait()
    rank = prio[...]
    high = lax.shift_right_logical(rank, 8)
    fields = (owner[...] + 1, sub[...], high, rank - high * RADIX)
    notes = [f.astype(jnp.float32) for f in fields]
    notes.append(jnp.zeros((NOTE_ROWS - len(fields), rows), jnp.float32))
    tiles = [embedding[:, i:i + rows] for i in range(0, width, rows)]
    block_ref[...] = jnp.concatenate(tiles + notes, axis=0).astype(jnp.bfloat16)


def embed(states, projection, owner, sub, prio):
    rows, depth = states.shape
    width = projection.shape[1]
    high = rows * (width // rows) + NOTE_ROWS
    return pl.pallas_call(
        embed_kernel,
        in_specs=[HBM] * 5,
        out_specs=VMEM,
        out_shape=jax.ShapeDtypeStruct((high, rows), jnp.bfloat16),
        scratch_shapes=[
            pltpu.VMEM((rows, depth), jnp.bfloat16),
            pltpu.VMEM((depth, width), jnp.bfloat16),
            pltpu.VMEM((1, rows), jnp.int32),
            pltpu.VMEM((1, rows), jnp.int32),
            pltpu.VMEM((1, rows), jnp.int32),
            pltpu.SemaphoreType.DMA((2, CHUNKS)),
            pltpu.SemaphoreType.DMA((3,)),
        ],
        compiler_params=pltpu.CompilerParams(vmem_limit_bytes=40 << 20),
        name="embed",
    )(*(pltpu.with_memory_space_constraint(x, pltpu.HBM) for x in (states, projection, owner, sub, prio)))


def read_notes(ref):
    tail = ref[ref.shape[0] - NOTE_ROWS:, :].astype(jnp.float32)
    owner, sub, high, low = (tail[i:i + 1] for i in range(4))
    return (owner - 1.0) * 4.0 + sub, high * float(RADIX) + low


def read_rows(refs):
    rows = refs[0].shape[1]
    firsts = range(0, refs[0].shape[0] - NOTE_ROWS, rows)
    return jnp.concatenate(
        [jnp.concatenate([ref[first:first + rows, :] for ref in refs], axis=0) for first in firsts],
        axis=1,
    )


def score_kernel(row_count, lane_count, products, parts, has_lines, seen_rows, hold, home, *refs):
    refs = list(refs)
    row_refs = [refs.pop(0) for _ in range(row_count)]
    lane_refs = [refs.pop(0) for _ in range(lane_count)]
    seen_lines = refs.pop(0) if has_lines else None
    seen_backs = refs.pop(0) if seen_rows else None
    lines_out = refs.pop(0)
    rows = lines_out.shape[1]
    if hold:
        refs[-1][...] = row_refs[0][...]
    row_notes = [read_notes(ref) for ref in row_refs]
    lane_notes = [read_notes(ref) for ref in lane_refs]
    fill = jnp.zeros((-2 * row_count % 8, rows), jnp.float32)
    lines = [line for pair in row_notes for line in pair]
    columns = jnp.concatenate(lines + ([fill] if fill.size else []), axis=0).T
    best, back = [None] * lane_count, [None] * row_count

    def top(old, new):
        return new if old is None else jnp.maximum(old, new)

    for row_set, lane_set in products:
        cosine = lax.dot_general(
            read_rows([row_refs[i] for i in row_set]),
            read_rows([lane_refs[j] for j in lane_set]),
            (((1,), (1,)), ((), ())),
            preferred_element_type=jnp.float32,
        )
        for m, i in enumerate(row_set):
            row_cluster, row_prio = columns[:, 2 * i:2 * i + 1], columns[:, 2 * i + 1:2 * i + 2]
            for n, j in enumerate(lane_set):
                lane_cluster, lane_prio = lane_notes[j]
                here = cosine[m * rows:(m + 1) * rows, n * rows:(n + 1) * rows]
                same = jnp.where(row_cluster == lane_cluster, here, -1.0)
                earlier = row_prio < lane_prio
                best[j] = top(best[j], jnp.where(earlier, same, -1.0))
                if j >= home:
                    back[i] = top(back[i], jnp.where(earlier, -1.0, same))
    lane_ids = lax.broadcasted_iota(jnp.int32, (rows, rows), 1)
    table = jnp.full((rows, rows), -1.0, jnp.float32)
    for i, each in enumerate(back):
        if each is not None:
            table = jnp.where(lane_ids == i, jnp.max(each, axis=1, keepdims=True), table)
    table = table.T
    if seen_rows:
        table = jnp.maximum(table[:row_count], seen_backs[...])
    for first, stop in parts:
        refs.pop(0)[...] = table[first:stop]
    lines = jnp.concatenate([jnp.max(b, axis=0, keepdims=True) for b in best], axis=0)
    if has_lines:
        count = seen_lines.shape[0]
        first = jnp.maximum(lines[:count], seen_lines[...])
        lines = first if count == lane_count else jnp.concatenate([first, lines[count:]], axis=0)
    lines_out[...] = lines


def score(name, row_blocks, lane_blocks, products, parts, lines=None, backs=None, hold=False, home=1):
    high, rows = row_blocks[0].shape
    width = high - NOTE_ROWS
    inputs = [*row_blocks, *lane_blocks, *(seen for seen in (lines, backs) if seen is not None)]
    shapes = [(len(lane_blocks), rows)] + [(stop - first, rows) for first, stop in parts]
    outs = [jax.ShapeDtypeStruct(shape, jnp.float32) for shape in shapes]
    if hold:
        outs.append(jax.ShapeDtypeStruct((high, rows), row_blocks[0].dtype))
    counts = len(row_blocks), len(lane_blocks)
    rest = products, parts, lines is not None, backs is not None, hold, home
    macs = sum(len(r) * len(c) for r, c in products) * rows * rows * width
    return pl.pallas_call(
        lambda *refs: score_kernel(*counts, *rest, *refs),
        in_specs=[VMEM] * len(inputs),
        out_specs=[VMEM] * len(outs),
        out_shape=outs,
        compiler_params=pltpu.CompilerParams(vmem_limit_bytes=48 << 20),
        cost_estimate=pl.CostEstimate(
            flops=2 * macs, bytes_accessed=2 * sum(counts) * rows * width, transcendentals=0
        ),
        name=name,
    )(*inputs)


def tournament(line):
    moves = [[(i, (i + s) % line) for i in range(line)] for s in range(1, (line + 1) // 2)]
    if line % 2 == 0:
        half = line // 2
        pairs = [(i, i + half) if i % 2 else (i + half, i) for i in range(half)]
        sent, met = {a for a, _ in pairs}, {b for _, b in pairs}
        idle = [i for i in range(line) if i not in sent]
        free = [i for i in range(line) if i not in met]
        moves.append(pairs + list(zip(idle, free)))
    return moves


def on_device(states, projection, owner_group, cluster_sub, priority):
    line, grp = lax.axis_size("line"), lax.axis_size("grp")
    plane = lax.axis_size("mid") * grp
    rows = states.shape[0]

    def move(array, pairs):
        whole = [(a * plane + p, b * plane + p) for a, b in pairs for p in range(plane)]
        return lax.ppermute(array, AXES, whole)

    def swap(array, step):
        pairs = [(i, i // plane * plane + (i % plane ^ step)) for i in range(line * plane)]
        return lax.ppermute(array, AXES, pairs)

    block = embed(
        states,
        projection,
        owner_group.reshape(1, rows),
        cluster_sub.reshape(1, rows),
        priority.reshape(1, rows),
    )
    moves = tournament(line)
    visitors = [move(block, pairs) for pairs in moves]
    bits = [1 << i for i in range(1, plane.bit_length() - 1)]
    found = {0: block}
    for bit in reversed(bits):
        found |= {step | bit: swap(here, bit) for step, here in found.items()}
    row_blocks = [found[step] for step in sorted(found)]

    lanes = [block] + visitors
    every, count = tuple(range(len(lanes))), len(row_blocks)
    half = count // 2
    soon = (0, half)
    rest = tuple(i for i in range(count) if i not in soon)
    lines, held = score(
        "score_soon", [row_blocks[i] for i in soon], lanes[:1], [((0, 1), (0,))], [], hold=True
    )
    row_blocks[0] = lanes[0] = held
    products = [(rest, every), (soon, every[1:])]
    lines, backs = score("score_late", row_blocks, lanes, products, [(0, count)], lines)
    partner = [held]
    partner += [visitor for visitor in visitors[:-1]]
    partner += [lax.optimization_barrier((visitors[-1], row_blocks[1]))[0]]
    partner = [swap(lane, 1) for lane in partner]
    theirs, backs = score(
        "score_partner", row_blocks, partner[:-1], [(tuple(range(count)), every[:-1])], [(0, count)], None, backs
    )
    parts = [(0, half), (half, count)]
    last, near, far = score(
        "score_last", row_blocks, partner[-1:], [(tuple(range(count)), (0,))], parts, None, backs, home=0
    )
    first = jnp.maximum(lines[:-1], swap(theirs, 1))
    last = lax.optimization_barrier((swap(last, 1), first))[0]
    lines = [first[i:i + 1] for i in every[:-1]] + [jnp.maximum(lines[-1:], last)]
    for bit in bits[:0:-1]:
        near = jnp.maximum(near, swap(far, bit))
        half = near.shape[0] // 2
        near, far = near[:half], near[half:]
    total = lines[0]
    for i, pairs in enumerate(moves):
        home = move(lines[i + 1], [(b, a) for a, b in pairs])
        total = lax.optimization_barrier(jnp.maximum(total, home))
    total = jnp.maximum(jnp.maximum(total, near), swap(far, bits[0]))
    return total.reshape(rows)


def solution(mesh):
    num_dp, num_grp = mesh.shape["dp"], mesh.shape["grp"]
    line = min(num_dp, 1 << (int(math.log2(num_dp * num_grp)) // 2))
    split = Mesh(mesh.devices.reshape(line, num_dp // line, num_grp), AXES)
    in_specs = (P(AXES, None), P(), P(AXES, None), P(AXES), P(AXES))
    return jax.shard_map(
        on_device, mesh=split, in_specs=in_specs, out_specs=P(AXES), check_vma=False
    )
```

```python
import math

import jax
import jax.numpy as jnp
from jax import lax
from jax.experimental import pallas as pl
from jax.experimental.pallas import tpu as pltpu
from jax.sharding import Mesh, PartitionSpec as P

AXES = ("line", "mid", "grp")
NOTE_ROWS = 8
RADIX = 256
CHUNKS = 4
VMEM = pl.BlockSpec(memory_space=pltpu.VMEM)
HBM = pl.BlockSpec(memory_space=pltpu.HBM)


def embed_kernel(
    states_hbm, proj_hbm, owner_hbm, sub_hbm, prio_hbm, block_ref,
    states, proj, owner, sub, prio, big_sem, small_sem,
):
    rows, depth = states.shape
    width = proj.shape[1]
    span = depth // CHUNKS
    whole = pltpu.make_async_copy(states_hbm, states, big_sem.at[CHUNKS])
    copies = [
        pltpu.make_async_copy(
            proj_hbm.at[pl.ds(i * span, span)], proj.at[pl.ds(i * span, span)], big_sem.at[i]
        )
        for i in range(CHUNKS)
    ]
    small = [
        pltpu.make_async_copy(src, dst, small_sem.at[i])
        for i, (src, dst) in enumerate(((owner_hbm, owner), (sub_hbm, sub), (prio_hbm, prio)))
    ]
    for copy in [whole] + copies + small:
        copy.start()
    whole.wait()
    projected = None
    for i, copy in enumerate(copies):
        copy.wait()
        part = slice(i * span, (i + 1) * span)
        term = jnp.dot(states[:, part], proj[part, :], preferred_element_type=jnp.float32)
        projected = term if projected is None else projected + term
    square_sum = jnp.sum(projected * projected, axis=1, keepdims=True)
    embedding = projected * lax.rsqrt(square_sum + 1e-06)
    for copy in small:
        copy.wait()
    rank = prio[...]
    high = lax.shift_right_logical(rank, 8)
    fields = (owner[...] + 1, sub[...], high, rank - high * RADIX)
    notes = [f.astype(jnp.float32) for f in fields]
    notes.append(jnp.zeros((NOTE_ROWS - len(fields), rows), jnp.float32))
    tiles = [embedding[:, i:i + rows] for i in range(0, width, rows)]
    block_ref[...] = jnp.concatenate(tiles + notes, axis=0).astype(jnp.bfloat16)


def embed(states, projection, owner, sub, prio):
    rows, depth = states.shape
    width = projection.shape[1]
    high = rows * (width // rows) + NOTE_ROWS
    return pl.pallas_call(
        embed_kernel,
        in_specs=[HBM] * 5,
        out_specs=VMEM,
        out_shape=jax.ShapeDtypeStruct((high, rows), jnp.bfloat16),
        scratch_shapes=[
            pltpu.VMEM((rows, depth), jnp.bfloat16),
            pltpu.VMEM((depth, width), jnp.bfloat16),
            pltpu.VMEM((1, rows), jnp.int32),
            pltpu.VMEM((1, rows), jnp.int32),
            pltpu.VMEM((1, rows), jnp.int32),
            pltpu.SemaphoreType.DMA((CHUNKS + 1,)),
            pltpu.SemaphoreType.DMA((3,)),
        ],
        compiler_params=pltpu.CompilerParams(vmem_limit_bytes=40 << 20),
        name="embed",
    )(*(pltpu.with_memory_space_constraint(x, pltpu.HBM) for x in (states, projection, owner, sub, prio)))


def read_notes(ref):
    tail = ref[ref.shape[0] - NOTE_ROWS:, :].astype(jnp.float32)
    owner, sub, high, low = (tail[i:i + 1] for i in range(4))
    return (owner - 1.0) * 4.0 + sub, high * float(RADIX) + low


def read_rows(refs):
    rows = refs[0].shape[1]
    firsts = range(0, refs[0].shape[0] - NOTE_ROWS, rows)
    return jnp.concatenate(
        [jnp.concatenate([ref[first:first + rows, :] for ref in refs], axis=0) for first in firsts],
        axis=1,
    )


def score_kernel(row_count, lane_count, products, parts, has_lines, seen_rows, hold, *refs):
    refs = list(refs)
    row_refs = [refs.pop(0) for _ in range(row_count)]
    lane_refs = [refs.pop(0) for _ in range(lane_count)]
    seen_lines = refs.pop(0) if has_lines else None
    seen_backs = refs.pop(0) if seen_rows else None
    lines_out = refs.pop(0)
    rows = lines_out.shape[1]
    if hold:
        refs[-1][...] = row_refs[0][...]
    row_notes = [read_notes(ref) for ref in row_refs]
    lane_notes = [read_notes(ref) for ref in lane_refs]
    fill = jnp.zeros((-2 * row_count % 8, rows), jnp.float32)
    lines = [line for pair in row_notes for line in pair]
    columns = jnp.concatenate(lines + ([fill] if fill.size else []), axis=0).T
    best, back = [None] * lane_count, [None] * row_count

    def top(old, new):
        return new if old is None else jnp.maximum(old, new)

    for row_set, lane_set in products:
        cosine = lax.dot_general(
            read_rows([row_refs[i] for i in row_set]),
            read_rows([lane_refs[j] for j in lane_set]),
            (((1,), (1,)), ((), ())),
            preferred_element_type=jnp.float32,
        )
        for m, i in enumerate(row_set):
            row_cluster, row_prio = columns[:, 2 * i:2 * i + 1], columns[:, 2 * i + 1:2 * i + 2]
            for n, j in enumerate(lane_set):
                lane_cluster, lane_prio = lane_notes[j]
                here = cosine[m * rows:(m + 1) * rows, n * rows:(n + 1) * rows]
                same = jnp.where(row_cluster == lane_cluster, here, -1.0)
                earlier = row_prio < lane_prio
                best[j] = top(best[j], jnp.where(earlier, same, -1.0))
                if j > 0:
                    back[i] = top(back[i], jnp.where(earlier, -1.0, same))
    lane_ids = lax.broadcasted_iota(jnp.int32, (rows, rows), 1)
    table = jnp.full((rows, rows), -1.0, jnp.float32)
    for i, each in enumerate(back):
        if each is not None:
            table = jnp.where(lane_ids == i, jnp.max(each, axis=1, keepdims=True), table)
    table = table.T
    if seen_rows:
        table = jnp.maximum(table[:row_count], seen_backs[...])
    for first, stop in parts:
        refs.pop(0)[...] = table[first:stop]
    lines = jnp.concatenate([jnp.max(b, axis=0, keepdims=True) for b in best], axis=0)
    if has_lines:
        count = seen_lines.shape[0]
        first = jnp.maximum(lines[:count], seen_lines[...])
        lines = first if count == lane_count else jnp.concatenate([first, lines[count:]], axis=0)
    lines_out[...] = lines


def score(name, row_blocks, lane_blocks, products, parts, lines=None, backs=None, hold=False):
    high, rows = row_blocks[0].shape
    width = high - NOTE_ROWS
    inputs = [*row_blocks, *lane_blocks, *(seen for seen in (lines, backs) if seen is not None)]
    shapes = [(len(lane_blocks), rows)] + [(stop - first, rows) for first, stop in parts]
    outs = [jax.ShapeDtypeStruct(shape, jnp.float32) for shape in shapes]
    if hold:
        outs.append(jax.ShapeDtypeStruct((high, rows), row_blocks[0].dtype))
    counts = len(row_blocks), len(lane_blocks)
    rest = products, parts, lines is not None, backs is not None, hold
    macs = sum(len(r) * len(c) for r, c in products) * rows * rows * width
    return pl.pallas_call(
        lambda *refs: score_kernel(*counts, *rest, *refs),
        in_specs=[VMEM] * len(inputs),
        out_specs=[VMEM] * len(outs),
        out_shape=outs,
        compiler_params=pltpu.CompilerParams(vmem_limit_bytes=48 << 20),
        cost_estimate=pl.CostEstimate(
            flops=2 * macs, bytes_accessed=2 * sum(counts) * rows * width, transcendentals=0
        ),
        name=name,
    )(*inputs)


def tournament(line):
    moves = [[(i, (i + s) % line) for i in range(line)] for s in range(1, (line + 1) // 2)]
    if line % 2 == 0:
        half = line // 2
        pairs = [(i, i + half) if i % 2 else (i + half, i) for i in range(half)]
        sent, met = {a for a, _ in pairs}, {b for _, b in pairs}
        idle = [i for i in range(line) if i not in sent]
        free = [i for i in range(line) if i not in met]
        moves.append(pairs + list(zip(idle, free)))
    return moves


def on_device(states, projection, owner_group, cluster_sub, priority):
    line, grp = lax.axis_size("line"), lax.axis_size("grp")
    plane = lax.axis_size("mid") * grp
    rows = states.shape[0]

    def move(array, pairs):
        whole = [(a * plane + p, b * plane + p) for a, b in pairs for p in range(plane)]
        return lax.ppermute(array, AXES, whole)

    def swap(array, step):
        pairs = [(i, i // plane * plane + (i % plane ^ step)) for i in range(line * plane)]
        return lax.ppermute(array, AXES, pairs)

    block = embed(
        states,
        projection,
        owner_group.reshape(1, rows),
        cluster_sub.reshape(1, rows),
        priority.reshape(1, rows),
    )
    moves = tournament(line)
    visitors = [move(block, pairs) for pairs in moves]
    bits = [1 << i for i in range(1, plane.bit_length() - 1)]
    found = {0: block}
    for bit in reversed(bits):
        found |= {step | bit: swap(here, bit) for step, here in found.items()}
    row_blocks = [found[step] for step in sorted(found)]

    lanes = [block] + visitors
    every, count = tuple(range(len(lanes))), len(row_blocks)
    half = count // 2
    soon = (0, half)
    rest = tuple(i for i in range(count) if i not in soon)
    lines, held = score(
        "score_soon", [row_blocks[i] for i in soon], lanes[:1], [((0, 1), (0,))], [], hold=True
    )
    row_blocks[0] = lanes[0] = held
    products = [(rest, every), (soon, every[1:])]
    lines, backs = score("score_late", row_blocks, lanes, products, [(0, count)], lines)
    partner = [held]
    partner += [lax.optimization_barrier((visitor, held))[0] for visitor in visitors[:-1]]
    partner += [lax.optimization_barrier((visitors[-1], row_blocks[1]))[0]]
    partner = [swap(lane, 1) for lane in partner]
    products, parts = [(tuple(range(count)), every)], [(0, half), (half, count)]
    theirs, near, far = score("score_partner", row_blocks, partner, products, parts, None, backs)
    lines = jnp.maximum(lines, swap(theirs, 1))
    for bit in bits[:0:-1]:
        near = jnp.maximum(near, swap(far, bit))
        half = near.shape[0] // 2
        near, far = near[:half], near[half:]
    total = lines[:1]
    for i, pairs in reversed(list(enumerate(moves))):
        total = jnp.maximum(total, move(lines[i + 1:i + 2], [(b, a) for a, b in pairs]))
    total = lax.optimization_barrier(total)
    total = jnp.maximum(jnp.maximum(total, near), swap(far, bits[0]))
    return total.reshape(rows)


def solution(mesh):
    num_dp, num_grp = mesh.shape["dp"], mesh.shape["grp"]
    line = min(num_dp, 1 << (int(math.log2(num_dp * num_grp)) // 2))
    split = Mesh(mesh.devices.reshape(line, num_dp // line, num_grp), AXES)
    in_specs = (P(AXES, None), P(), P(AXES, None), P(AXES), P(AXES))
    return jax.shard_map(
        on_device, mesh=split, in_specs=in_specs, out_specs=P(AXES), check_vma=False
    )
```

```python
import math

import jax
import jax.numpy as jnp
from jax import lax
from jax.experimental import pallas as pl
from jax.experimental.pallas import tpu as pltpu
from jax.sharding import Mesh, PartitionSpec as P

AXES = ("line", "mid", "grp")
NOTE_ROWS = 8
MORE_ROWS = 56
RADIX = 256
CHUNKS = 4
VMEM = pl.BlockSpec(memory_space=pltpu.VMEM)
HBM = pl.BlockSpec(memory_space=pltpu.HBM)


def embed_kernel(
    states_hbm, proj_hbm, owner_hbm, sub_hbm, prio_hbm, block_ref, tall_ref,
    states, proj, owner, sub, prio, big_sem, small_sem,
):
    rows, depth = states.shape
    width = proj.shape[1]
    span = depth // CHUNKS
    whole = pltpu.make_async_copy(states_hbm, states, big_sem.at[CHUNKS])
    copies = [
        pltpu.make_async_copy(
            proj_hbm.at[pl.ds(i * span, span)], proj.at[pl.ds(i * span, span)], big_sem.at[i]
        )
        for i in range(CHUNKS)
    ]
    small = [
        pltpu.make_async_copy(src, dst, small_sem.at[i])
        for i, (src, dst) in enumerate(((owner_hbm, owner), (sub_hbm, sub), (prio_hbm, prio)))
    ]
    for copy in [whole] + copies + small:
        copy.start()
    whole.wait()
    projected = None
    for i, copy in enumerate(copies):
        copy.wait()
        part = slice(i * span, (i + 1) * span)
        term = jnp.dot(states[:, part], proj[part, :], preferred_element_type=jnp.float32)
        projected = term if projected is None else projected + term
    square_sum = jnp.sum(projected * projected, axis=1, keepdims=True)
    embedding = projected * lax.rsqrt(square_sum + 1e-06)
    for copy in small:
        copy.wait()
    rank = prio[...]
    high = lax.shift_right_logical(rank, 8)
    fields = (owner[...] + 1, sub[...], high, rank - high * RADIX)
    notes = [f.astype(jnp.float32) for f in fields]
    notes.append(jnp.zeros((NOTE_ROWS - len(fields), rows), jnp.float32))
    tiles = [embedding[:, i:i + rows] for i in range(0, width, rows)]
    block = jnp.concatenate(tiles + notes, axis=0).astype(jnp.bfloat16)
    block_ref[...] = block
    tall_ref[:block.shape[0], :] = block
    tall_ref[block.shape[0]:, :] = block[:tall_ref.shape[0] - block.shape[0]]


def embed(states, projection, owner, sub, prio):
    rows, depth = states.shape
    width = projection.shape[1]
    high = rows * (width // rows) + NOTE_ROWS
    return pl.pallas_call(
        embed_kernel,
        in_specs=[HBM] * 5,
        out_specs=[VMEM] * 2,
        out_shape=[jax.ShapeDtypeStruct((tall, rows), jnp.bfloat16) for tall in (high, high + MORE_ROWS)],
        scratch_shapes=[
            pltpu.VMEM((rows, depth), jnp.bfloat16),
            pltpu.VMEM((depth, width), jnp.bfloat16),
            pltpu.VMEM((1, rows), jnp.int32),
            pltpu.VMEM((1, rows), jnp.int32),
            pltpu.VMEM((1, rows), jnp.int32),
            pltpu.SemaphoreType.DMA((CHUNKS + 1,)),
            pltpu.SemaphoreType.DMA((3,)),
        ],
        compiler_params=pltpu.CompilerParams(vmem_limit_bytes=40 << 20),
        name="embed",
    )(*(pltpu.with_memory_space_constraint(x, pltpu.HBM) for x in (states, projection, owner, sub, prio)))


def read_notes(ref):
    first = ref.shape[0] // ref.shape[1] * ref.shape[1]
    tail = ref[first:first + NOTE_ROWS, :].astype(jnp.float32)
    owner, sub, high, low = (tail[i:i + 1] for i in range(4))
    return (owner - 1.0) * 4.0 + sub, high * float(RADIX) + low


def read_rows(refs):
    rows = refs[0].shape[1]
    return jnp.concatenate(
        [
            jnp.concatenate([ref[i * rows:(i + 1) * rows, :] for ref in refs], axis=0)
            for i in range(refs[0].shape[0] // rows)
        ],
        axis=1,
    )


def score_kernel(row_count, lane_count, products, parts, has_lines, seen_rows, hold, *refs):
    refs = list(refs)
    row_refs = [refs.pop(0) for _ in range(row_count)]
    lane_refs = [refs.pop(0) for _ in range(lane_count)]
    seen_lines = refs.pop(0) if has_lines else None
    seen_backs = refs.pop(0) if seen_rows else None
    lines_out = refs.pop(0)
    rows = lines_out.shape[1]
    if hold:
        refs[-1][...] = row_refs[0][...]
    row_notes = [read_notes(ref) for ref in row_refs]
    lane_notes = [read_notes(ref) for ref in lane_refs]
    fill = jnp.zeros((-2 * row_count % 8, rows), jnp.float32)
    lines = [line for pair in row_notes for line in pair]
    columns = jnp.concatenate(lines + ([fill] if fill.size else []), axis=0).T
    best, back = [None] * lane_count, [None] * row_count

    def top(old, new):
        return new if old is None else jnp.maximum(old, new)

    for row_set, lane_set in products:
        cosine = lax.dot_general(
            read_rows([row_refs[i] for i in row_set]),
            read_rows([lane_refs[j] for j in lane_set]),
            (((1,), (1,)), ((), ())),
            preferred_element_type=jnp.float32,
        )
        for m, i in enumerate(row_set):
            row_cluster, row_prio = columns[:, 2 * i:2 * i + 1], columns[:, 2 * i + 1:2 * i + 2]
            for n, j in enumerate(lane_set):
                lane_cluster, lane_prio = lane_notes[j]
                here = cosine[m * rows:(m + 1) * rows, n * rows:(n + 1) * rows]
                same = jnp.where(row_cluster == lane_cluster, here, -1.0)
                earlier = row_prio < lane_prio
                best[j] = top(best[j], jnp.where(earlier, same, -1.0))
                if j > 0:
                    back[i] = top(back[i], jnp.where(earlier, -1.0, same))
    lane_ids = lax.broadcasted_iota(jnp.int32, (rows, rows), 1)
    table = jnp.full((rows, rows), -1.0, jnp.float32)
    for i, each in enumerate(back):
        if each is not None:
            table = jnp.where(lane_ids == i, jnp.max(each, axis=1, keepdims=True), table)
    table = table.T
    if seen_rows:
        table = jnp.maximum(table[:row_count], seen_backs[...])
    for first, stop in parts:
        refs.pop(0)[...] = table[first:stop]
    lines = jnp.concatenate([jnp.max(b, axis=0, keepdims=True) for b in best], axis=0)
    if has_lines:
        count = seen_lines.shape[0]
        first = jnp.maximum(lines[:count], seen_lines[...])
        lines = first if count == lane_count else jnp.concatenate([first, lines[count:]], axis=0)
    lines_out[...] = lines


def score(name, row_blocks, lane_blocks, products, parts, lines=None, backs=None, hold=False):
    high, rows = row_blocks[0].shape
    width = high - NOTE_ROWS
    inputs = [*row_blocks, *lane_blocks, *(seen for seen in (lines, backs) if seen is not None)]
    shapes = [(len(lane_blocks), rows)] + [(stop - first, rows) for first, stop in parts]
    outs = [jax.ShapeDtypeStruct(shape, jnp.float32) for shape in shapes]
    if hold:
        outs.append(jax.ShapeDtypeStruct((high, rows), row_blocks[0].dtype))
    counts = len(row_blocks), len(lane_blocks)
    rest = products, parts, lines is not None, backs is not None, hold
    macs = sum(len(r) * len(c) for r, c in products) * rows * rows * width
    return pl.pallas_call(
        lambda *refs: score_kernel(*counts, *rest, *refs),
        in_specs=[VMEM] * len(inputs),
        out_specs=[VMEM] * len(outs),
        out_shape=outs,
        compiler_params=pltpu.CompilerParams(vmem_limit_bytes=48 << 20),
        cost_estimate=pl.CostEstimate(
            flops=2 * macs, bytes_accessed=2 * sum(counts) * rows * width, transcendentals=0
        ),
        name=name,
    )(*inputs)


def tournament(line):
    moves = [[(i, (i + s) % line) for i in range(line)] for s in range(1, (line + 1) // 2)]
    if line % 2 == 0:
        half = line // 2
        pairs = [(i, i + half) if i % 2 else (i + half, i) for i in range(half)]
        sent, met = {a for a, _ in pairs}, {b for _, b in pairs}
        idle = [i for i in range(line) if i not in sent]
        free = [i for i in range(line) if i not in met]
        moves.append(pairs + list(zip(idle, free)))
    return moves


def on_device(states, projection, owner_group, cluster_sub, priority):
    line, grp = lax.axis_size("line"), lax.axis_size("grp")
    plane = lax.axis_size("mid") * grp
    rows = states.shape[0]

    def move(array, pairs):
        whole = [(a * plane + p, b * plane + p) for a, b in pairs for p in range(plane)]
        return lax.ppermute(array, AXES, whole)

    def swap(array, step):
        pairs = [(i, i // plane * plane + (i % plane ^ step)) for i in range(line * plane)]
        return lax.ppermute(array, AXES, pairs)

    block, tall = embed(
        states,
        projection,
        owner_group.reshape(1, rows),
        cluster_sub.reshape(1, rows),
        priority.reshape(1, rows),
    )
    moves = tournament(line)
    visitors = [move(tall, moves[0])] + [move(block, pairs) for pairs in moves[1:]]
    bits = [1 << i for i in range(1, plane.bit_length() - 1)]
    found = {0: block}
    for bit in reversed(bits):
        found |= {step | bit: swap(here, bit) for step, here in found.items()}
    row_blocks = [found[step] for step in sorted(found)]

    lanes = [block] + visitors
    every, count = tuple(range(len(lanes))), len(row_blocks)
    half = count // 2
    soon = (0, half)
    rest = tuple(i for i in range(count) if i not in soon)
    lines, held = score(
        "score_soon", [row_blocks[i] for i in soon], lanes[:1], [((0, 1), (0,))], [], hold=True
    )
    row_blocks[0] = lanes[0] = held
    products = [(rest, every), (soon, every[1:])]
    lines, backs = score("score_late", row_blocks, lanes, products, [(0, count)], lines)
    partner = [held]
    partner += [lax.optimization_barrier((visitor, held))[0] for visitor in visitors[:-1]]
    partner += [lax.optimization_barrier((visitors[-1], row_blocks[1]))[0]]
    partner = [swap(lane, 1) for lane in partner]
    products, parts = [(tuple(range(count)), every)], [(0, half), (half, count)]
    theirs, near, far = score("score_partner", row_blocks, partner, products, parts, None, backs)
    lines = jnp.maximum(lines, swap(theirs, 1))
    for bit in bits[:0:-1]:
        near = jnp.maximum(near, swap(far, bit))
        half = near.shape[0] // 2
        near, far = near[:half], near[half:]
    total = lines[:1]
    for i, pairs in reversed(list(enumerate(moves))):
        total = jnp.maximum(total, move(lines[i + 1:i + 2], [(b, a) for a, b in pairs]))
    total = lax.optimization_barrier(total)
    total = jnp.maximum(jnp.maximum(total, near), swap(far, bits[0]))
    return total.reshape(rows)


def solution(mesh):
    num_dp, num_grp = mesh.shape["dp"], mesh.shape["grp"]
    line = min(num_dp, 1 << (int(math.log2(num_dp * num_grp)) // 2))
    split = Mesh(mesh.devices.reshape(line, num_dp // line, num_grp), AXES)
    in_specs = (P(AXES, None), P(), P(AXES, None), P(AXES), P(AXES))
    return jax.shard_map(
        on_device, mesh=split, in_specs=in_specs, out_specs=P(AXES), check_vma=False
    )
```

```python
import math

import jax
import jax.numpy as jnp
from jax import lax
from jax.experimental import pallas as pl
from jax.experimental.pallas import tpu as pltpu
from jax.sharding import Mesh, PartitionSpec as P

AXES = ("line", "mid", "grp")
NOTE_ROWS = 8
MORE_ROWS = 48
RADIX = 256
CHUNKS = 4
VMEM = pl.BlockSpec(memory_space=pltpu.VMEM)
HBM = pl.BlockSpec(memory_space=pltpu.HBM)


def embed_kernel(
    states_hbm, proj_hbm, owner_hbm, sub_hbm, prio_hbm, block_ref, tall_ref,
    states, proj, owner, sub, prio, big_sem, small_sem,
):
    rows, depth = states.shape
    width = proj.shape[1]
    span = depth // CHUNKS
    whole = pltpu.make_async_copy(states_hbm, states, big_sem.at[CHUNKS])
    copies = [
        pltpu.make_async_copy(
            proj_hbm.at[pl.ds(i * span, span)], proj.at[pl.ds(i * span, span)], big_sem.at[i]
        )
        for i in range(CHUNKS)
    ]
    small = [
        pltpu.make_async_copy(src, dst, small_sem.at[i])
        for i, (src, dst) in enumerate(((owner_hbm, owner), (sub_hbm, sub), (prio_hbm, prio)))
    ]
    for copy in [whole] + copies + small:
        copy.start()
    whole.wait()
    projected = None
    for i, copy in enumerate(copies):
        copy.wait()
        part = slice(i * span, (i + 1) * span)
        term = jnp.dot(states[:, part], proj[part, :], preferred_element_type=jnp.float32)
        projected = term if projected is None else projected + term
    square_sum = jnp.sum(projected * projected, axis=1, keepdims=True)
    embedding = projected * lax.rsqrt(square_sum + 1e-06)
    for copy in small:
        copy.wait()
    rank = prio[...]
    high = lax.shift_right_logical(rank, 8)
    fields = (owner[...] + 1, sub[...], high, rank - high * RADIX)
    notes = [f.astype(jnp.float32) for f in fields]
    notes.append(jnp.zeros((NOTE_ROWS - len(fields), rows), jnp.float32))
    tiles = [embedding[:, i:i + rows] for i in range(0, width, rows)]
    block = jnp.concatenate(tiles + notes, axis=0).astype(jnp.bfloat16)
    block_ref[...] = block
    tall_ref[:block.shape[0], :] = block
    tall_ref[block.shape[0]:, :] = block[:tall_ref.shape[0] - block.shape[0]]


def embed(states, projection, owner, sub, prio):
    rows, depth = states.shape
    width = projection.shape[1]
    high = rows * (width // rows) + NOTE_ROWS
    return pl.pallas_call(
        embed_kernel,
        in_specs=[HBM] * 5,
        out_specs=[VMEM] * 2,
        out_shape=[jax.ShapeDtypeStruct((tall, rows), jnp.bfloat16) for tall in (high, high + MORE_ROWS)],
        scratch_shapes=[
            pltpu.VMEM((rows, depth), jnp.bfloat16),
            pltpu.VMEM((depth, width), jnp.bfloat16),
            pltpu.VMEM((1, rows), jnp.int32),
            pltpu.VMEM((1, rows), jnp.int32),
            pltpu.VMEM((1, rows), jnp.int32),
            pltpu.SemaphoreType.DMA((CHUNKS + 1,)),
            pltpu.SemaphoreType.DMA((3,)),
        ],
        compiler_params=pltpu.CompilerParams(vmem_limit_bytes=40 << 20),
        name="embed",
    )(*(pltpu.with_memory_space_constraint(x, pltpu.HBM) for x in (states, projection, owner, sub, prio)))


def read_notes(ref):
    first = ref.shape[0] // ref.shape[1] * ref.shape[1]
    tail = ref[first:first + NOTE_ROWS, :].astype(jnp.float32)
    owner, sub, high, low = (tail[i:i + 1] for i in range(4))
    return (owner - 1.0) * 4.0 + sub, high * float(RADIX) + low


def read_rows(refs):
    rows = refs[0].shape[1]
    return jnp.concatenate(
        [
            jnp.concatenate([ref[i * rows:(i + 1) * rows, :] for ref in refs], axis=0)
            for i in range(refs[0].shape[0] // rows)
        ],
        axis=1,
    )


def score_kernel(row_count, lane_count, products, parts, has_lines, seen_rows, hold, *refs):
    refs = list(refs)
    row_refs = [refs.pop(0) for _ in range(row_count)]
    lane_refs = [refs.pop(0) for _ in range(lane_count)]
    seen_lines = refs.pop(0) if has_lines else None
    seen_backs = refs.pop(0) if seen_rows else None
    lines_out = refs.pop(0)
    rows = lines_out.shape[1]
    if hold:
        refs[-1][...] = row_refs[0][...]
    row_notes = [read_notes(ref) for ref in row_refs]
    lane_notes = [read_notes(ref) for ref in lane_refs]
    fill = jnp.zeros((-2 * row_count % 8, rows), jnp.float32)
    lines = [line for pair in row_notes for line in pair]
    columns = jnp.concatenate(lines + ([fill] if fill.size else []), axis=0).T
    best, back = [None] * lane_count, [None] * row_count

    def top(old, new):
        return new if old is None else jnp.maximum(old, new)

    for row_set, lane_set in products:
        cosine = lax.dot_general(
            read_rows([row_refs[i] for i in row_set]),
            read_rows([lane_refs[j] for j in lane_set]),
            (((1,), (1,)), ((), ())),
            preferred_element_type=jnp.float32,
        )
        for m, i in enumerate(row_set):
            row_cluster, row_prio = columns[:, 2 * i:2 * i + 1], columns[:, 2 * i + 1:2 * i + 2]
            for n, j in enumerate(lane_set):
                lane_cluster, lane_prio = lane_notes[j]
                here = cosine[m * rows:(m + 1) * rows, n * rows:(n + 1) * rows]
                same = jnp.where(row_cluster == lane_cluster, here, -1.0)
                earlier = row_prio < lane_prio
                best[j] = top(best[j], jnp.where(earlier, same, -1.0))
                if j > 0:
                    back[i] = top(back[i], jnp.where(earlier, -1.0, same))
    lane_ids = lax.broadcasted_iota(jnp.int32, (rows, rows), 1)
    table = jnp.full((rows, rows), -1.0, jnp.float32)
    for i, each in enumerate(back):
        if each is not None:
            table = jnp.where(lane_ids == i, jnp.max(each, axis=1, keepdims=True), table)
    table = table.T
    if seen_rows:
        table = jnp.maximum(table[:row_count], seen_backs[...])
    for first, stop in parts:
        refs.pop(0)[...] = table[first:stop]
    lines = jnp.concatenate([jnp.max(b, axis=0, keepdims=True) for b in best], axis=0)
    if has_lines:
        count = seen_lines.shape[0]
        first = jnp.maximum(lines[:count], seen_lines[...])
        lines = first if count == lane_count else jnp.concatenate([first, lines[count:]], axis=0)
    lines_out[...] = lines


def score(name, row_blocks, lane_blocks, products, parts, lines=None, backs=None, hold=False):
    high, rows = row_blocks[0].shape
    width = high - NOTE_ROWS
    inputs = [*row_blocks, *lane_blocks, *(seen for seen in (lines, backs) if seen is not None)]
    shapes = [(len(lane_blocks), rows)] + [(stop - first, rows) for first, stop in parts]
    outs = [jax.ShapeDtypeStruct(shape, jnp.float32) for shape in shapes]
    if hold:
        outs.append(jax.ShapeDtypeStruct((high, rows), row_blocks[0].dtype))
    counts = len(row_blocks), len(lane_blocks)
    rest = products, parts, lines is not None, backs is not None, hold
    macs = sum(len(r) * len(c) for r, c in products) * rows * rows * width
    return pl.pallas_call(
        lambda *refs: score_kernel(*counts, *rest, *refs),
        in_specs=[VMEM] * len(inputs),
        out_specs=[VMEM] * len(outs),
        out_shape=outs,
        compiler_params=pltpu.CompilerParams(vmem_limit_bytes=48 << 20),
        cost_estimate=pl.CostEstimate(
            flops=2 * macs, bytes_accessed=2 * sum(counts) * rows * width, transcendentals=0
        ),
        name=name,
    )(*inputs)


def tournament(line):
    moves = [[(i, (i + s) % line) for i in range(line)] for s in range(1, (line + 1) // 2)]
    if line % 2 == 0:
        half = line // 2
        pairs = [(i, i + half) if i % 2 else (i + half, i) for i in range(half)]
        sent, met = {a for a, _ in pairs}, {b for _, b in pairs}
        idle = [i for i in range(line) if i not in sent]
        free = [i for i in range(line) if i not in met]
        moves.append(pairs + list(zip(idle, free)))
    return moves


def on_device(states, projection, owner_group, cluster_sub, priority):
    line, grp = lax.axis_size("line"), lax.axis_size("grp")
    plane = lax.axis_size("mid") * grp
    rows = states.shape[0]

    def move(array, pairs):
        whole = [(a * plane + p, b * plane + p) for a, b in pairs for p in range(plane)]
        return lax.ppermute(array, AXES, whole)

    def swap(array, step):
        pairs = [(i, i // plane * plane + (i % plane ^ step)) for i in range(line * plane)]
        return lax.ppermute(array, AXES, pairs)

    block, tall = embed(
        states,
        projection,
        owner_group.reshape(1, rows),
        cluster_sub.reshape(1, rows),
        priority.reshape(1, rows),
    )
    moves = tournament(line)
    visitors = [move(tall, moves[0])] + [move(block, pairs) for pairs in moves[1:]]
    bits = [1 << i for i in range(1, plane.bit_length() - 1)]
    found = {0: block}
    for bit in reversed(bits):
        found |= {step | bit: swap(here, bit) for step, here in found.items()}
    row_blocks = [found[step] for step in sorted(found)]

    lanes = [block] + visitors
    every, count = tuple(range(len(lanes))), len(row_blocks)
    half = count // 2
    soon, early = tuple(range(half + 1)), every[:-1]
    rest = tuple(range(half + 1, count))
    lines, backs, held = score(
        "score_soon", [row_blocks[i] for i in soon], lanes[:-1], [(soon, early)], [(0, count)], hold=True
    )
    row_blocks[0] = lanes[0] = held
    products = [(rest, every), (soon, every[-1:])]
    lines, backs = score("score_late", row_blocks, lanes, products, [(0, count)], lines, backs)
    partner = [block, *visitors[:-1], lax.optimization_barrier((visitors[-1], held))[0]]
    partner = [swap(lane, 1) for lane in partner]
    products, parts = [(tuple(range(count)), every)], [(0, half), (half, count)]
    theirs, near, far = score("score_partner", row_blocks, partner, products, parts, None, backs)
    lines = jnp.maximum(lines, swap(theirs, 1))
    for bit in bits[:0:-1]:
        near = jnp.maximum(near, swap(far, bit))
        half = near.shape[0] // 2
        near, far = near[:half], near[half:]
    total = lines[:1]
    for i, pairs in reversed(list(enumerate(moves))):
        total = jnp.maximum(total, move(lines[i + 1:i + 2], [(b, a) for a, b in pairs]))
    total = lax.optimization_barrier(total)
    total = jnp.maximum(jnp.maximum(total, near), swap(far, bits[0]))
    return total.reshape(rows)


def solution(mesh):
    num_dp, num_grp = mesh.shape["dp"], mesh.shape["grp"]
    line = min(num_dp, 1 << (int(math.log2(num_dp * num_grp)) // 2))
    split = Mesh(mesh.devices.reshape(line, num_dp // line, num_grp), AXES)
    in_specs = (P(AXES, None), P(), P(AXES, None), P(AXES), P(AXES))
    return jax.shard_map(
        on_device, mesh=split, in_specs=in_specs, out_specs=P(AXES), check_vma=False
    )
```

```python
import math

import jax
import jax.numpy as jnp
from jax import lax
from jax.experimental import pallas as pl
from jax.experimental.pallas import tpu as pltpu
from jax.sharding import Mesh, PartitionSpec as P

AXES = ("line", "mid", "grp")
NOTE_ROWS = 8
MORE_ROWS = 48
RADIX = 256
CHUNKS = 4
VMEM = pl.BlockSpec(memory_space=pltpu.VMEM)
HBM = pl.BlockSpec(memory_space=pltpu.HBM)


def embed_kernel(
    states_hbm, proj_hbm, owner_hbm, sub_hbm, prio_hbm, block_ref, tall_ref,
    states, proj, owner, sub, prio, big_sem, small_sem,
):
    rows, depth = states.shape
    width = proj.shape[1]
    span = depth // CHUNKS
    whole = pltpu.make_async_copy(states_hbm, states, big_sem.at[CHUNKS])
    copies = [
        pltpu.make_async_copy(
            proj_hbm.at[pl.ds(i * span, span)], proj.at[pl.ds(i * span, span)], big_sem.at[i]
        )
        for i in range(CHUNKS)
    ]
    small = [
        pltpu.make_async_copy(src, dst, small_sem.at[i])
        for i, (src, dst) in enumerate(((owner_hbm, owner), (sub_hbm, sub), (prio_hbm, prio)))
    ]
    whole.start(priority=1)
    for i, copy in enumerate(copies):
        copy.start(priority=1 if i < CHUNKS // 2 else 0)
    for copy in small:
        copy.start()
    whole.wait()
    projected = None
    for i, copy in enumerate(copies):
        copy.wait()
        part = slice(i * span, (i + 1) * span)
        term = jnp.dot(states[:, part], proj[part, :], preferred_element_type=jnp.float32)
        projected = term if projected is None else projected + term
    square_sum = jnp.sum(projected * projected, axis=1, keepdims=True)
    embedding = projected * lax.rsqrt(square_sum + 1e-06)
    for copy in small:
        copy.wait()
    rank = prio[...]
    high = lax.shift_right_logical(rank, 8)
    fields = (owner[...] + 1, sub[...], high, rank - high * RADIX)
    notes = [f.astype(jnp.float32) for f in fields]
    notes.append(jnp.zeros((NOTE_ROWS - len(fields), rows), jnp.float32))
    tiles = [embedding[:, i:i + rows] for i in range(0, width, rows)]
    block = jnp.concatenate(tiles + notes, axis=0).astype(jnp.bfloat16)
    block_ref[...] = block
    tall_ref[:block.shape[0], :] = block
    tall_ref[block.shape[0]:, :] = block[:tall_ref.shape[0] - block.shape[0]]


def embed(states, projection, owner, sub, prio):
    rows, depth = states.shape
    width = projection.shape[1]
    high = rows * (width // rows) + NOTE_ROWS
    return pl.pallas_call(
        embed_kernel,
        in_specs=[HBM] * 5,
        out_specs=[VMEM] * 2,
        out_shape=[jax.ShapeDtypeStruct((tall, rows), jnp.bfloat16) for tall in (high, high + MORE_ROWS)],
        scratch_shapes=[
            pltpu.VMEM((rows, depth), jnp.bfloat16),
            pltpu.VMEM((depth, width), jnp.bfloat16),
            pltpu.VMEM((1, rows), jnp.int32),
            pltpu.VMEM((1, rows), jnp.int32),
            pltpu.VMEM((1, rows), jnp.int32),
            pltpu.SemaphoreType.DMA((CHUNKS + 1,)),
            pltpu.SemaphoreType.DMA((3,)),
        ],
        compiler_params=pltpu.CompilerParams(vmem_limit_bytes=40 << 20),
        name="embed",
    )(*(pltpu.with_memory_space_constraint(x, pltpu.HBM) for x in (states, projection, owner, sub, prio)))


def read_notes(ref):
    first = ref.shape[0] // ref.shape[1] * ref.shape[1]
    tail = ref[first:first + NOTE_ROWS, :].astype(jnp.float32)
    owner, sub, high, low = (tail[i:i + 1] for i in range(4))
    return (owner - 1.0) * 4.0 + sub, high * float(RADIX) + low


def read_rows(refs):
    rows = refs[0].shape[1]
    return jnp.concatenate(
        [
            jnp.concatenate([ref[i * rows:(i + 1) * rows, :] for ref in refs], axis=0)
            for i in range(refs[0].shape[0] // rows)
        ],
        axis=1,
    )


def score_kernel(row_count, lane_count, products, parts, has_lines, seen_rows, hold, *refs):
    refs = list(refs)
    row_refs = [refs.pop(0) for _ in range(row_count)]
    lane_refs = [refs.pop(0) for _ in range(lane_count)]
    seen_lines = refs.pop(0) if has_lines else None
    seen_backs = refs.pop(0) if seen_rows else None
    lines_out = refs.pop(0)
    rows = lines_out.shape[1]
    if hold:
        refs[-1][...] = row_refs[0][...]
    row_notes = [read_notes(ref) for ref in row_refs]
    lane_notes = [read_notes(ref) for ref in lane_refs]
    fill = jnp.zeros((-2 * row_count % 8, rows), jnp.float32)
    lines = [line for pair in row_notes for line in pair]
    columns = jnp.concatenate(lines + ([fill] if fill.size else []), axis=0).T
    best, back = [None] * lane_count, [None] * row_count

    def top(old, new):
        return new if old is None else jnp.maximum(old, new)

    for row_set, lane_set in products:
        cosine = lax.dot_general(
            read_rows([row_refs[i] for i in row_set]),
            read_rows([lane_refs[j] for j in lane_set]),
            (((1,), (1,)), ((), ())),
            preferred_element_type=jnp.float32,
        )
        for m, i in enumerate(row_set):
            row_cluster, row_prio = columns[:, 2 * i:2 * i + 1], columns[:, 2 * i + 1:2 * i + 2]
            for n, j in enumerate(lane_set):
                lane_cluster, lane_prio = lane_notes[j]
                here = cosine[m * rows:(m + 1) * rows, n * rows:(n + 1) * rows]
                same = jnp.where(row_cluster == lane_cluster, here, -1.0)
                earlier = row_prio < lane_prio
                best[j] = top(best[j], jnp.where(earlier, same, -1.0))
                if j > 0:
                    back[i] = top(back[i], jnp.where(earlier, -1.0, same))
    lane_ids = lax.broadcasted_iota(jnp.int32, (rows, rows), 1)
    table = jnp.full((rows, rows), -1.0, jnp.float32)
    for i, each in enumerate(back):
        if each is not None:
            table = jnp.where(lane_ids == i, jnp.max(each, axis=1, keepdims=True), table)
    table = table.T
    if seen_rows:
        table = jnp.maximum(table[:row_count], seen_backs[...])
    for first, stop in parts:
        refs.pop(0)[...] = table[first:stop]
    lines = jnp.concatenate([jnp.max(b, axis=0, keepdims=True) for b in best], axis=0)
    if has_lines:
        count = seen_lines.shape[0]
        first = jnp.maximum(lines[:count], seen_lines[...])
        lines = first if count == lane_count else jnp.concatenate([first, lines[count:]], axis=0)
    lines_out[...] = lines


def score(name, row_blocks, lane_blocks, products, parts, lines=None, backs=None, hold=False):
    high, rows = row_blocks[0].shape
    width = high - NOTE_ROWS
    inputs = [*row_blocks, *lane_blocks, *(seen for seen in (lines, backs) if seen is not None)]
    shapes = [(len(lane_blocks), rows)] + [(stop - first, rows) for first, stop in parts]
    outs = [jax.ShapeDtypeStruct(shape, jnp.float32) for shape in shapes]
    if hold:
        outs.append(jax.ShapeDtypeStruct((high, rows), row_blocks[0].dtype))
    counts = len(row_blocks), len(lane_blocks)
    rest = products, parts, lines is not None, backs is not None, hold
    macs = sum(len(r) * len(c) for r, c in products) * rows * rows * width
    return pl.pallas_call(
        lambda *refs: score_kernel(*counts, *rest, *refs),
        in_specs=[VMEM] * len(inputs),
        out_specs=[VMEM] * len(outs),
        out_shape=outs,
        compiler_params=pltpu.CompilerParams(vmem_limit_bytes=48 << 20),
        cost_estimate=pl.CostEstimate(
            flops=2 * macs, bytes_accessed=2 * sum(counts) * rows * width, transcendentals=0
        ),
        name=name,
    )(*inputs)


def tournament(line):
    moves = [[(i, (i + s) % line) for i in range(line)] for s in range(1, (line + 1) // 2)]
    if line % 2 == 0:
        half = line // 2
        pairs = [(i, i + half) if i % 2 else (i + half, i) for i in range(half)]
        sent, met = {a for a, _ in pairs}, {b for _, b in pairs}
        idle = [i for i in range(line) if i not in sent]
        free = [i for i in range(line) if i not in met]
        moves.append(pairs + list(zip(idle, free)))
    return moves


def on_device(states, projection, owner_group, cluster_sub, priority):
    line, grp = lax.axis_size("line"), lax.axis_size("grp")
    plane = lax.axis_size("mid") * grp
    rows = states.shape[0]

    def move(array, pairs):
        whole = [(a * plane + p, b * plane + p) for a, b in pairs for p in range(plane)]
        return lax.ppermute(array, AXES, whole)

    def swap(array, step):
        pairs = [(i, i // plane * plane + (i % plane ^ step)) for i in range(line * plane)]
        return lax.ppermute(array, AXES, pairs)

    block, tall = embed(
        states,
        projection,
        owner_group.reshape(1, rows),
        cluster_sub.reshape(1, rows),
        priority.reshape(1, rows),
    )
    moves = tournament(line)
    visitors = [move(tall, moves[0])] + [move(block, pairs) for pairs in moves[1:]]
    bits = [1 << i for i in range(1, plane.bit_length() - 1)]
    found = {0: block}
    for bit in reversed(bits):
        found |= {step | bit: swap(here, bit) for step, here in found.items()}
    row_blocks = [found[step] for step in sorted(found)]

    lanes = [block] + visitors
    every, count = tuple(range(len(lanes))), len(row_blocks)
    half = count // 2
    soon = (0, half)
    rest = tuple(i for i in range(count) if i not in soon)
    lines, held = score(
        "score_soon", [row_blocks[i] for i in soon], lanes[:1], [((0, 1), (0,))], [], hold=True
    )
    row_blocks[0] = lanes[0] = held
    products = [(rest, every), (soon, every[1:])]
    lines, backs = score("score_late", row_blocks, lanes, products, [(0, count)], lines)
    partner = [held]
    partner += [lax.optimization_barrier((visitor, held))[0] for visitor in visitors[:-1]]
    partner += [lax.optimization_barrier((visitors[-1], row_blocks[1]))[0]]
    partner = [swap(lane, 1) for lane in partner]
    products, parts = [(tuple(range(count)), every)], [(0, half), (half, count)]
    theirs, near, far = score("score_partner", row_blocks, partner, products, parts, None, backs)
    lines = jnp.maximum(lines, swap(theirs, 1))
    for bit in bits[:0:-1]:
        near = jnp.maximum(near, swap(far, bit))
        half = near.shape[0] // 2
        near, far = near[:half], near[half:]
    total = lines[:1]
    for i, pairs in reversed(list(enumerate(moves))):
        total = jnp.maximum(total, move(lines[i + 1:i + 2], [(b, a) for a, b in pairs]))
    total = lax.optimization_barrier(total)
    total = jnp.maximum(jnp.maximum(total, near), swap(far, bits[0]))
    return total.reshape(rows)


def solution(mesh):
    num_dp, num_grp = mesh.shape["dp"], mesh.shape["grp"]
    line = min(num_dp, 1 << (int(math.log2(num_dp * num_grp)) // 2))
    split = Mesh(mesh.devices.reshape(line, num_dp // line, num_grp), AXES)
    in_specs = (P(AXES, None), P(), P(AXES, None), P(AXES), P(AXES))
    return jax.shard_map(
        on_device, mesh=split, in_specs=in_specs, out_specs=P(AXES), check_vma=False
    )
```

```python
import math

import jax
import jax.numpy as jnp
from jax import lax
from jax.experimental import pallas as pl
from jax.experimental.pallas import tpu as pltpu
from jax.sharding import Mesh, PartitionSpec as P

AXES = ("line", "mid", "grp")
NOTE_ROWS = 8
MORE_ROWS = 56
RADIX = 256
CHUNKS = 4
VMEM = pl.BlockSpec(memory_space=pltpu.VMEM)
HBM = pl.BlockSpec(memory_space=pltpu.HBM)


def embed_kernel(
    states_hbm, proj_hbm, owner_hbm, sub_hbm, prio_hbm, block_ref, tall_ref,
    states, proj, owner, sub, prio, big_sem, small_sem,
):
    rows, depth = states.shape
    width = proj.shape[1]
    span = depth // CHUNKS
    whole = pltpu.make_async_copy(states_hbm, states, big_sem.at[CHUNKS])
    copies = [
        pltpu.make_async_copy(
            proj_hbm.at[pl.ds(i * span, span)], proj.at[pl.ds(i * span, span)], big_sem.at[i]
        )
        for i in range(CHUNKS)
    ]
    small = [
        pltpu.make_async_copy(src, dst, small_sem.at[i])
        for i, (src, dst) in enumerate(((owner_hbm, owner), (sub_hbm, sub), (prio_hbm, prio)))
    ]
    for copy in [whole] + copies + small:
        copy.start()
    whole.wait()
    projected = None
    for i, copy in enumerate(copies):
        copy.wait()
        part = slice(i * span, (i + 1) * span)
        term = jnp.dot(states[:, part], proj[part, :], preferred_element_type=jnp.float32)
        projected = term if projected is None else projected + term
    square_sum = jnp.sum(projected * projected, axis=1, keepdims=True)
    embedding = projected * lax.rsqrt(square_sum + 1e-06)
    for copy in small:
        copy.wait()
    rank = prio[...]
    high = lax.shift_right_logical(rank, 8)
    fields = (owner[...] + 1, sub[...], high, rank - high * RADIX)
    notes = [f.astype(jnp.float32) for f in fields]
    notes.append(jnp.zeros((NOTE_ROWS - len(fields), rows), jnp.float32))
    tiles = [embedding[:, i:i + rows] for i in range(0, width, rows)]
    block = jnp.concatenate(tiles + notes, axis=0).astype(jnp.bfloat16)
    block_ref[...] = block
    tall_ref[:block.shape[0], :] = block
    tall_ref[block.shape[0]:, :] = block[:tall_ref.shape[0] - block.shape[0]]


def embed(states, projection, owner, sub, prio):
    rows, depth = states.shape
    width = projection.shape[1]
    high = rows * (width // rows) + NOTE_ROWS
    return pl.pallas_call(
        embed_kernel,
        in_specs=[HBM] * 5,
        out_specs=[VMEM] * 2,
        out_shape=[jax.ShapeDtypeStruct((tall, rows), jnp.bfloat16) for tall in (high, high + MORE_ROWS)],
        scratch_shapes=[
            pltpu.VMEM((rows, depth), jnp.bfloat16),
            pltpu.VMEM((depth, width), jnp.bfloat16),
            pltpu.VMEM((1, rows), jnp.int32),
            pltpu.VMEM((1, rows), jnp.int32),
            pltpu.VMEM((1, rows), jnp.int32),
            pltpu.SemaphoreType.DMA((CHUNKS + 1,)),
            pltpu.SemaphoreType.DMA((3,)),
        ],
        compiler_params=pltpu.CompilerParams(vmem_limit_bytes=40 << 20),
        name="embed",
    )(*(pltpu.with_memory_space_constraint(x, pltpu.HBM) for x in (states, projection, owner, sub, prio)))


def read_notes(ref):
    first = ref.shape[0] // ref.shape[1] * ref.shape[1]
    tail = ref[first:first + NOTE_ROWS, :].astype(jnp.float32)
    owner, sub, high, low = (tail[i:i + 1] for i in range(4))
    return (owner - 1.0) * 4.0 + sub, high * float(RADIX) + low


def read_rows(refs):
    rows = refs[0].shape[1]
    return jnp.concatenate(
        [
            jnp.concatenate([ref[i * rows:(i + 1) * rows, :] for ref in refs], axis=0)
            for i in range(refs[0].shape[0] // rows)
        ],
        axis=1,
    )


def score_kernel(row_count, lane_count, products, parts, has_lines, has_state, hand_on, hold, *refs):
    refs = list(refs)
    row_refs = [refs.pop(0) for _ in range(row_count)]
    lane_refs = [refs.pop(0) for _ in range(lane_count)]
    seen_lines = refs.pop(0) if has_lines else None
    seen_table, seen_columns = (refs.pop(0), refs.pop(0)) if has_state else (None, None)
    lines_out = refs.pop(0)
    rows = lines_out.shape[1]
    if hold:
        refs[-1][...] = row_refs[0][...]
    lane_notes = [read_notes(ref) for ref in lane_refs]
    if has_state:
        columns = seen_columns[...]
    else:
        fill = jnp.zeros((-2 * row_count % 8, rows), jnp.float32)
        lines = [line for ref in row_refs for line in read_notes(ref)]
        columns = jnp.concatenate(lines + ([fill] if fill.size else []), axis=0).T
    best, back = [None] * lane_count, [None] * row_count

    def top(old, new):
        return new if old is None else jnp.maximum(old, new)

    for row_set, lane_set in products:
        cosine = lax.dot_general(
            read_rows([row_refs[i] for i in row_set]),
            read_rows([lane_refs[j] for j in lane_set]),
            (((1,), (1,)), ((), ())),
            preferred_element_type=jnp.float32,
        )
        for m, i in enumerate(row_set):
            row_cluster, row_prio = columns[:, 2 * i:2 * i + 1], columns[:, 2 * i + 1:2 * i + 2]
            for n, j in enumerate(lane_set):
                lane_cluster, lane_prio = lane_notes[j]
                here = cosine[m * rows:(m + 1) * rows, n * rows:(n + 1) * rows]
                same = jnp.where(row_cluster == lane_cluster, here, -1.0)
                earlier = row_prio < lane_prio
                best[j] = top(best[j], jnp.where(earlier, same, -1.0))
                if j > 0:
                    back[i] = top(back[i], jnp.where(earlier, -1.0, same))
    lane_ids = lax.broadcasted_iota(jnp.int32, (rows, rows), 1)
    table = jnp.full((rows, rows), -1.0, jnp.float32)
    for i, each in enumerate(back):
        if each is not None:
            table = jnp.where(lane_ids == i, jnp.max(each, axis=1, keepdims=True), table)
    if has_state:
        table = jnp.maximum(table, seen_table[...])
    if hand_on:
        refs.pop(0)[...] = table
        refs.pop(0)[...] = columns
    elif parts:
        table = table.T
        for first, stop in parts:
            refs.pop(0)[...] = table[first:stop]
    lines = jnp.concatenate([jnp.max(b, axis=0, keepdims=True) for b in best], axis=0)
    if has_lines:
        count = seen_lines.shape[0]
        first = jnp.maximum(lines[:count], seen_lines[...])
        lines = first if count == lane_count else jnp.concatenate([first, lines[count:]], axis=0)
    lines_out[...] = lines


def score(name, row_blocks, lane_blocks, products, parts, lines=None, state=None, hand_on=False, hold=False):
    high, rows = row_blocks[0].shape
    width = high - NOTE_ROWS
    inputs = [*row_blocks, *lane_blocks, *([] if lines is None else [lines]), *(state or ())]
    shapes = [(len(lane_blocks), rows)] + [(stop - first, rows) for first, stop in parts]
    if hand_on:
        shapes += [(rows, rows), (rows, -(-2 * len(row_blocks) // 8) * 8)]
    outs = [jax.ShapeDtypeStruct(shape, jnp.float32) for shape in shapes]
    if hold:
        outs.append(jax.ShapeDtypeStruct((high, rows), row_blocks[0].dtype))
    counts = len(row_blocks), len(lane_blocks)
    rest = products, parts, lines is not None, state is not None, hand_on, hold
    macs = sum(len(r) * len(c) for r, c in products) * rows * rows * width
    return pl.pallas_call(
        lambda *refs: score_kernel(*counts, *rest, *refs),
        in_specs=[VMEM] * len(inputs),
        out_specs=[VMEM] * len(outs),
        out_shape=outs,
        compiler_params=pltpu.CompilerParams(vmem_limit_bytes=48 << 20),
        cost_estimate=pl.CostEstimate(
            flops=2 * macs, bytes_accessed=2 * sum(counts) * rows * width, transcendentals=0
        ),
        name=name,
    )(*inputs)


def tournament(line):
    moves = [[(i, (i + s) % line) for i in range(line)] for s in range(1, (line + 1) // 2)]
    if line % 2 == 0:
        half = line // 2
        pairs = [(i, i + half) if i % 2 else (i + half, i) for i in range(half)]
        sent, met = {a for a, _ in pairs}, {b for _, b in pairs}
        idle = [i for i in range(line) if i not in sent]
        free = [i for i in range(line) if i not in met]
        moves.append(pairs + list(zip(idle, free)))
    return moves


def on_device(states, projection, owner_group, cluster_sub, priority):
    line, grp = lax.axis_size("line"), lax.axis_size("grp")
    plane = lax.axis_size("mid") * grp
    rows = states.shape[0]

    def move(array, pairs):
        whole = [(a * plane + p, b * plane + p) for a, b in pairs for p in range(plane)]
        return lax.ppermute(array, AXES, whole)

    def swap(array, step):
        pairs = [(i, i // plane * plane + (i % plane ^ step)) for i in range(line * plane)]
        return lax.ppermute(array, AXES, pairs)

    block, tall = embed(
        states,
        projection,
        owner_group.reshape(1, rows),
        cluster_sub.reshape(1, rows),
        priority.reshape(1, rows),
    )
    moves = tournament(line)
    visitors = [move(tall, moves[0])] + [move(block, pairs) for pairs in moves[1:]]
    bits = [1 << i for i in range(1, plane.bit_length() - 1)]
    found = {0: block}
    for bit in reversed(bits):
        found |= {step | bit: swap(here, bit) for step, here in found.items()}
    row_blocks = [found[step] for step in sorted(found)]

    lanes = [block] + visitors
    every, count = tuple(range(len(lanes))), len(row_blocks)
    half = count // 2
    soon = (0, half)
    rest = tuple(i for i in range(count) if i not in soon)
    lines, held = score(
        "score_soon", [row_blocks[i] for i in soon], lanes[:1], [((0, 1), (0,))], [], hold=True
    )
    row_blocks[0] = lanes[0] = held
    products = [(rest, every), (soon, every[1:])]
    lines, *state = score("score_late", row_blocks, lanes, products, [], lines, hand_on=True)
    partner = [held]
    partner += [lax.optimization_barrier((visitor, held))[0] for visitor in visitors[:-1]]
    partner += [lax.optimization_barrier((visitors[-1], row_blocks[1]))[0]]
    partner = [swap(lane, 1) for lane in partner]
    products, parts = [(tuple(range(count)), every)], [(0, half), (half, count)]
    theirs, near, far = score("score_partner", row_blocks, partner, products, parts, state=state)
    lines = jnp.maximum(lines, swap(theirs, 1))
    for bit in bits[:0:-1]:
        near = jnp.maximum(near, swap(far, bit))
        half = near.shape[0] // 2
        near, far = near[:half], near[half:]
    total = lines[:1]
    for i, pairs in reversed(list(enumerate(moves))):
        total = jnp.maximum(total, move(lines[i + 1:i + 2], [(b, a) for a, b in pairs]))
    total = lax.optimization_barrier(total)
    total = jnp.maximum(jnp.maximum(total, near), swap(far, bits[0]))
    return total.reshape(rows)


def solution(mesh):
    num_dp, num_grp = mesh.shape["dp"], mesh.shape["grp"]
    line = min(num_dp, 1 << (int(math.log2(num_dp * num_grp)) // 2))
    split = Mesh(mesh.devices.reshape(line, num_dp // line, num_grp), AXES)
    in_specs = (P(AXES, None), P(), P(AXES, None), P(AXES), P(AXES))
    return jax.shard_map(
        on_device, mesh=split, in_specs=in_specs, out_specs=P(AXES), check_vma=False
    )
```

```python
import math

import jax
import jax.numpy as jnp
from jax import lax
from jax.experimental import pallas as pl
from jax.experimental.pallas import tpu as pltpu
from jax.sharding import Mesh, PartitionSpec as P

AXES = ("line", "mid", "grp")
NOTE_ROWS = 16
MORE_ROWS = 48
RADIX = 256
CHUNKS = 4
VMEM = pl.BlockSpec(memory_space=pltpu.VMEM)
HBM = pl.BlockSpec(memory_space=pltpu.HBM)


def embed_kernel(
    states_hbm, proj_hbm, owner_hbm, sub_hbm, prio_hbm, block_ref, tall_ref,
    states, proj, owner, sub, prio, big_sem, small_sem,
):
    rows, depth = states.shape
    width = proj.shape[1]
    span = depth // CHUNKS
    whole = pltpu.make_async_copy(states_hbm, states, big_sem.at[CHUNKS])
    copies = [
        pltpu.make_async_copy(
            proj_hbm.at[pl.ds(i * span, span)], proj.at[pl.ds(i * span, span)], big_sem.at[i]
        )
        for i in range(CHUNKS)
    ]
    small = [
        pltpu.make_async_copy(src, dst, small_sem.at[i])
        for i, (src, dst) in enumerate(((owner_hbm, owner), (sub_hbm, sub), (prio_hbm, prio)))
    ]
    for copy in [whole] + copies + small:
        copy.start()
    whole.wait()
    projected = None
    for i, copy in enumerate(copies):
        copy.wait()
        part = slice(i * span, (i + 1) * span)
        term = jnp.dot(states[:, part], proj[part, :], preferred_element_type=jnp.float32)
        projected = term if projected is None else projected + term
    square_sum = jnp.sum(projected * projected, axis=1, keepdims=True)
    embedding = projected * lax.rsqrt(square_sum + 1e-06)
    for copy in small:
        copy.wait()
    rank = prio[...]
    high = lax.shift_right_logical(rank, 8)
    fields = (owner[...] + 1, sub[...], high, rank - high * RADIX)
    notes = [f.astype(jnp.float32) for f in fields]
    notes.append(jnp.zeros((NOTE_ROWS - len(fields), rows), jnp.float32))
    tiles = [embedding[:, i:i + rows] for i in range(0, width, rows)]
    block = jnp.concatenate(tiles + notes, axis=0).astype(jnp.bfloat16)
    block_ref[...] = block
    tall_ref[:block.shape[0], :] = block
    tall_ref[block.shape[0]:, :] = block[:tall_ref.shape[0] - block.shape[0]]


def embed(states, projection, owner, sub, prio):
    rows, depth = states.shape
    width = projection.shape[1]
    high = rows * (width // rows) + NOTE_ROWS
    return pl.pallas_call(
        embed_kernel,
        in_specs=[HBM] * 5,
        out_specs=[VMEM] * 2,
        out_shape=[jax.ShapeDtypeStruct((tall, rows), jnp.bfloat16) for tall in (high, high + MORE_ROWS)],
        scratch_shapes=[
            pltpu.VMEM((rows, depth), jnp.bfloat16),
            pltpu.VMEM((depth, width), jnp.bfloat16),
            pltpu.VMEM((1, rows), jnp.int32),
            pltpu.VMEM((1, rows), jnp.int32),
            pltpu.VMEM((1, rows), jnp.int32),
            pltpu.SemaphoreType.DMA((CHUNKS + 1,)),
            pltpu.SemaphoreType.DMA((3,)),
        ],
        compiler_params=pltpu.CompilerParams(vmem_limit_bytes=40 << 20),
        name="embed",
    )(*(pltpu.with_memory_space_constraint(x, pltpu.HBM) for x in (states, projection, owner, sub, prio)))


def read_notes(ref):
    first = ref.shape[0] // ref.shape[1] * ref.shape[1]
    tail = ref[first:first + NOTE_ROWS, :].astype(jnp.float32)
    owner, sub, high, low = (tail[i:i + 1] for i in range(4))
    return (owner - 1.0) * 4.0 + sub, high * float(RADIX) + low


def read_rows(refs):
    rows = refs[0].shape[1]
    return jnp.concatenate(
        [
            jnp.concatenate([ref[i * rows:(i + 1) * rows, :] for ref in refs], axis=0)
            for i in range(refs[0].shape[0] // rows)
        ],
        axis=1,
    )


def score_kernel(row_count, lane_count, products, parts, has_lines, has_state, hand_on, hold, *refs):
    refs = list(refs)
    row_refs = [refs.pop(0) for _ in range(row_count)]
    lane_refs = [refs.pop(0) for _ in range(lane_count)]
    seen_lines = refs.pop(0) if has_lines else None
    seen_table, seen_columns = (refs.pop(0), refs.pop(0)) if has_state else (None, None)
    lines_out = refs.pop(0)
    rows = lines_out.shape[1]
    if hold:
        refs[-1][...] = row_refs[0][...]
    lane_notes = [read_notes(ref) for ref in lane_refs]
    if has_state:
        columns = seen_columns[...]
    else:
        fill = jnp.zeros((-2 * row_count % 8, rows), jnp.float32)
        lines = [line for ref in row_refs for line in read_notes(ref)]
        columns = jnp.concatenate(lines + ([fill] if fill.size else []), axis=0).T
    best, back = [None] * lane_count, [None] * row_count

    def top(old, new):
        return new if old is None else jnp.maximum(old, new)

    for row_set, lane_set in products:
        cosine = lax.dot_general(
            read_rows([row_refs[i] for i in row_set]),
            read_rows([lane_refs[j] for j in lane_set]),
            (((1,), (1,)), ((), ())),
            preferred_element_type=jnp.float32,
        )
        for m, i in enumerate(row_set):
            row_cluster, row_prio = columns[:, 2 * i:2 * i + 1], columns[:, 2 * i + 1:2 * i + 2]
            for n, j in enumerate(lane_set):
                lane_cluster, lane_prio = lane_notes[j]
                here = cosine[m * rows:(m + 1) * rows, n * rows:(n + 1) * rows]
                same = jnp.where(row_cluster == lane_cluster, here, -1.0)
                earlier = row_prio < lane_prio
                best[j] = top(best[j], jnp.where(earlier, same, -1.0))
                if j > 0:
                    back[i] = top(back[i], jnp.where(earlier, -1.0, same))
    lane_ids = lax.broadcasted_iota(jnp.int32, (rows, rows), 1)
    table = jnp.full((rows, rows), -1.0, jnp.float32)
    for i, each in enumerate(back):
        if each is not None:
            table = jnp.where(lane_ids == i, jnp.max(each, axis=1, keepdims=True), table)
    if has_state:
        table = jnp.maximum(table, seen_table[...])
    if hand_on:
        refs.pop(0)[...] = table
        refs.pop(0)[...] = columns
    elif parts:
        table = table.T
        for first, stop in parts:
            refs.pop(0)[...] = table[first:stop]
    lines = jnp.concatenate([jnp.max(b, axis=0, keepdims=True) for b in best], axis=0)
    if has_lines:
        count = seen_lines.shape[0]
        first = jnp.maximum(lines[:count], seen_lines[...])
        lines = first if count == lane_count else jnp.concatenate([first, lines[count:]], axis=0)
    lines_out[...] = lines


def score(name, row_blocks, lane_blocks, products, parts, lines=None, state=None, hand_on=False, hold=False):
    high, rows = row_blocks[0].shape
    width = high - NOTE_ROWS
    inputs = [*row_blocks, *lane_blocks, *([] if lines is None else [lines]), *(state or ())]
    shapes = [(len(lane_blocks), rows)] + [(stop - first, rows) for first, stop in parts]
    if hand_on:
        shapes += [(rows, rows), (rows, -(-2 * len(row_blocks) // 8) * 8)]
    outs = [jax.ShapeDtypeStruct(shape, jnp.float32) for shape in shapes]
    if hold:
        outs.append(jax.ShapeDtypeStruct((high, rows), row_blocks[0].dtype))
    counts = len(row_blocks), len(lane_blocks)
    rest = products, parts, lines is not None, state is not None, hand_on, hold
    macs = sum(len(r) * len(c) for r, c in products) * rows * rows * width
    return pl.pallas_call(
        lambda *refs: score_kernel(*counts, *rest, *refs),
        in_specs=[VMEM] * len(inputs),
        out_specs=[VMEM] * len(outs),
        out_shape=outs,
        compiler_params=pltpu.CompilerParams(vmem_limit_bytes=48 << 20),
        cost_estimate=pl.CostEstimate(
            flops=2 * macs, bytes_accessed=2 * sum(counts) * rows * width, transcendentals=0
        ),
        name=name,
    )(*inputs)


def tournament(line):
    moves = [[(i, (i + s) % line) for i in range(line)] for s in range(1, (line + 1) // 2)]
    if line % 2 == 0:
        half = line // 2
        pairs = [(i, i + half) if i % 2 else (i + half, i) for i in range(half)]
        sent, met = {a for a, _ in pairs}, {b for _, b in pairs}
        idle = [i for i in range(line) if i not in sent]
        free = [i for i in range(line) if i not in met]
        moves.append(pairs + list(zip(idle, free)))
    return moves


def on_device(states, projection, owner_group, cluster_sub, priority):
    line, grp = lax.axis_size("line"), lax.axis_size("grp")
    plane = lax.axis_size("mid") * grp
    rows = states.shape[0]

    def move(array, pairs):
        whole = [(a * plane + p, b * plane + p) for a, b in pairs for p in range(plane)]
        return lax.ppermute(array, AXES, whole)

    def swap(array, step):
        pairs = [(i, i // plane * plane + (i % plane ^ step)) for i in range(line * plane)]
        return lax.ppermute(array, AXES, pairs)

    block, tall = embed(
        states,
        projection,
        owner_group.reshape(1, rows),
        cluster_sub.reshape(1, rows),
        priority.reshape(1, rows),
    )
    moves = tournament(line)
    visitors = [move(tall, moves[0])] + [move(block, pairs) for pairs in moves[1:]]
    bits = [1 << i for i in range(1, plane.bit_length() - 1)]
    found = {0: block}
    for bit in reversed(bits):
        found |= {step | bit: swap(here, bit) for step, here in found.items()}
    row_blocks = [found[step] for step in sorted(found)]

    lanes = [block] + visitors
    every, count = tuple(range(len(lanes))), len(row_blocks)
    half = count // 2
    soon = (0, half)
    rest = tuple(i for i in range(count) if i not in soon)
    lines, held = score(
        "score_soon", [row_blocks[i] for i in soon], lanes[:1], [((0, 1), (0,))], [], hold=True
    )
    row_blocks[0] = lanes[0] = held
    products = [(rest, every), (soon, every[1:])]
    lines, *state = score("score_late", row_blocks, lanes, products, [], lines, hand_on=True)
    partner = [held]
    partner += [lax.optimization_barrier((visitor, held))[0] for visitor in visitors[:-1]]
    partner += [lax.optimization_barrier((visitors[-1], row_blocks[1]))[0]]
    partner = [swap(lane, 1) for lane in partner]
    products, parts = [(tuple(range(count)), every)], [(0, half), (half, count)]
    theirs, near, far = score("score_partner", row_blocks, partner, products, parts, state=state)
    lines = jnp.maximum(lines, swap(theirs, 1))
    for bit in bits[:0:-1]:
        near = jnp.maximum(near, swap(far, bit))
        half = near.shape[0] // 2
        near, far = near[:half], near[half:]
    total = lines[:1]
    for i, pairs in reversed(list(enumerate(moves))):
        total = jnp.maximum(total, move(lines[i + 1:i + 2], [(b, a) for a, b in pairs]))
    total = lax.optimization_barrier(total)
    total = jnp.maximum(jnp.maximum(total, near), swap(far, bits[0]))
    return total.reshape(rows)


def solution(mesh):
    num_dp, num_grp = mesh.shape["dp"], mesh.shape["grp"]
    line = min(num_dp, 1 << (int(math.log2(num_dp * num_grp)) // 2))
    split = Mesh(mesh.devices.reshape(line, num_dp // line, num_grp), AXES)
    in_specs = (P(AXES, None), P(), P(AXES, None), P(AXES), P(AXES))
    return jax.shard_map(
        on_device, mesh=split, in_specs=in_specs, out_specs=P(AXES), check_vma=False
    )
```

```python
import math

import jax
import jax.numpy as jnp
from jax import lax
from jax.experimental import pallas as pl
from jax.experimental.pallas import tpu as pltpu
from jax.sharding import Mesh, PartitionSpec as P

AXES = ("line", "mid", "grp")
NOTE_ROWS = 16
MORE_ROWS = 48
RADIX = 256
CHUNKS = 2
VMEM = pl.BlockSpec(memory_space=pltpu.VMEM)
HBM = pl.BlockSpec(memory_space=pltpu.HBM)


def embed_kernel(
    states_hbm, proj_hbm, owner_hbm, sub_hbm, prio_hbm, block_ref, tall_ref,
    states, proj, owner, sub, prio, big_sem, small_sem,
):
    rows, depth = states.shape
    width = proj.shape[1]
    span = depth // CHUNKS
    whole = pltpu.make_async_copy(states_hbm, states, big_sem.at[CHUNKS])
    copies = [
        pltpu.make_async_copy(
            proj_hbm.at[pl.ds(i * span, span)], proj.at[pl.ds(i * span, span)], big_sem.at[i]
        )
        for i in range(CHUNKS)
    ]
    small = [
        pltpu.make_async_copy(src, dst, small_sem.at[i])
        for i, (src, dst) in enumerate(((owner_hbm, owner), (sub_hbm, sub), (prio_hbm, prio)))
    ]
    for copy in [whole] + copies + small:
        copy.start()
    whole.wait()
    projected = None
    for i, copy in enumerate(copies):
        copy.wait()
        part = slice(i * span, (i + 1) * span)
        term = jnp.dot(states[:, part], proj[part, :], preferred_element_type=jnp.float32)
        projected = term if projected is None else projected + term
    square_sum = jnp.sum(projected * projected, axis=1, keepdims=True)
    embedding = projected * lax.rsqrt(square_sum + 1e-06)
    for copy in small:
        copy.wait()
    rank = prio[...]
    high = lax.shift_right_logical(rank, 8)
    fields = (owner[...] + 1, sub[...], high, rank - high * RADIX)
    notes = [f.astype(jnp.float32) for f in fields]
    notes.append(jnp.zeros((NOTE_ROWS - len(fields), rows), jnp.float32))
    tiles = [embedding[:, i:i + rows] for i in range(0, width, rows)]
    block = jnp.concatenate(tiles + notes, axis=0).astype(jnp.bfloat16)
    block_ref[...] = block
    tall_ref[:block.shape[0], :] = block
    tall_ref[block.shape[0]:, :] = block[:tall_ref.shape[0] - block.shape[0]]


def embed(states, projection, owner, sub, prio):
    rows, depth = states.shape
    width = projection.shape[1]
    high = rows * (width // rows) + NOTE_ROWS
    return pl.pallas_call(
        embed_kernel,
        in_specs=[HBM] * 5,
        out_specs=[VMEM] * 2,
        out_shape=[jax.ShapeDtypeStruct((tall, rows), jnp.bfloat16) for tall in (high, high + MORE_ROWS)],
        scratch_shapes=[
            pltpu.VMEM((rows, depth), jnp.bfloat16),
            pltpu.VMEM((depth, width), jnp.bfloat16),
            pltpu.VMEM((1, rows), jnp.int32),
            pltpu.VMEM((1, rows), jnp.int32),
            pltpu.VMEM((1, rows), jnp.int32),
            pltpu.SemaphoreType.DMA((CHUNKS + 1,)),
            pltpu.SemaphoreType.DMA((3,)),
        ],
        compiler_params=pltpu.CompilerParams(vmem_limit_bytes=40 << 20),
        name="embed",
    )(*(pltpu.with_memory_space_constraint(x, pltpu.HBM) for x in (states, projection, owner, sub, prio)))


def read_notes(ref):
    first = ref.shape[0] // ref.shape[1] * ref.shape[1]
    tail = ref[first:first + NOTE_ROWS, :].astype(jnp.float32)
    owner, sub, high, low = (tail[i:i + 1] for i in range(4))
    return (owner - 1.0) * 4.0 + sub, high * float(RADIX) + low


def read_rows(refs):
    rows = refs[0].shape[1]
    return jnp.concatenate(
        [
            jnp.concatenate([ref[i * rows:(i + 1) * rows, :] for ref in refs], axis=0)
            for i in range(refs[0].shape[0] // rows)
        ],
        axis=1,
    )


def score_kernel(row_count, lane_count, products, parts, has_lines, has_state, hand_on, hold, *refs):
    refs = list(refs)
    row_refs = [refs.pop(0) for _ in range(row_count)]
    lane_refs = [refs.pop(0) for _ in range(lane_count)]
    seen_lines = refs.pop(0) if has_lines else None
    seen_table, seen_columns = (refs.pop(0), refs.pop(0)) if has_state else (None, None)
    lines_out = refs.pop(0)
    rows = lines_out.shape[1]
    if hold:
        refs[-1][...] = row_refs[0][...]
    lane_notes = [read_notes(ref) for ref in lane_refs]
    if has_state:
        columns = seen_columns[...]
    else:
        fill = jnp.zeros((-2 * row_count % 8, rows), jnp.float32)
        lines = [line for ref in row_refs for line in read_notes(ref)]
        columns = jnp.concatenate(lines + ([fill] if fill.size else []), axis=0).T
    best, back = [None] * lane_count, [None] * row_count

    def top(old, new):
        return new if old is None else jnp.maximum(old, new)

    for row_set, lane_set in products:
        cosine = lax.dot_general(
            read_rows([row_refs[i] for i in row_set]),
            read_rows([lane_refs[j] for j in lane_set]),
            (((1,), (1,)), ((), ())),
            preferred_element_type=jnp.float32,
        )
        for m, i in enumerate(row_set):
            row_cluster, row_prio = columns[:, 2 * i:2 * i + 1], columns[:, 2 * i + 1:2 * i + 2]
            for n, j in enumerate(lane_set):
                lane_cluster, lane_prio = lane_notes[j]
                here = cosine[m * rows:(m + 1) * rows, n * rows:(n + 1) * rows]
                same = jnp.where(row_cluster == lane_cluster, here, -1.0)
                earlier = row_prio < lane_prio
                best[j] = top(best[j], jnp.where(earlier, same, -1.0))
                if j > 0:
                    back[i] = top(back[i], jnp.where(earlier, -1.0, same))
    lane_ids = lax.broadcasted_iota(jnp.int32, (rows, rows), 1)
    table = jnp.full((rows, rows), -1.0, jnp.float32)
    for i, each in enumerate(back):
        if each is not None:
            table = jnp.where(lane_ids == i, jnp.max(each, axis=1, keepdims=True), table)
    if has_state:
        table = jnp.maximum(table, seen_table[...])
    if hand_on:
        refs.pop(0)[...] = table
        refs.pop(0)[...] = columns
    elif parts:
        table = table.T
        for first, stop in parts:
            refs.pop(0)[...] = table[first:stop]
    lines = jnp.concatenate([jnp.max(b, axis=0, keepdims=True) for b in best], axis=0)
    if has_lines:
        count = seen_lines.shape[0]
        first = jnp.maximum(lines[:count], seen_lines[...])
        lines = first if count == lane_count else jnp.concatenate([first, lines[count:]], axis=0)
    lines_out[...] = lines


def score(name, row_blocks, lane_blocks, products, parts, lines=None, state=None, hand_on=False, hold=False):
    high, rows = row_blocks[0].shape
    width = high - NOTE_ROWS
    inputs = [*row_blocks, *lane_blocks, *([] if lines is None else [lines]), *(state or ())]
    shapes = [(len(lane_blocks), rows)] + [(stop - first, rows) for first, stop in parts]
    if hand_on:
        shapes += [(rows, rows), (rows, -(-2 * len(row_blocks) // 8) * 8)]
    outs = [jax.ShapeDtypeStruct(shape, jnp.float32) for shape in shapes]
    if hold:
        outs.append(jax.ShapeDtypeStruct((high, rows), row_blocks[0].dtype))
    counts = len(row_blocks), len(lane_blocks)
    rest = products, parts, lines is not None, state is not None, hand_on, hold
    macs = sum(len(r) * len(c) for r, c in products) * rows * rows * width
    return pl.pallas_call(
        lambda *refs: score_kernel(*counts, *rest, *refs),
        in_specs=[VMEM] * len(inputs),
        out_specs=[VMEM] * len(outs),
        out_shape=outs,
        compiler_params=pltpu.CompilerParams(vmem_limit_bytes=48 << 20),
        cost_estimate=pl.CostEstimate(
            flops=2 * macs, bytes_accessed=2 * sum(counts) * rows * width, transcendentals=0
        ),
        name=name,
    )(*inputs)


def tournament(line):
    moves = [[(i, (i + s) % line) for i in range(line)] for s in range(1, (line + 1) // 2)]
    if line % 2 == 0:
        half = line // 2
        pairs = [(i, i + half) if i % 2 else (i + half, i) for i in range(half)]
        sent, met = {a for a, _ in pairs}, {b for _, b in pairs}
        idle = [i for i in range(line) if i not in sent]
        free = [i for i in range(line) if i not in met]
        moves.append(pairs + list(zip(idle, free)))
    return moves


def on_device(states, projection, owner_group, cluster_sub, priority):
    line, grp = lax.axis_size("line"), lax.axis_size("grp")
    plane = lax.axis_size("mid") * grp
    rows = states.shape[0]

    def move(array, pairs):
        whole = [(a * plane + p, b * plane + p) for a, b in pairs for p in range(plane)]
        return lax.ppermute(array, AXES, whole)

    def swap(array, step):
        pairs = [(i, i // plane * plane + (i % plane ^ step)) for i in range(line * plane)]
        return lax.ppermute(array, AXES, pairs)

    block, tall = embed(
        states,
        projection,
        owner_group.reshape(1, rows),
        cluster_sub.reshape(1, rows),
        priority.reshape(1, rows),
    )
    moves = tournament(line)
    visitors = [move(tall, moves[0])] + [move(block, pairs) for pairs in moves[1:]]
    bits = [1 << i for i in range(1, plane.bit_length() - 1)]
    found = {0: block}
    for bit in reversed(bits):
        found |= {step | bit: swap(here, bit) for step, here in found.items()}
    row_blocks = [found[step] for step in sorted(found)]

    lanes = [block] + visitors
    every, count = tuple(range(len(lanes))), len(row_blocks)
    half = count // 2
    soon = (0, half)
    lines, held = score(
        "score_soon", [row_blocks[i] for i in soon], lanes[:1], [((0, 1), (0,))], [], hold=True
    )
    row_blocks[0] = lanes[0] = held
    products = [(tuple(range(count)), every)]
    lines, *state = score("score_late", row_blocks, lanes, products, [], lines, hand_on=True)
    partner = [held]
    partner += [lax.optimization_barrier((visitor, held))[0] for visitor in visitors[:-1]]
    partner += [lax.optimization_barrier((visitors[-1], row_blocks[1]))[0]]
    partner = [swap(lane, 1) for lane in partner]
    products, parts = [(tuple(range(count)), every)], [(0, half), (half, count)]
    theirs, near, far = score("score_partner", row_blocks, partner, products, parts, state=state)
    lines = jnp.maximum(lines, swap(theirs, 1))
    for bit in bits[:0:-1]:
        near = jnp.maximum(near, swap(far, bit))
        half = near.shape[0] // 2
        near, far = near[:half], near[half:]
    total = lines[:1]
    for i, pairs in reversed(list(enumerate(moves))):
        total = jnp.maximum(total, move(lines[i + 1:i + 2], [(b, a) for a, b in pairs]))
    total = lax.optimization_barrier(total)
    total = jnp.maximum(jnp.maximum(total, near), swap(far, bits[0]))
    return total.reshape(rows)


def solution(mesh):
    num_dp, num_grp = mesh.shape["dp"], mesh.shape["grp"]
    line = min(num_dp, 1 << (int(math.log2(num_dp * num_grp)) // 2))
    split = Mesh(mesh.devices.reshape(line, num_dp // line, num_grp), AXES)
    in_specs = (P(AXES, None), P(), P(AXES, None), P(AXES), P(AXES))
    return jax.shard_map(
        on_device, mesh=split, in_specs=in_specs, out_specs=P(AXES), check_vma=False
    )
```

```python
import math

import jax
import jax.numpy as jnp
from jax import lax
from jax.experimental import pallas as pl
from jax.experimental.pallas import tpu as pltpu
from jax.sharding import Mesh, PartitionSpec as P

AXES = ("line", "mid", "grp")
NOTE_ROWS = 16
MORE_ROWS = 48
RADIX = 256
CHUNKS = 8
VMEM = pl.BlockSpec(memory_space=pltpu.VMEM)
HBM = pl.BlockSpec(memory_space=pltpu.HBM)


def embed_kernel(
    states_hbm, proj_hbm, owner_hbm, sub_hbm, prio_hbm, block_ref, tall_ref,
    states, proj, owner, sub, prio, big_sem, small_sem,
):
    rows, depth = states.shape
    width = proj.shape[1]
    span = depth // CHUNKS
    whole = pltpu.make_async_copy(states_hbm, states, big_sem.at[CHUNKS])
    copies = [
        pltpu.make_async_copy(
            proj_hbm.at[pl.ds(i * span, span)], proj.at[pl.ds(i * span, span)], big_sem.at[i]
        )
        for i in range(CHUNKS)
    ]
    small = [
        pltpu.make_async_copy(src, dst, small_sem.at[i])
        for i, (src, dst) in enumerate(((owner_hbm, owner), (sub_hbm, sub), (prio_hbm, prio)))
    ]
    for copy in [whole] + copies + small:
        copy.start()
    whole.wait()
    projected = None
    for i, copy in enumerate(copies):
        copy.wait()
        part = slice(i * span, (i + 1) * span)
        term = jnp.dot(states[:, part], proj[part, :], preferred_element_type=jnp.float32)
        projected = term if projected is None else projected + term
    square_sum = jnp.sum(projected * projected, axis=1, keepdims=True)
    embedding = projected * lax.rsqrt(square_sum + 1e-06)
    for copy in small:
        copy.wait()
    rank = prio[...]
    high = lax.shift_right_logical(rank, 8)
    fields = (owner[...] + 1, sub[...], high, rank - high * RADIX)
    notes = [f.astype(jnp.float32) for f in fields]
    notes.append(jnp.zeros((NOTE_ROWS - len(fields), rows), jnp.float32))
    tiles = [embedding[:, i:i + rows] for i in range(0, width, rows)]
    block = jnp.concatenate(tiles + notes, axis=0).astype(jnp.bfloat16)
    block_ref[...] = block
    tall_ref[:block.shape[0], :] = block
    tall_ref[block.shape[0]:, :] = block[:tall_ref.shape[0] - block.shape[0]]


def embed(states, projection, owner, sub, prio):
    rows, depth = states.shape
    width = projection.shape[1]
    high = rows * (width // rows) + NOTE_ROWS
    return pl.pallas_call(
        embed_kernel,
        in_specs=[HBM] * 5,
        out_specs=[VMEM] * 2,
        out_shape=[jax.ShapeDtypeStruct((tall, rows), jnp.bfloat16) for tall in (high, high + MORE_ROWS)],
        scratch_shapes=[
            pltpu.VMEM((rows, depth), jnp.bfloat16),
            pltpu.VMEM((depth, width), jnp.bfloat16),
            pltpu.VMEM((1, rows), jnp.int32),
            pltpu.VMEM((1, rows), jnp.int32),
            pltpu.VMEM((1, rows), jnp.int32),
            pltpu.SemaphoreType.DMA((CHUNKS + 1,)),
            pltpu.SemaphoreType.DMA((3,)),
        ],
        compiler_params=pltpu.CompilerParams(vmem_limit_bytes=40 << 20),
        name="embed",
    )(*(pltpu.with_memory_space_constraint(x, pltpu.HBM) for x in (states, projection, owner, sub, prio)))


def read_notes(ref):
    first = ref.shape[0] // ref.shape[1] * ref.shape[1]
    tail = ref[first:first + NOTE_ROWS, :].astype(jnp.float32)
    owner, sub, high, low = (tail[i:i + 1] for i in range(4))
    return (owner - 1.0) * 4.0 + sub, high * float(RADIX) + low


def read_rows(refs):
    rows = refs[0].shape[1]
    return jnp.concatenate(
        [
            jnp.concatenate([ref[i * rows:(i + 1) * rows, :] for ref in refs], axis=0)
            for i in range(refs[0].shape[0] // rows)
        ],
        axis=1,
    )


def score_kernel(row_count, lane_count, products, parts, has_lines, has_state, hand_on, hold, *refs):
    refs = list(refs)
    row_refs = [refs.pop(0) for _ in range(row_count)]
    lane_refs = [refs.pop(0) for _ in range(lane_count)]
    seen_lines = refs.pop(0) if has_lines else None
    seen_table, seen_columns = (refs.pop(0), refs.pop(0)) if has_state else (None, None)
    lines_out = refs.pop(0)
    rows = lines_out.shape[1]
    if hold:
        refs[-1][...] = row_refs[0][...]
    lane_notes = [read_notes(ref) for ref in lane_refs]
    if has_state:
        columns = seen_columns[...]
    else:
        fill = jnp.zeros((-2 * row_count % 8, rows), jnp.float32)
        lines = [line for ref in row_refs for line in read_notes(ref)]
        columns = jnp.concatenate(lines + ([fill] if fill.size else []), axis=0).T
    best, back = [None] * lane_count, [None] * row_count

    def top(old, new):
        return new if old is None else jnp.maximum(old, new)

    for row_set, lane_set in products:
        cosine = lax.dot_general(
            read_rows([row_refs[i] for i in row_set]),
            read_rows([lane_refs[j] for j in lane_set]),
            (((1,), (1,)), ((), ())),
            preferred_element_type=jnp.float32,
        )
        for m, i in enumerate(row_set):
            row_cluster, row_prio = columns[:, 2 * i:2 * i + 1], columns[:, 2 * i + 1:2 * i + 2]
            for n, j in enumerate(lane_set):
                lane_cluster, lane_prio = lane_notes[j]
                here = cosine[m * rows:(m + 1) * rows, n * rows:(n + 1) * rows]
                same = jnp.where(row_cluster == lane_cluster, here, -1.0)
                earlier = row_prio < lane_prio
                best[j] = top(best[j], jnp.where(earlier, same, -1.0))
                if j > 0:
                    back[i] = top(back[i], jnp.where(earlier, -1.0, same))
    lane_ids = lax.broadcasted_iota(jnp.int32, (rows, rows), 1)
    table = jnp.full((rows, rows), -1.0, jnp.float32)
    for i, each in enumerate(back):
        if each is not None:
            table = jnp.where(lane_ids == i, jnp.max(each, axis=1, keepdims=True), table)
    if has_state:
        table = jnp.maximum(table, seen_table[...])
    if hand_on:
        refs.pop(0)[...] = table
        refs.pop(0)[...] = columns
    elif parts:
        table = table.T
        for first, stop in parts:
            refs.pop(0)[...] = table[first:stop]
    lines = jnp.concatenate([jnp.max(b, axis=0, keepdims=True) for b in best], axis=0)
    if has_lines:
        count = seen_lines.shape[0]
        first = jnp.maximum(lines[:count], seen_lines[...])
        lines = first if count == lane_count else jnp.concatenate([first, lines[count:]], axis=0)
    lines_out[...] = lines


def score(name, row_blocks, lane_blocks, products, parts, lines=None, state=None, hand_on=False, hold=False):
    high, rows = row_blocks[0].shape
    width = high - NOTE_ROWS
    inputs = [*row_blocks, *lane_blocks, *([] if lines is None else [lines]), *(state or ())]
    shapes = [(len(lane_blocks), rows)] + [(stop - first, rows) for first, stop in parts]
    if hand_on:
        shapes += [(rows, rows), (rows, -(-2 * len(row_blocks) // 8) * 8)]
    outs = [jax.ShapeDtypeStruct(shape, jnp.float32) for shape in shapes]
    if hold:
        outs.append(jax.ShapeDtypeStruct((high, rows), row_blocks[0].dtype))
    counts = len(row_blocks), len(lane_blocks)
    rest = products, parts, lines is not None, state is not None, hand_on, hold
    macs = sum(len(r) * len(c) for r, c in products) * rows * rows * width
    return pl.pallas_call(
        lambda *refs: score_kernel(*counts, *rest, *refs),
        in_specs=[VMEM] * len(inputs),
        out_specs=[VMEM] * len(outs),
        out_shape=outs,
        compiler_params=pltpu.CompilerParams(vmem_limit_bytes=48 << 20),
        cost_estimate=pl.CostEstimate(
            flops=2 * macs, bytes_accessed=2 * sum(counts) * rows * width, transcendentals=0
        ),
        name=name,
    )(*inputs)


def tournament(line):
    moves = [[(i, (i + s) % line) for i in range(line)] for s in range(1, (line + 1) // 2)]
    if line % 2 == 0:
        half = line // 2
        pairs = [(i, i + half) if i % 2 else (i + half, i) for i in range(half)]
        sent, met = {a for a, _ in pairs}, {b for _, b in pairs}
        idle = [i for i in range(line) if i not in sent]
        free = [i for i in range(line) if i not in met]
        moves.append(pairs + list(zip(idle, free)))
    return moves


def on_device(states, projection, owner_group, cluster_sub, priority):
    line, grp = lax.axis_size("line"), lax.axis_size("grp")
    plane = lax.axis_size("mid") * grp
    rows = states.shape[0]

    def move(array, pairs):
        whole = [(a * plane + p, b * plane + p) for a, b in pairs for p in range(plane)]
        return lax.ppermute(array, AXES, whole)

    def swap(array, step):
        pairs = [(i, i // plane * plane + (i % plane ^ step)) for i in range(line * plane)]
        return lax.ppermute(array, AXES, pairs)

    block, tall = embed(
        states,
        projection,
        owner_group.reshape(1, rows),
        cluster_sub.reshape(1, rows),
        priority.reshape(1, rows),
    )
    moves = tournament(line)
    visitors = [move(tall, moves[0])] + [move(block, pairs) for pairs in moves[1:]]
    bits = [1 << i for i in range(1, plane.bit_length() - 1)]
    found = {0: block}
    for bit in reversed(bits):
        found |= {step | bit: swap(here, bit) for step, here in found.items()}
    row_blocks = [found[step] for step in sorted(found)]

    lanes = [block] + visitors
    every, count = tuple(range(len(lanes))), len(row_blocks)
    half = count // 2
    soon = (0, half)
    rest = tuple(i for i in range(count) if i not in soon)
    lines, held = score(
        "score_soon", [row_blocks[i] for i in soon], lanes[:1], [((0, 1), (0,))], [], hold=True
    )
    row_blocks[0] = lanes[0] = held
    products = [(rest, every), (soon, every[1:])]
    lines, *state = score("score_late", row_blocks, lanes, products, [], lines, hand_on=True)
    partner = [held]
    partner += [lax.optimization_barrier((visitor, held))[0] for visitor in visitors[:-1]]
    partner += [lax.optimization_barrier((visitors[-1], row_blocks[1]))[0]]
    partner = [swap(lane, 1) for lane in partner]
    products, parts = [(tuple(range(count)), every)], [(0, half), (half, count)]
    theirs, near, far = score("score_partner", row_blocks, partner, products, parts, state=state)
    lines = jnp.maximum(lines, swap(theirs, 1))
    for bit in bits[:0:-1]:
        near = jnp.maximum(near, swap(far, bit))
        half = near.shape[0] // 2
        near, far = near[:half], near[half:]
    total = lines[:1]
    for i, pairs in reversed(list(enumerate(moves))):
        total = jnp.maximum(total, move(lines[i + 1:i + 2], [(b, a) for a, b in pairs]))
    total = lax.optimization_barrier(total)
    total = jnp.maximum(jnp.maximum(total, near), swap(far, bits[0]))
    return total.reshape(rows)


def solution(mesh):
    num_dp, num_grp = mesh.shape["dp"], mesh.shape["grp"]
    line = min(num_dp, 1 << (int(math.log2(num_dp * num_grp)) // 2))
    split = Mesh(mesh.devices.reshape(line, num_dp // line, num_grp), AXES)
    in_specs = (P(AXES, None), P(), P(AXES, None), P(AXES), P(AXES))
    return jax.shard_map(
        on_device, mesh=split, in_specs=in_specs, out_specs=P(AXES), check_vma=False
    )
```

```python
import math

import jax
import jax.numpy as jnp
from jax import lax
from jax.experimental import pallas as pl
from jax.experimental.pallas import tpu as pltpu
from jax.sharding import Mesh, PartitionSpec as P

AXES = ("line", "mid", "grp")
NOTE_ROWS = 16
MORE_ROWS = 48
RADIX = 256
CHUNKS = 4
VMEM = pl.BlockSpec(memory_space=pltpu.VMEM)
HBM = pl.BlockSpec(memory_space=pltpu.HBM)


def embed_kernel(
    states_hbm, proj_hbm, owner_hbm, sub_hbm, prio_hbm, block_ref, tall_ref,
    states, proj, owner, sub, prio, big_sem, small_sem,
):
    rows, depth = states.shape
    width = proj.shape[1]
    span = depth // CHUNKS
    whole = pltpu.make_async_copy(states_hbm, states, big_sem.at[CHUNKS])
    copies = [
        pltpu.make_async_copy(
            proj_hbm.at[pl.ds(i * span, span)], proj.at[pl.ds(i * span, span)], big_sem.at[i]
        )
        for i in range(CHUNKS)
    ]
    small = [
        pltpu.make_async_copy(src, dst, small_sem.at[i])
        for i, (src, dst) in enumerate(((owner_hbm, owner), (sub_hbm, sub), (prio_hbm, prio)))
    ]
    for copy in small + [whole] + copies:
        copy.start()
    whole.wait()
    projected = None
    for i, copy in enumerate(copies):
        copy.wait()
        part = slice(i * span, (i + 1) * span)
        term = jnp.dot(states[:, part], proj[part, :], preferred_element_type=jnp.float32)
        projected = term if projected is None else projected + term
    square_sum = jnp.sum(projected * projected, axis=1, keepdims=True)
    embedding = projected * lax.rsqrt(square_sum + 1e-06)
    for copy in small:
        copy.wait()
    rank = prio[...]
    high = lax.shift_right_logical(rank, 8)
    fields = (owner[...] + 1, sub[...], high, rank - high * RADIX)
    notes = [f.astype(jnp.float32) for f in fields]
    notes.append(jnp.zeros((NOTE_ROWS - len(fields), rows), jnp.float32))
    tiles = [embedding[:, i:i + rows] for i in range(0, width, rows)]
    block = jnp.concatenate(tiles + notes, axis=0).astype(jnp.bfloat16)
    block_ref[...] = block
    tall_ref[:block.shape[0], :] = block
    tall_ref[block.shape[0]:, :] = block[:tall_ref.shape[0] - block.shape[0]]


def embed(states, projection, owner, sub, prio):
    rows, depth = states.shape
    width = projection.shape[1]
    high = rows * (width // rows) + NOTE_ROWS
    return pl.pallas_call(
        embed_kernel,
        in_specs=[HBM] * 5,
        out_specs=[VMEM] * 2,
        out_shape=[jax.ShapeDtypeStruct((tall, rows), jnp.bfloat16) for tall in (high, high + MORE_ROWS)],
        scratch_shapes=[
            pltpu.VMEM((rows, depth), jnp.bfloat16),
            pltpu.VMEM((depth, width), jnp.bfloat16),
            pltpu.VMEM((1, rows), jnp.int32),
            pltpu.VMEM((1, rows), jnp.int32),
            pltpu.VMEM((1, rows), jnp.int32),
            pltpu.SemaphoreType.DMA((CHUNKS + 1,)),
            pltpu.SemaphoreType.DMA((3,)),
        ],
        compiler_params=pltpu.CompilerParams(vmem_limit_bytes=40 << 20),
        name="embed",
    )(*(pltpu.with_memory_space_constraint(x, pltpu.HBM) for x in (states, projection, owner, sub, prio)))


def read_notes(ref):
    first = ref.shape[0] // ref.shape[1] * ref.shape[1]
    tail = ref[first:first + NOTE_ROWS, :].astype(jnp.float32)
    owner, sub, high, low = (tail[i:i + 1] for i in range(4))
    return (owner - 1.0) * 4.0 + sub, high * float(RADIX) + low


def read_rows(refs):
    rows = refs[0].shape[1]
    return jnp.concatenate(
        [
            jnp.concatenate([ref[i * rows:(i + 1) * rows, :] for ref in refs], axis=0)
            for i in range(refs[0].shape[0] // rows)
        ],
        axis=1,
    )


def score_kernel(row_count, lane_count, products, parts, has_lines, has_state, hand_on, hold, *refs):
    refs = list(refs)
    row_refs = [refs.pop(0) for _ in range(row_count)]
    lane_refs = [refs.pop(0) for _ in range(lane_count)]
    seen_lines = refs.pop(0) if has_lines else None
    seen_table, seen_columns = (refs.pop(0), refs.pop(0)) if has_state else (None, None)
    lines_out = refs.pop(0)
    rows = lines_out.shape[1]
    if hold:
        refs[-1][...] = row_refs[0][...]
    lane_notes = [read_notes(ref) for ref in lane_refs]
    if has_state:
        columns = seen_columns[...]
    else:
        fill = jnp.zeros((-2 * row_count % 8, rows), jnp.float32)
        lines = [line for ref in row_refs for line in read_notes(ref)]
        columns = jnp.concatenate(lines + ([fill] if fill.size else []), axis=0).T
    best, back = [None] * lane_count, [None] * row_count

    def top(old, new):
        return new if old is None else jnp.maximum(old, new)

    for row_set, lane_set in products:
        cosine = lax.dot_general(
            read_rows([row_refs[i] for i in row_set]),
            read_rows([lane_refs[j] for j in lane_set]),
            (((1,), (1,)), ((), ())),
            preferred_element_type=jnp.float32,
        )
        for m, i in enumerate(row_set):
            row_cluster, row_prio = columns[:, 2 * i:2 * i + 1], columns[:, 2 * i + 1:2 * i + 2]
            for n, j in enumerate(lane_set):
                lane_cluster, lane_prio = lane_notes[j]
                here = cosine[m * rows:(m + 1) * rows, n * rows:(n + 1) * rows]
                same = jnp.where(row_cluster == lane_cluster, here, -1.0)
                earlier = row_prio < lane_prio
                best[j] = top(best[j], jnp.where(earlier, same, -1.0))
                if j > 0:
                    back[i] = top(back[i], jnp.where(earlier, -1.0, same))
    lane_ids = lax.broadcasted_iota(jnp.int32, (rows, rows), 1)
    table = jnp.full((rows, rows), -1.0, jnp.float32)
    for i, each in enumerate(back):
        if each is not None:
            table = jnp.where(lane_ids == i, jnp.max(each, axis=1, keepdims=True), table)
    if has_state:
        table = jnp.maximum(table, seen_table[...])
    if hand_on:
        refs.pop(0)[...] = table
        refs.pop(0)[...] = columns
    elif parts:
        table = table.T
        for first, stop in parts:
            refs.pop(0)[...] = table[first:stop]
    lines = jnp.concatenate([jnp.max(b, axis=0, keepdims=True) for b in best], axis=0)
    if has_lines:
        count = seen_lines.shape[0]
        first = jnp.maximum(lines[:count], seen_lines[...])
        lines = first if count == lane_count else jnp.concatenate([first, lines[count:]], axis=0)
    lines_out[...] = lines


def score(name, row_blocks, lane_blocks, products, parts, lines=None, state=None, hand_on=False, hold=False):
    high, rows = row_blocks[0].shape
    width = high - NOTE_ROWS
    inputs = [*row_blocks, *lane_blocks, *([] if lines is None else [lines]), *(state or ())]
    shapes = [(len(lane_blocks), rows)] + [(stop - first, rows) for first, stop in parts]
    if hand_on:
        shapes += [(rows, rows), (rows, -(-2 * len(row_blocks) // 8) * 8)]
    outs = [jax.ShapeDtypeStruct(shape, jnp.float32) for shape in shapes]
    if hold:
        outs.append(jax.ShapeDtypeStruct((high, rows), row_blocks[0].dtype))
    counts = len(row_blocks), len(lane_blocks)
    rest = products, parts, lines is not None, state is not None, hand_on, hold
    macs = sum(len(r) * len(c) for r, c in products) * rows * rows * width
    return pl.pallas_call(
        lambda *refs: score_kernel(*counts, *rest, *refs),
        in_specs=[VMEM] * len(inputs),
        out_specs=[VMEM] * len(outs),
        out_shape=outs,
        compiler_params=pltpu.CompilerParams(vmem_limit_bytes=48 << 20),
        cost_estimate=pl.CostEstimate(
            flops=2 * macs, bytes_accessed=2 * sum(counts) * rows * width, transcendentals=0
        ),
        name=name,
    )(*inputs)


def tournament(line):
    moves = [[(i, (i + s) % line) for i in range(line)] for s in range(1, (line + 1) // 2)]
    if line % 2 == 0:
        half = line // 2
        pairs = [(i, i + half) if i % 2 else (i + half, i) for i in range(half)]
        sent, met = {a for a, _ in pairs}, {b for _, b in pairs}
        idle = [i for i in range(line) if i not in sent]
        free = [i for i in range(line) if i not in met]
        moves.append(pairs + list(zip(idle, free)))
    return moves


def on_device(states, projection, owner_group, cluster_sub, priority):
    line, grp = lax.axis_size("line"), lax.axis_size("grp")
    plane = lax.axis_size("mid") * grp
    rows = states.shape[0]

    def move(array, pairs):
        whole = [(a * plane + p, b * plane + p) for a, b in pairs for p in range(plane)]
        return lax.ppermute(array, AXES, whole)

    def swap(array, step):
        pairs = [(i, i // plane * plane + (i % plane ^ step)) for i in range(line * plane)]
        return lax.ppermute(array, AXES, pairs)

    block, tall = embed(
        states,
        projection,
        owner_group.reshape(1, rows),
        cluster_sub.reshape(1, rows),
        priority.reshape(1, rows),
    )
    moves = tournament(line)
    visitors = [move(tall, moves[0])] + [move(block, pairs) for pairs in moves[1:]]
    bits = [1 << i for i in range(1, plane.bit_length() - 1)]
    found = {0: block}
    for bit in reversed(bits):
        found |= {step | bit: swap(here, bit) for step, here in found.items()}
    row_blocks = [found[step] for step in sorted(found)]

    lanes = [block] + visitors
    every, count = tuple(range(len(lanes))), len(row_blocks)
    half = count // 2
    soon = (0, half)
    rest = tuple(i for i in range(count) if i not in soon)
    lines, held = score(
        "score_soon", [row_blocks[i] for i in soon], lanes[:1], [((0, 1), (0,))], [], hold=True
    )
    row_blocks[0] = lanes[0] = held
    products = [(rest, every), (soon, every[1:])]
    lines, *state = score("score_late", row_blocks, lanes, products, [], lines, hand_on=True)
    partner = [held]
    partner += [lax.optimization_barrier((visitor, held))[0] for visitor in visitors[:-1]]
    partner += [lax.optimization_barrier((visitors[-1], row_blocks[1]))[0]]
    partner = [swap(lane, 1) for lane in partner]
    products, parts = [(tuple(range(count)), every)], [(0, half), (half, count)]
    theirs, near, far = score("score_partner", row_blocks, partner, products, parts, state=state)
    lines = jnp.maximum(lines, swap(theirs, 1))
    for bit in bits[:0:-1]:
        near = jnp.maximum(near, swap(far, bit))
        half = near.shape[0] // 2
        near, far = near[:half], near[half:]
    total = lines[:1]
    for i, pairs in reversed(list(enumerate(moves))):
        total = jnp.maximum(total, move(lines[i + 1:i + 2], [(b, a) for a, b in pairs]))
    total = lax.optimization_barrier(total)
    total = jnp.maximum(jnp.maximum(total, near), swap(far, bits[0]))
    return total.reshape(rows)


def solution(mesh):
    num_dp, num_grp = mesh.shape["dp"], mesh.shape["grp"]
    line = min(num_dp, 1 << (int(math.log2(num_dp * num_grp)) // 2))
    split = Mesh(mesh.devices.reshape(line, num_dp // line, num_grp), AXES)
    in_specs = (P(AXES, None), P(), P(AXES, None), P(AXES), P(AXES))
    return jax.shard_map(
        on_device, mesh=split, in_specs=in_specs, out_specs=P(AXES), check_vma=False
    )
```
